256 devices in a mesh: gx: 64 (over y, z, core), gy: 4 (over x).
Axes of the slice: x: 4, y: 4, z: 8, core: 2. Of those that a mesh axis runs over, the one named last changes fastest.
Arguments:
- state: float32 [256, 1048576], P(('gx', 'gy')), may hold values from -6 to 6
- locations: int32 [1024], replicated, may hold values from 0 to 1048575, as said below
- tile_mask: int32 [2048, 1024], P(('gx', 'gy')), may hold values from 0 to 1, as said below
- plan: int32 [1024], replicated, may hold values from 0 to 1023, each once
- obs_value: float32 [1024], replicated, may hold values from -6 to 6
- obs_error: float32 [1024], replicated, may hold values from 0.2 to 2
Outputs:
- analysis: float32 [256, 1048576], P(('gx', 'gy'))
The draws below stay inside these ranges and needn't reach their ends.
Inputs may be any that keep to these rules, and one draw needn't show every extreme that they name: `locations`: observations with an even index lie anywhere in the grid; those with an odd index gather in 8 clusters of tiles. tile_mask is 1 only where the tile lies within 4 tiles, counted cyclically, of the tile that holds the observed variable.
All inputs are finite; a program needn't handle non-finite values.
Results may differ from the reference program's by a relative error of at most 0.0003.
Values sent between devices are 32-bit elements; how exact they have to be, the bound alone decides.
No kernel may reach another device: no remote copies, remote signals or barrier semaphores. Data moves between devices by JAX's collectives and lax.ppermute only.
A program may use at most 64 MiB of HBM per device.

```python
import math
import jax
import jax.numpy as jnp
from jax import lax

M = 256
V_DEV = 4096
TILE = 512
BATCH_OBS = 256
BATCHES = 4
RADIUS = 4
SPREAD = 8
CLUSTERS = 8
NVAR = 1048576
NTILES = 2048
NOBS = 1024


def cluster_sites(key):
    first_key, second_key, third_key, fourth_key, fifth_key = jax.random.split(key, 5)
    centers = jax.random.randint(first_key, (CLUSTERS,), 0, NTILES)
    chosen = jax.random.randint(second_key, (NOBS,), 0, CLUSTERS)
    shifted = jax.random.randint(third_key, (NOBS,), -SPREAD, SPREAD + 1)
    clustered = (centers[chosen] + shifted) % NTILES
    anywhere = jax.random.randint(fifth_key, (NOBS,), 0, NTILES)
    parity = jnp.arange(NOBS, dtype=jnp.int32) % 2
    obs_tile = jnp.where(parity == 0, anywhere, clustered)
    tiles_each = V_DEV // TILE
    pinned = jnp.array([NTILES - 1, 0, tiles_each, NTILES - tiles_each - 1], dtype=jnp.int32)
    obs_tile = obs_tile.at[jnp.array([0, 2, 4, 6], dtype=jnp.int32)].set(pinned)
    within = jax.random.randint(fourth_key, (NOBS,), 0, TILE)
    return ((obs_tile * TILE + within).astype(jnp.int32), obs_tile.astype(jnp.int32))


def draw_locations(key, part):
    sites, obs_tile = cluster_sites(key)
    return sites


def draw_tile_mask(key, part):
    sites, obs_tile = cluster_sites(key)
    key = jax.random.fold_in(key, 7)
    tiles = jnp.arange(NTILES, dtype=jnp.int32)[:, None]
    distance = jnp.abs(tiles - obs_tile[None, :])
    distance = jnp.minimum(distance, NTILES - distance)
    nearby = distance <= RADIUS
    retained = (jax.random.randint(key, (NTILES, NOBS), 0, 4) > 0) | (distance <= 1)
    return (nearby & retained).astype(jnp.int32)


def block_scale(rng, dims, shards, smallest, top_value):
    level = 1.0
    for position, blocks in shards:
        heights = jax.random.uniform(jax.random.fold_in(jax.random.fold_in(rng, 6), position), (blocks,), jnp.float32, smallest / len(shards), top_value / len(shards))
        level = level * jnp.repeat(jnp.exp(heights), dims[position] // blocks).reshape((-1,) + (1,) * (len(dims) - 1 - position))
    return level


def centred(own_key, extent, scale, reach, cuts=(), kind=jnp.bfloat16):
    values = scale * jax.random.normal(own_key, extent, jnp.float32)
    if cuts:
        values = values * block_scale(own_key, extent, cuts, -0.22, 0.18)
    return jnp.clip(values, -reach, reach).astype(kind)


def setup_inputs(seed: int = 0) -> dict:
    streams_of = jax.random.split(jax.random.key(seed), 7)
    state = centred(streams_of[0], (M, NVAR), 1.0, 6.0, ((0, 256),), jnp.float32)
    locations = draw_locations(jax.random.fold_in(streams_of[6], 71), 0)
    tile_mask = draw_tile_mask(jax.random.fold_in(streams_of[6], 71), 0)
    plan = jax.random.permutation(streams_of[3], NOBS).astype(jnp.int32)
    obs_value = centred(streams_of[4], (NOBS,), 1.5, 6.0, (), jnp.float32)
    obs_error = jnp.clip(jnp.exp(jax.random.uniform(streams_of[5], (NOBS,), jnp.float32, math.log(0.2), math.log(2.0))), 0.2, 2.0)
    return {"state": state, "locations": locations, "tile_mask": tile_mask, "plan": plan, "obs_value": obs_value, "obs_error": obs_error}


epsilon = 1e-06

def adjust(prior_rows, obs_values, obs_errors):
    members = prior_rows.shape[0]
    average = lax.optimization_barrier(jnp.mean(prior_rows, axis=0))
    obs_anomaly = prior_rows - average[None, :]
    spread = lax.optimization_barrier(jnp.sum(obs_anomaly * obs_anomaly, axis=0)) / (members - 1) + epsilon
    shrink = jnp.sqrt(obs_errors / (spread + obs_errors))
    post_mean = (average * obs_errors + obs_values * spread) / (spread + obs_errors)
    increments = (shrink - 1.0)[None, :] * obs_anomaly + (post_mean - average)[None, :]
    obs_gains = 1.0 / ((members - 1) * spread)
    return (obs_anomaly, increments, obs_gains)

def update_tile(tile_block, tile_weights, obs_anomaly, increments):
    anomaly = tile_block - lax.optimization_barrier(jnp.mean(tile_block, axis=0))[None, :]
    covariance = lax.dot_general(anomaly, obs_anomaly, (((0,), (0,)), ((), ())), precision=lax.Precision.HIGHEST, preferred_element_type=jnp.float32)
    coefficient = covariance * tile_weights[None, :]
    return tile_block + lax.dot_general(increments, coefficient, (((1,), (1,)), ((), ())), precision=lax.Precision.HIGHEST, preferred_element_type=jnp.float32)

def reference(state, locations, tile_mask, plan, obs_value, obs_error):
    ensemble = state
    for batch_step in range(BATCHES):
        picked = plan[batch_step * BATCH_OBS:(batch_step + 1) * BATCH_OBS]
        prior_rows = ensemble[:, locations[picked]]
        obs_anomaly, increments, obs_gains = adjust(prior_rows, obs_value[picked], obs_error[picked])
        weights = tile_mask[:, picked].astype(jnp.float32) * obs_gains[None, :]
        blocks = ensemble.reshape(M, NTILES, TILE).transpose(1, 0, 2)

        def visit(operands):
            tile_block, tile_weights = operands
            return lax.cond(jnp.any(tile_weights > 0), lambda: update_tile(tile_block, tile_weights, obs_anomaly, increments), lambda: tile_block)
        updated = lax.map(visit, (blocks, weights))
        ensemble = updated.transpose(1, 0, 2).reshape(M, NVAR)
    return ensemble
```

```python
import functools

import jax
import jax.numpy as jnp
from jax import lax
from jax.experimental import pallas as pl
from jax.experimental.pallas import tpu as pltpu
from jax.sharding import Mesh, PartitionSpec as P

MEMBERS = 256
TILE = 512
NTILES = 2048
RADIUS = 4
WINDOW = 2 * RADIUS + 1
BATCH_OBS = 256
BATCHES = 4
NOBS = BATCH_OBS * BATCHES

ALL = ("y", "h", "l", "c", "x")
PEERS = ("y", "l", "c", "x")
GROUP = 64
SUMS = 4
RESIDUES = 16
SLICES = 4
LANES = 128
HALF = 64
OWN_TILES = NTILES // RESIDUES
PAIRS = OWN_TILES // 2
ROWS = NTILES * TILE // LANES
CHUNK = NOBS // 2 // SUMS

epsilon = 1e-06
f32 = jnp.float32
bf16 = jnp.bfloat16
i32 = jnp.int32

VMEM = pl.BlockSpec(memory_space=pltpu.VMEM)
SMEM = pl.BlockSpec(memory_space=pltpu.SMEM)


def kernel_params(mib):
    return pltpu.CompilerParams(vmem_limit_bytes=mib * 1024 * 1024)


def struct(shape, dtype=f32):
    return jax.ShapeDtypeStruct(shape, dtype)


def two_parts(value):
    high = value.astype(bf16)
    return high, (value - high.astype(f32)).astype(bf16)


def three_parts(value):
    high = value.astype(bf16)
    rest = value - high.astype(f32)
    middle = rest.astype(bf16)
    return high, middle, (rest - middle.astype(f32)).astype(bf16)


def dot(a, b):
    return lax.dot_general(a, b, (((1,), (0,)), ((), ())), preferred_element_type=f32)


def dot_parts(a_high, a_low, b_high, b_low):
    return dot(a_high, b_high) + dot(a_high, b_low) + dot(a_low, b_high)


def accurate_dot(a, b):
    return dot_parts(*two_parts(a), *two_parts(b))


def columns_kernel(plan_ref, locations_ref, state_ref, out_ref, picked_ref):
    lane = lax.broadcasted_iota(i32, (1, LANES), 1)

    def step(i, carry):
        base = pl.multiple_of(i * 8, 8)
        found = []
        for u in range(8):
            where = locations_ref[plan_ref[base + u]]
            row = state_ref[pl.ds(where >> 7, 1), :]
            found.append(jnp.where(lane == (where & (LANES - 1)), row, 0.0))
        picked_ref[pl.ds(base, 8), :] = jnp.concatenate(found, axis=0)
        return carry

    lax.fori_loop(0, NOBS // 8, step, 0, unroll=2)
    ones = jnp.ones((16, LANES), bf16)
    total = jnp.zeros((16, NOBS), f32)
    for part in three_parts(picked_ref[...]):
        total = total + lax.dot_general(ones, part, (((1,), (1,)), ((), ())), preferred_element_type=f32)
    for g in range(NOBS // LANES):
        out_ref[pl.ds(g, 1), :] = total[0:1, g * LANES : (g + 1) * LANES]


def own_columns(plan, locations, rows):
    return pl.pallas_call(
        columns_kernel,
        out_shape=struct((NOBS // LANES, LANES)),
        in_specs=[SMEM, SMEM, VMEM],
        out_specs=VMEM,
        scratch_shapes=[pltpu.VMEM((NOBS, LANES), f32)],
        compiler_params=kernel_params(24),
        cost_estimate=pl.CostEstimate(flops=10**6, bytes_accessed=8 * 2**20, transcendentals=0),
        name="own_columns",
    )(plan, locations, rows)


def spread_kernel(state_ref, first_ref, second_ref):
    low_lanes = lax.broadcasted_iota(i32, (PAIRS, LANES), 1) < HALF

    def step(d, carry):
        upper = state_ref[pl.ds(d, PAIRS, stride=GROUP), :]
        lower = state_ref[pl.ds(d + ROWS // 2, PAIRS, stride=GROUP), :]
        first_ref[d] = jnp.where(low_lanes, upper, lower)
        second_ref[d] = jnp.where(low_lanes, lower, upper)
        return carry

    lax.fori_loop(0, GROUP, step, 0)


def spread_out(rows):
    half = struct((GROUP, PAIRS, LANES))
    return pl.pallas_call(
        spread_kernel,
        out_shape=(half, half),
        in_specs=[VMEM],
        out_specs=(VMEM, VMEM),
        compiler_params=kernel_params(24),
        cost_estimate=pl.CostEstimate(flops=10**6, bytes_accessed=8 * 2**20, transcendentals=0),
        name="spread_out",
    )(rows)


def collect_kernel(first_ref, second_ref, state_ref):
    low_lanes = lax.broadcasted_iota(i32, (PAIRS, LANES), 1) < HALF

    def step(d, carry):
        first = first_ref[d]
        second = second_ref[d]
        state_ref[pl.ds(d, PAIRS, stride=GROUP), :] = jnp.where(low_lanes, first, second)
        state_ref[pl.ds(d + ROWS // 2, PAIRS, stride=GROUP), :] = jnp.where(low_lanes, second, first)
        return carry

    lax.fori_loop(0, GROUP, step, 0)


def collect(first, second):
    return pl.pallas_call(
        collect_kernel,
        out_shape=struct((ROWS, LANES)),
        in_specs=[VMEM, VMEM],
        out_specs=VMEM,
        compiler_params=kernel_params(24),
        cost_estimate=pl.CostEstimate(flops=10**6, bytes_accessed=8 * 2**20, transcendentals=0),
        name="collect",
    )(first, second)


def observation_kernel(
    position_ref, plan_ref, facts_ref, gathered_ref, masks_ref,
    anomalies_high_ref, anomalies_low_ref, increments_high_ref, increments_low_ref,
    links_high_ref, links_low_ref, column_facts_ref, row_facts_ref,
    ensemble_ref, increments_ref, one_hot_ref, facts_scratch, in_columns_ref,
):
    for d in range(SUMS):
        for g in range(NOBS // LANES):
            ensemble_ref[d * GROUP : (d + 1) * GROUP, g * LANES : (g + 1) * LANES] = gathered_ref[
                pl.ds(d * 8 + g, GROUP, stride=40), :
            ]
    for g in range(NOBS // LANES):
        facts_scratch[0:16, g * LANES : (g + 1) * LANES] = masks_ref[pl.ds(g, 16, stride=8), :]
    facts_scratch[16:24, :] = facts_ref[...]
    facts_scratch[24:128, :] = jnp.zeros((104, NOBS), f32)
    source = lax.broadcasted_iota(i32, (NOBS, NOBS), 0)
    one_hot_ref[...] = jnp.where(source == plan_ref[...], 1.0, 0.0).astype(bf16)
    high, middle, low = three_parts(facts_scratch[0:32, :])
    ordered = dot(high, one_hot_ref[...]) + dot(middle, one_hot_ref[...]) + dot(low, one_hot_ref[...])
    facts_scratch[0:32, :] = ordered
    for g in range(NOBS // LANES):
        in_columns_ref[g * LANES : (g + 1) * LANES, :] = facts_scratch[:, g * LANES : (g + 1) * LANES].T

    residue = position_ref[0]
    tile_row = facts_scratch[16:17, :].astype(i32)
    tile_column = in_columns_ref[:, 16:17].astype(i32)
    nth_row = (residue - tile_row + RADIUS) & (RESIDUES - 1)
    nth_column = (residue - tile_column + RADIUS) & (RESIDUES - 1)
    own_row = ((tile_row - RADIUS + nth_row) & (NTILES - 1)) >> 4
    own_column = ((tile_column - RADIUS + nth_column) & (NTILES - 1)) >> 4
    own_row = jnp.where(nth_row < WINDOW, own_row, -1)
    own_column = jnp.where(nth_column < WINDOW, own_column, -2)
    mask_column = jnp.zeros((NOBS, 1), f32)
    for n in range(WINDOW):
        mask_column = mask_column + jnp.where(nth_column == n, in_columns_ref[:, n : n + 1], 0.0)

    row_facts_ref[...] = jnp.broadcast_to(jnp.where(own_row < 0, -256, own_row & (PAIRS - 1)).astype(f32), (16, NOBS))
    lane = lax.broadcasted_iota(i32, (NOBS, LANES), 1)
    pair_column = jnp.where(own_column < 0, -256, own_column & (PAIRS - 1)).astype(f32)
    half_column = jnp.where(own_column >= PAIRS, 1.0, 0.0)

    for b in range(BATCHES):
        here = slice(b * BATCH_OBS, (b + 1) * BATCH_OBS)
        prior = ensemble_ref[:, here]
        average = jnp.sum(prior, axis=0, keepdims=True) / MEMBERS
        anomaly = prior - average
        spread = jnp.sum(anomaly * anomaly, axis=0, keepdims=True) / (MEMBERS - 1) + epsilon
        value = facts_scratch[17:18, here]
        error = facts_scratch[18:19, here]
        shrink = jnp.sqrt(error / (spread + error))
        moved = (average * error + value * spread) / (spread + error)
        increments = (shrink - 1.0) * anomaly + (moved - average)
        increments_ref[:, here] = increments
        turned = anomaly.T
        spread_column = jnp.sum(turned * turned, axis=1, keepdims=True) / (MEMBERS - 1) + epsilon
        gain_column = 1.0 / ((MEMBERS - 1) * spread_column)
        turned_high, turned_low = two_parts(turned)
        own_high = turned_high[:, 0:GROUP]
        own_low = turned_low[:, 0:GROUP]
        anomalies_high_ref[here, :] = jnp.concatenate([own_high] * 4, axis=1)
        anomalies_low_ref[here, :] = jnp.concatenate([own_low] * 4, axis=1)
        own_increments = two_parts(increments[0:GROUP, :])
        increments_high_ref[:, here] = own_increments[0]
        increments_low_ref[:, here] = own_increments[1]
        weight = mask_column[here] * gain_column
        column_facts_ref[here, :] = jnp.where(
            lane[here] == 0, weight, jnp.where(lane[here] == 1, pair_column[here], half_column[here])
        )
        if b > 0:
            before = b * BATCH_OBS
            links = accurate_dot(turned, increments_ref[:, 0:before])
            links = jnp.where(own_column[here] == own_row[:, 0:before], links * weight, 0.0)
            links_high, links_low = two_parts(links)
            links_high_ref[here, 0:before] = links_high
            links_low_ref[here, 0:before] = links_low
        if b < BATCHES - 1:
            after = slice((b + 1) * BATCH_OBS, NOBS)
            later = ensemble_ref[:, after]
            covariance = dot_parts(turned_high, turned_low, *two_parts(later))
            apart = (tile_row[:, after] - tile_column[here] + RADIUS) & (NTILES - 1)
            masks = jnp.zeros(apart.shape, f32)
            for n in range(WINDOW):
                masks = jnp.where(apart == n, in_columns_ref[here, n : n + 1], masks)
            ensemble_ref[:, after] = later + accurate_dot(increments, covariance * masks * gain_column)


def observations(position, plan, facts, gathered, masks):
    wide = struct((NOBS, 4 * GROUP), bf16)
    narrow = struct((GROUP, NOBS), bf16)
    links = struct((NOBS, NOBS), bf16)
    return pl.pallas_call(
        observation_kernel,
        out_shape=(wide, wide, narrow, narrow, links, links, struct((NOBS, LANES)), struct((16, NOBS))),
        in_specs=[SMEM, VMEM, VMEM, VMEM, VMEM],
        out_specs=(VMEM,) * 8,
        scratch_shapes=[
            pltpu.VMEM((MEMBERS, NOBS), f32),
            pltpu.VMEM((MEMBERS, NOBS), f32),
            pltpu.VMEM((NOBS, NOBS), bf16),
            pltpu.VMEM((128, NOBS), f32),
            pltpu.VMEM((NOBS, 128), f32),
        ],
        compiler_params=kernel_params(40),
        cost_estimate=pl.CostEstimate(flops=12 * 10**9, bytes_accessed=8 * 2**20, transcendentals=10**5),
        name="observations",
    )(position, plan, facts, gathered, masks)


def half_of(column_facts, second):
    half = column_facts[:, 2:3] > 0.5
    return jnp.logical_not(half) if second else half


def covariance_kernel(second, position_ref, block_ref, anomalies_high_ref, anomalies_low_ref, facts_ref, *refs):
    out_refs, (total_ref, pair_ref) = refs[:SUMS], refs[SUMS:]
    lane_block = lax.broadcasted_iota(i32, (NOBS, 4 * GROUP), 1) >> 6
    pair_ref[...] = (facts_ref[:, 1:2] - lane_block.astype(f32)).astype(bf16)
    total_ref[...] = jnp.zeros_like(total_ref)

    def step(g, carry):
        found = pair_ref[...] == jnp.full((NOBS, 4 * GROUP), (g * 4).astype(f32)).astype(bf16)
        zero = jnp.zeros((NOBS, 4 * GROUP), bf16)
        left_high = jnp.where(found, anomalies_high_ref[...], zero)
        left_low = jnp.where(found, anomalies_low_ref[...], zero)
        right = jnp.concatenate(
            [block_ref[pl.ds(g * 4 + u, GROUP, stride=PAIRS), :] for u in range(4)], axis=0
        )
        right_high, right_low = two_parts(right)
        both = dot(left_high, jnp.concatenate([right_high, right_low], axis=1))
        total_ref[...] += both[:, :LANES] + both[:, LANES:] + dot(left_low, right_high)
        return carry

    lax.fori_loop(0, PAIRS // 4, step, 0)
    total = total_ref[...]
    other = pltpu.roll(total, HALF, 1)
    half = half_of(facts_ref[...], second)
    low_lanes = lax.broadcasted_iota(i32, (NOBS // 2, LANES), 1) < HALF
    upper = jnp.where(half, other, total)[: NOBS // 2]
    lower = jnp.where(half, total, other)[NOBS // 2 :]
    total_ref[0 : NOBS // 2, :] = jnp.where(low_lanes, upper, lower)
    for d in range(SUMS):
        start = ((position_ref[1] + d) & (SUMS - 1)) * CHUNK
        out_refs[d][...] = total_ref[pl.ds(pl.multiple_of(start, CHUNK), CHUNK), :]


def covariances(second, position, block, anomalies_high, anomalies_low, facts):
    return pl.pallas_call(
        functools.partial(covariance_kernel, second),
        out_shape=(struct((CHUNK, LANES)),) * SUMS,
        in_specs=[SMEM] + [VMEM] * 4,
        out_specs=(VMEM,) * SUMS,
        scratch_shapes=[pltpu.VMEM((NOBS, LANES), f32), pltpu.VMEM((NOBS, 4 * GROUP), bf16)],
        compiler_params=kernel_params(24),
        cost_estimate=pl.CostEstimate(flops=3 * 10**9, bytes_accessed=4 * 2**20, transcendentals=0),
        name="covariances",
    )(position, block.reshape(GROUP * PAIRS, LANES), anomalies_high, anomalies_low, facts)


def update_kernel(
    second, position_ref, *refs
):
    sums_refs = refs[:SUMS]
    (block_ref, increments_high_ref, increments_low_ref, links_high_ref, links_low_ref,
     facts_ref, row_facts_ref, out_ref, sums_ref, coefficient_ref, right_ref) = refs[SUMS:]
    for d in range(SUMS):
        start = ((position_ref[1] - d) & (SUMS - 1)) * CHUNK
        sums_ref[pl.ds(pl.multiple_of(start, CHUNK), CHUNK), :] = sums_refs[d][...]
    packed = sums_ref[...]
    weight = facts_ref[:, 0:1]
    coefficient_ref[0 : NOBS // 2, :] = packed * weight[: NOBS // 2]
    coefficient_ref[NOBS // 2 :, :] = pltpu.roll(packed, HALF, 1) * weight[NOBS // 2 :]
    for b in range(1, BATCHES):
        here = slice(b * BATCH_OBS, (b + 1) * BATCH_OBS)
        before = slice(0, b * BATCH_OBS)
        coefficient_ref[here, :] += dot_parts(
            links_high_ref[here, before], links_low_ref[here, before], *two_parts(coefficient_ref[before, :])
        )
    coefficient = coefficient_ref[...]
    half = half_of(facts_ref[...], second)
    high_lanes = lax.broadcasted_iota(i32, (NOBS, LANES), 1) >= HALF
    placed = jnp.where(
        high_lanes,
        jnp.where(half, pltpu.roll(coefficient, HALF, 1), 0.0),
        jnp.where(half, 0.0, coefficient),
    )
    right_high, right_low = two_parts(placed)
    right_ref[:, :LANES] = right_high
    right_ref[:, LANES:] = right_low
    pair_row = row_facts_ref[...].astype(bf16)[0:1, :]

    def step(g, carry):
        highs, lows = [], []
        zero = jnp.zeros((GROUP, NOBS), bf16)
        for u in range(4):
            found = pair_row == jnp.full((1, NOBS), (g * 4 + u).astype(f32)).astype(bf16)
            found = jnp.broadcast_to(found, (GROUP, NOBS))
            highs.append(jnp.where(found, increments_high_ref[...], zero))
            lows.append(jnp.where(found, increments_low_ref[...], zero))
        both = dot(jnp.concatenate(highs, axis=0), right_ref[...])
        change = both[:, :LANES] + both[:, LANES:] + dot(jnp.concatenate(lows, axis=0), right_ref[:, :LANES])
        for u in range(4):
            rows = pl.ds(g * 4 + u, GROUP, stride=PAIRS)
            out_ref[rows, :] = block_ref[rows, :] + change[u * GROUP : (u + 1) * GROUP]
        return carry

    lax.fori_loop(0, PAIRS // 4, step, 0)


def updated(second, position, sums, block, increments_high, increments_low, links_high, links_low, facts, row_facts):
    out = pl.pallas_call(
        functools.partial(update_kernel, second),
        out_shape=struct((GROUP * PAIRS, LANES)),
        in_specs=[SMEM] + [VMEM] * (SUMS + 7),
        out_specs=VMEM,
        scratch_shapes=[
            pltpu.VMEM((NOBS // 2, LANES), f32),
            pltpu.VMEM((NOBS, LANES), f32),
            pltpu.VMEM((NOBS, 2 * LANES), bf16),
        ],
        compiler_params=kernel_params(32),
        cost_estimate=pl.CostEstimate(flops=4 * 10**9, bytes_accessed=8 * 2**20, transcendentals=0),
        name="updated",
    )(
        position, *sums, block.reshape(GROUP * PAIRS, LANES), increments_high, increments_low,
        links_high, links_low, facts, row_facts,
    )
    return out.reshape(GROUP, PAIRS, LANES)


def exchange(value):
    return lax.all_to_all(value, PEERS, 0, 0, tiled=True)


def passed_along(value, by):
    return lax.ppermute(value, "h", [(i, (i + by) % SUMS) for i in range(SUMS)])


def summed(parts):
    total = parts[0]
    for by in range(1, SUMS):
        total = total + passed_along(parts[by], by)
    return (total, *(passed_along(total, by) for by in range(1, SUMS)))


def shards(state, locations, tile_mask, plan, obs_value, obs_error):
    group_index = lax.axis_index(PEERS)
    position = jnp.stack([group_index // SLICES, lax.axis_index("h")]).astype(i32)
    rows = state.reshape(ROWS, LANES)

    tiles_here = tile_mask.shape[0]
    tiles = locations // TILE
    nth = jnp.arange(16, dtype=i32)[:, None]
    local = (tiles[None, :] - RADIUS + nth - lax.axis_index(ALL) * tiles_here) & (NTILES - 1)
    masks = jnp.zeros((16, NOBS), i32)
    for i in range(tiles_here):
        masks = masks + jnp.where((local == i) & (nth < WINDOW), tile_mask[i][None, :], 0)
    masks = exchange(masks.astype(f32).reshape(GROUP, 2, LANES)).sum(axis=0)

    columns = own_columns(plan, locations, rows)
    payload = jnp.concatenate(
        [columns, *(passed_along(columns, by) for by in range(1, SUMS)), masks, jnp.zeros((6, LANES), f32)], axis=0
    )
    gathered = exchange(jnp.broadcast_to(payload[None], (GROUP, 40, LANES)))

    first, second = spread_out(rows)
    first, gathered = lax.optimization_barrier((first, gathered))
    first = exchange(first)

    all_masks = gathered[:, 32:34, :]
    all_masks = all_masks + sum(passed_along(all_masks, by) for by in range(1, SUMS))
    facts = jnp.concatenate(
        [tiles.astype(f32)[None], obs_value[None], obs_error[None], jnp.zeros((5, NOBS), f32)], axis=0
    )
    (anomalies_high, anomalies_low, increments_high, increments_low, links_high, links_low, column_facts, row_facts) = (
        observations(
            position, plan[None], facts, gathered.reshape(GROUP * 40, LANES), all_masks.reshape(2 * GROUP, LANES)
        )
    )

    first, second = lax.optimization_barrier((first, second))
    second = exchange(second)

    def assimilated(is_second, block):
        parts = covariances(is_second, position, block, anomalies_high, anomalies_low, column_facts)
        return updated(
            is_second, position, summed(parts), block,
            increments_high, increments_low, links_high, links_low, column_facts, row_facts,
        )

    first = exchange(assimilated(False, first))
    second = exchange(assimilated(True, second))
    return collect(first, second).reshape(state.shape)


def solution(mesh):
    fine = Mesh(mesh.devices.reshape(4, 4, 2, 2, 4), ALL)
    placed = (P(ALL, None), P(), P(ALL, None), P(), P(), P())
    return jax.shard_map(shards, mesh=fine, in_specs=placed, out_specs=P(ALL, None), check_vma=False)
```

```python
import functools

import jax
import jax.numpy as jnp
from jax import lax
from jax.experimental import pallas as pl
from jax.experimental.pallas import tpu as pltpu
from jax.sharding import Mesh, PartitionSpec as P

MEMBERS = 256
TILE = 512
NTILES = 2048
RADIUS = 4
WINDOW = 2 * RADIUS + 1
BATCH_OBS = 256
BATCHES = 4
NOBS = BATCH_OBS * BATCHES

ALL = ("y", "h", "l", "c", "x")
PEERS = ("c", "y", "l", "x")
CHIPS = ("y", "l", "x")
GROUP = 64
CORES = 2
GROUP_CHIPS = GROUP // CORES
SUMS = 4
RESIDUES = 16
SLICES = 4
LANES = 128
HALF = 64
OWN_TILES = NTILES // RESIDUES
PAIRS = OWN_TILES // 2
ROWS = NTILES * TILE // LANES
CHUNK = NOBS // 2 // SUMS

epsilon = 1e-06
f32 = jnp.float32
bf16 = jnp.bfloat16
i32 = jnp.int32

VMEM = pl.BlockSpec(memory_space=pltpu.VMEM)
SMEM = pl.BlockSpec(memory_space=pltpu.SMEM)


def kernel_params(mib):
    return pltpu.CompilerParams(vmem_limit_bytes=mib * 1024 * 1024)


def struct(shape, dtype=f32):
    return jax.ShapeDtypeStruct(shape, dtype)


def two_parts(value):
    high = value.astype(bf16)
    return high, (value - high.astype(f32)).astype(bf16)


def three_parts(value):
    high = value.astype(bf16)
    rest = value - high.astype(f32)
    middle = rest.astype(bf16)
    return high, middle, (rest - middle.astype(f32)).astype(bf16)


def dot(a, b):
    return lax.dot_general(a, b, (((1,), (0,)), ((), ())), preferred_element_type=f32)


def dot_parts(a_high, a_low, b_high, b_low):
    return dot(a_high, b_high) + dot(a_high, b_low) + dot(a_low, b_high)


def accurate_dot(a, b):
    return dot_parts(*two_parts(a), *two_parts(b))


def columns_kernel(plan_ref, locations_ref, state_ref, out_ref, picked_ref):
    lane = lax.broadcasted_iota(i32, (1, LANES), 1)

    def step(i, carry):
        base = pl.multiple_of(i * 8, 8)
        found = []
        for u in range(8):
            where = locations_ref[plan_ref[base + u]]
            row = state_ref[pl.ds(where >> 7, 1), :]
            found.append(jnp.where(lane == (where & (LANES - 1)), row, 0.0))
        picked_ref[pl.ds(base, 8), :] = jnp.concatenate(found, axis=0)
        return carry

    lax.fori_loop(0, NOBS // 8, step, 0, unroll=2)
    ones = jnp.ones((16, LANES), bf16)
    total = jnp.zeros((16, NOBS), f32)
    for part in three_parts(picked_ref[...]):
        total = total + lax.dot_general(ones, part, (((1,), (1,)), ((), ())), preferred_element_type=f32)
    for g in range(NOBS // LANES):
        out_ref[pl.ds(g, 1), :] = total[0:1, g * LANES : (g + 1) * LANES]


def own_columns(plan, locations, rows):
    return pl.pallas_call(
        columns_kernel,
        out_shape=struct((NOBS // LANES, LANES)),
        in_specs=[SMEM, SMEM, VMEM],
        out_specs=VMEM,
        scratch_shapes=[pltpu.VMEM((NOBS, LANES), f32)],
        compiler_params=kernel_params(24),
        cost_estimate=pl.CostEstimate(flops=10**6, bytes_accessed=8 * 2**20, transcendentals=0),
        name="own_columns",
    )(plan, locations, rows)


def spread_kernel(state_ref, first_ref, second_ref):
    low_lanes = lax.broadcasted_iota(i32, (PAIRS, LANES), 1) < HALF

    def step(d, carry):
        upper = state_ref[pl.ds(d, PAIRS, stride=GROUP), :]
        lower = state_ref[pl.ds(d + ROWS // 2, PAIRS, stride=GROUP), :]
        first_ref[d] = jnp.where(low_lanes, upper, lower)
        second_ref[d] = jnp.where(low_lanes, lower, upper)
        return carry

    lax.fori_loop(0, GROUP, step, 0)


def spread_out(rows):
    half = struct((GROUP, PAIRS, LANES))
    return pl.pallas_call(
        spread_kernel,
        out_shape=(half, half),
        in_specs=[VMEM],
        out_specs=(VMEM, VMEM),
        compiler_params=kernel_params(24),
        cost_estimate=pl.CostEstimate(flops=10**6, bytes_accessed=8 * 2**20, transcendentals=0),
        name="spread_out",
    )(rows)


def collect_kernel(first_ref, second_ref, state_ref):
    low_lanes = lax.broadcasted_iota(i32, (PAIRS, LANES), 1) < HALF

    def step(d, carry):
        first = first_ref[d]
        second = second_ref[d]
        state_ref[pl.ds(d, PAIRS, stride=GROUP), :] = jnp.where(low_lanes, first, second)
        state_ref[pl.ds(d + ROWS // 2, PAIRS, stride=GROUP), :] = jnp.where(low_lanes, second, first)
        return carry

    lax.fori_loop(0, GROUP, step, 0)


def collect(first, second):
    return pl.pallas_call(
        collect_kernel,
        out_shape=struct((ROWS, LANES)),
        in_specs=[VMEM, VMEM],
        out_specs=VMEM,
        compiler_params=kernel_params(24),
        cost_estimate=pl.CostEstimate(flops=10**6, bytes_accessed=8 * 2**20, transcendentals=0),
        name="collect",
    )(first, second)


def observation_kernel(
    position_ref, plan_ref, facts_ref, own_ref, other_ref,
    anomalies_high_ref, anomalies_low_ref, increments_high_ref, increments_low_ref,
    links_high_ref, links_low_ref, column_facts_ref, row_facts_ref,
    ensemble_ref, increments_ref, one_hot_ref, facts_scratch, in_columns_ref,
):
    core = position_ref[2]
    for d in range(SUMS):
        for gathered_ref, start in ((own_ref, core), (other_ref, 1 - core)):
            rows = pl.ds(pl.multiple_of(d * GROUP + start * GROUP_CHIPS, GROUP_CHIPS), GROUP_CHIPS)
            for g in range(NOBS // LANES):
                ensemble_ref[rows, g * LANES : (g + 1) * LANES] = gathered_ref[
                    pl.ds(d * 8 + g, GROUP_CHIPS, stride=40), :
                ]
    for g in range(NOBS // LANES):
        rows = pl.ds((g // 4) * 40 + 32 + g % 4, 16, stride=80)
        facts_scratch[0:16, g * LANES : (g + 1) * LANES] = own_ref[rows, :] + other_ref[rows, :]
    facts_scratch[16:24, :] = facts_ref[...]
    facts_scratch[24:128, :] = jnp.zeros((104, NOBS), f32)
    source = lax.broadcasted_iota(i32, (NOBS, NOBS), 0)
    one_hot_ref[...] = jnp.where(source == plan_ref[...], 1.0, 0.0).astype(bf16)
    high, middle, low = three_parts(facts_scratch[0:32, :])
    ordered = dot(high, one_hot_ref[...]) + dot(middle, one_hot_ref[...]) + dot(low, one_hot_ref[...])
    facts_scratch[0:32, :] = ordered
    for g in range(NOBS // LANES):
        in_columns_ref[g * LANES : (g + 1) * LANES, :] = facts_scratch[:, g * LANES : (g + 1) * LANES].T

    residue = position_ref[0]
    tile_row = facts_scratch[16:17, :].astype(i32)
    tile_column = in_columns_ref[:, 16:17].astype(i32)
    nth_row = (residue - tile_row + RADIUS) & (RESIDUES - 1)
    nth_column = (residue - tile_column + RADIUS) & (RESIDUES - 1)
    own_row = ((tile_row - RADIUS + nth_row) & (NTILES - 1)) >> 4
    own_column = ((tile_column - RADIUS + nth_column) & (NTILES - 1)) >> 4
    own_row = jnp.where(nth_row < WINDOW, own_row, -1)
    own_column = jnp.where(nth_column < WINDOW, own_column, -2)
    mask_column = jnp.zeros((NOBS, 1), f32)
    for n in range(WINDOW):
        mask_column = mask_column + jnp.where(nth_column == n, in_columns_ref[:, n : n + 1], 0.0)

    row_facts_ref[...] = jnp.broadcast_to(jnp.where(own_row < 0, -256, own_row & (PAIRS - 1)).astype(f32), (16, NOBS))
    lane = lax.broadcasted_iota(i32, (NOBS, LANES), 1)
    pair_column = jnp.where(own_column < 0, -256, own_column & (PAIRS - 1)).astype(f32)
    half_column = jnp.where(own_column >= PAIRS, 1.0, 0.0)

    for b in range(BATCHES):
        here = slice(b * BATCH_OBS, (b + 1) * BATCH_OBS)
        prior = ensemble_ref[:, here]
        average = jnp.sum(prior, axis=0, keepdims=True) / MEMBERS
        anomaly = prior - average
        spread = jnp.sum(anomaly * anomaly, axis=0, keepdims=True) / (MEMBERS - 1) + epsilon
        value = facts_scratch[17:18, here]
        error = facts_scratch[18:19, here]
        shrink = jnp.sqrt(error / (spread + error))
        moved = (average * error + value * spread) / (spread + error)
        increments = (shrink - 1.0) * anomaly + (moved - average)
        increments_ref[:, here] = increments
        turned = anomaly.T
        spread_column = jnp.sum(turned * turned, axis=1, keepdims=True) / (MEMBERS - 1) + epsilon
        gain_column = 1.0 / ((MEMBERS - 1) * spread_column)
        turned_high, turned_low = two_parts(turned)
        own_high = turned_high[:, 0:GROUP]
        own_low = turned_low[:, 0:GROUP]
        anomalies_high_ref[here, :] = jnp.concatenate([own_high] * 4, axis=1)
        anomalies_low_ref[here, :] = jnp.concatenate([own_low] * 4, axis=1)
        own_increments = two_parts(increments[0:GROUP, :])
        increments_high_ref[:, here] = own_increments[0]
        increments_low_ref[:, here] = own_increments[1]
        weight = mask_column[here] * gain_column
        column_facts_ref[here, :] = jnp.where(
            lane[here] == 0, weight, jnp.where(lane[here] == 1, pair_column[here], half_column[here])
        )
        if b > 0:
            before = b * BATCH_OBS
            links = accurate_dot(turned, increments_ref[:, 0:before])
            links = jnp.where(own_column[here] == own_row[:, 0:before], links * weight, 0.0)
            links_high, links_low = two_parts(links)
            links_high_ref[here, 0:before] = links_high
            links_low_ref[here, 0:before] = links_low
        if b < BATCHES - 1:
            after = slice((b + 1) * BATCH_OBS, NOBS)
            later = ensemble_ref[:, after]
            covariance = dot_parts(turned_high, turned_low, *two_parts(later))
            apart = (tile_row[:, after] - tile_column[here] + RADIUS) & (NTILES - 1)
            masks = jnp.zeros(apart.shape, f32)
            for n in range(WINDOW):
                masks = jnp.where(apart == n, in_columns_ref[here, n : n + 1], masks)
            ensemble_ref[:, after] = later + accurate_dot(increments, covariance * masks * gain_column)


def observations(position, plan, facts, own, other):
    wide = struct((NOBS, 4 * GROUP), bf16)
    narrow = struct((GROUP, NOBS), bf16)
    links = struct((NOBS, NOBS), bf16)
    return pl.pallas_call(
        observation_kernel,
        out_shape=(wide, wide, narrow, narrow, links, links, struct((NOBS, LANES)), struct((16, NOBS))),
        in_specs=[SMEM, VMEM, VMEM, VMEM, VMEM],
        out_specs=(VMEM,) * 8,
        scratch_shapes=[
            pltpu.VMEM((MEMBERS, NOBS), f32),
            pltpu.VMEM((MEMBERS, NOBS), f32),
            pltpu.VMEM((NOBS, NOBS), bf16),
            pltpu.VMEM((128, NOBS), f32),
            pltpu.VMEM((NOBS, 128), f32),
        ],
        compiler_params=kernel_params(40),
        cost_estimate=pl.CostEstimate(flops=12 * 10**9, bytes_accessed=8 * 2**20, transcendentals=10**5),
        name="observations",
    )(position, plan, facts, own, other)


def half_of(column_facts, second):
    half = column_facts[:, 2:3] > 0.5
    return jnp.logical_not(half) if second else half


def covariance_kernel(second, position_ref, block_ref, anomalies_high_ref, anomalies_low_ref, facts_ref, *refs):
    out_refs, (total_ref, pair_ref) = refs[:SUMS], refs[SUMS:]
    lane_block = lax.broadcasted_iota(i32, (NOBS, 4 * GROUP), 1) >> 6
    pair_ref[...] = (facts_ref[:, 1:2] - lane_block.astype(f32)).astype(bf16)
    total_ref[...] = jnp.zeros_like(total_ref)

    def step(g, carry):
        found = pair_ref[...] == jnp.full((NOBS, 4 * GROUP), (g * 4).astype(f32)).astype(bf16)
        zero = jnp.zeros((NOBS, 4 * GROUP), bf16)
        left_high = jnp.where(found, anomalies_high_ref[...], zero)
        left_low = jnp.where(found, anomalies_low_ref[...], zero)
        right = jnp.concatenate(
            [block_ref[pl.ds(g * 4 + u, GROUP, stride=PAIRS), :] for u in range(4)], axis=0
        )
        right_high, right_low = two_parts(right)
        both = dot(left_high, jnp.concatenate([right_high, right_low], axis=1))
        total_ref[...] += both[:, :LANES] + both[:, LANES:] + dot(left_low, right_high)
        return carry

    lax.fori_loop(0, PAIRS // 4, step, 0)
    total = total_ref[...]
    other = pltpu.roll(total, HALF, 1)
    half = half_of(facts_ref[...], second)
    low_lanes = lax.broadcasted_iota(i32, (NOBS // 2, LANES), 1) < HALF
    upper = jnp.where(half, other, total)[: NOBS // 2]
    lower = jnp.where(half, total, other)[NOBS // 2 :]
    total_ref[0 : NOBS // 2, :] = jnp.where(low_lanes, upper, lower)
    for d in range(SUMS):
        start = ((position_ref[1] + d) & (SUMS - 1)) * CHUNK
        out_refs[d][...] = total_ref[pl.ds(pl.multiple_of(start, CHUNK), CHUNK), :]


def covariances(second, position, block, anomalies_high, anomalies_low, facts):
    return pl.pallas_call(
        functools.partial(covariance_kernel, second),
        out_shape=(struct((CHUNK, LANES)),) * SUMS,
        in_specs=[SMEM] + [VMEM] * 4,
        out_specs=(VMEM,) * SUMS,
        scratch_shapes=[pltpu.VMEM((NOBS, LANES), f32), pltpu.VMEM((NOBS, 4 * GROUP), bf16)],
        compiler_params=kernel_params(24),
        cost_estimate=pl.CostEstimate(flops=3 * 10**9, bytes_accessed=4 * 2**20, transcendentals=0),
        name="covariances",
    )(position, block.reshape(GROUP * PAIRS, LANES), anomalies_high, anomalies_low, facts)


def update_kernel(
    second, position_ref, *refs
):
    sums_refs = refs[:SUMS]
    (block_ref, increments_high_ref, increments_low_ref, links_high_ref, links_low_ref,
     facts_ref, row_facts_ref, out_ref, sums_ref, coefficient_ref, right_ref) = refs[SUMS:]
    for d in range(SUMS):
        start = ((position_ref[1] - d) & (SUMS - 1)) * CHUNK
        sums_ref[pl.ds(pl.multiple_of(start, CHUNK), CHUNK), :] = sums_refs[d][...]
    packed = sums_ref[...]
    weight = facts_ref[:, 0:1]
    coefficient_ref[0 : NOBS // 2, :] = packed * weight[: NOBS // 2]
    coefficient_ref[NOBS // 2 :, :] = pltpu.roll(packed, HALF, 1) * weight[NOBS // 2 :]
    for b in range(1, BATCHES):
        here = slice(b * BATCH_OBS, (b + 1) * BATCH_OBS)
        before = slice(0, b * BATCH_OBS)
        coefficient_ref[here, :] += dot_parts(
            links_high_ref[here, before], links_low_ref[here, before], *two_parts(coefficient_ref[before, :])
        )
    coefficient = coefficient_ref[...]
    half = half_of(facts_ref[...], second)
    high_lanes = lax.broadcasted_iota(i32, (NOBS, LANES), 1) >= HALF
    placed = jnp.where(
        high_lanes,
        jnp.where(half, pltpu.roll(coefficient, HALF, 1), 0.0),
        jnp.where(half, 0.0, coefficient),
    )
    right_high, right_low = two_parts(placed)
    right_ref[:, :LANES] = right_high
    right_ref[:, LANES:] = right_low
    pair_row = row_facts_ref[...].astype(bf16)[0:1, :]

    def step(g, carry):
        highs, lows = [], []
        zero = jnp.zeros((GROUP, NOBS), bf16)
        for u in range(4):
            found = pair_row == jnp.full((1, NOBS), (g * 4 + u).astype(f32)).astype(bf16)
            found = jnp.broadcast_to(found, (GROUP, NOBS))
            highs.append(jnp.where(found, increments_high_ref[...], zero))
            lows.append(jnp.where(found, increments_low_ref[...], zero))
        both = dot(jnp.concatenate(highs, axis=0), right_ref[...])
        change = both[:, :LANES] + both[:, LANES:] + dot(jnp.concatenate(lows, axis=0), right_ref[:, :LANES])
        for u in range(4):
            rows = pl.ds(g * 4 + u, GROUP, stride=PAIRS)
            out_ref[rows, :] = block_ref[rows, :] + change[u * GROUP : (u + 1) * GROUP]
        return carry

    lax.fori_loop(0, PAIRS // 4, step, 0)


def updated(second, position, sums, block, increments_high, increments_low, links_high, links_low, facts, row_facts):
    out = pl.pallas_call(
        functools.partial(update_kernel, second),
        out_shape=struct((GROUP * PAIRS, LANES)),
        in_specs=[SMEM] + [VMEM] * (SUMS + 7),
        out_specs=VMEM,
        scratch_shapes=[
            pltpu.VMEM((NOBS // 2, LANES), f32),
            pltpu.VMEM((NOBS, LANES), f32),
            pltpu.VMEM((NOBS, 2 * LANES), bf16),
        ],
        compiler_params=kernel_params(32),
        cost_estimate=pl.CostEstimate(flops=4 * 10**9, bytes_accessed=8 * 2**20, transcendentals=0),
        name="updated",
    )(
        position, *sums, block.reshape(GROUP * PAIRS, LANES), increments_high, increments_low,
        links_high, links_low, facts, row_facts,
    )
    return out.reshape(GROUP, PAIRS, LANES)


def exchange(value, axes=PEERS):
    return lax.all_to_all(value, axes, 0, 0, tiled=True)


def passed_along(value, by):
    return lax.ppermute(value, "h", [(i, (i + by) % SUMS) for i in range(SUMS)])


def summed(parts):
    total = parts[0]
    for by in range(1, SUMS):
        total = total + passed_along(parts[by], by)
    return (total, *(passed_along(total, by) for by in range(1, SUMS)))


def shards(state, locations, tile_mask, plan, obs_value, obs_error):
    residue = lax.axis_index(PEERS) // SLICES
    position = jnp.stack([residue, lax.axis_index("h"), lax.axis_index("c")]).astype(i32)
    rows = state.reshape(ROWS, LANES)

    tiles_here = tile_mask.shape[0]
    tiles = locations // TILE
    nth = jnp.arange(16, dtype=i32)[:, None]
    local = (tiles[None, :] - RADIUS + nth - lax.axis_index(ALL) * tiles_here) & (NTILES - 1)
    masks = jnp.zeros((16, NOBS), i32)
    for i in range(tiles_here):
        masks = masks + jnp.where((local == i) & (nth < WINDOW), tile_mask[i][None, :], 0)
    masks = exchange(masks.astype(f32).reshape(GROUP_CHIPS, 4, LANES), CHIPS).sum(axis=0)

    columns = own_columns(plan, locations, rows)
    mine = jnp.concatenate([columns, masks], axis=0)
    all_four = [mine] + [passed_along(mine, by) for by in range(1, SUMS)]
    payload = jnp.concatenate(
        [*(each[0:8] for each in all_four), sum(each[8:12] for each in all_four), jnp.zeros((4, LANES), f32)], axis=0
    )
    first, second = spread_out(rows)
    first, _ = lax.optimization_barrier((first, masks))
    first = exchange(first)
    payload, first = lax.optimization_barrier((payload, first))
    gathered = exchange(jnp.broadcast_to(payload[None], (GROUP_CHIPS, 40, LANES)), CHIPS)
    second, gathered = lax.optimization_barrier((second, gathered))
    second = exchange(second)

    other = lax.ppermute(gathered, "c", [(0, 1), (1, 0)])
    facts = jnp.concatenate(
        [tiles.astype(f32)[None], obs_value[None], obs_error[None], jnp.zeros((5, NOBS), f32)], axis=0
    )
    (anomalies_high, anomalies_low, increments_high, increments_low, links_high, links_low, column_facts, row_facts) = (
        observations(
            position, plan[None], facts, gathered.reshape(-1, LANES), other.reshape(-1, LANES)
        )
    )

    def covariance_parts(is_second, block):
        return covariances(is_second, position, block, anomalies_high, anomalies_low, column_facts)

    def update(is_second, sums, block):
        return updated(
            is_second, position, sums, block,
            increments_high, increments_low, links_high, links_low, column_facts, row_facts,
        )

    first_sums = summed(covariance_parts(False, first))
    second_parts = covariance_parts(True, second)
    first_sums, second_parts = lax.optimization_barrier((first_sums, second_parts))
    first = exchange(update(False, first_sums, first))
    second = exchange(update(True, summed(second_parts), second))
    return collect(first, second).reshape(state.shape)


def solution(mesh):
    fine = Mesh(mesh.devices.reshape(4, 4, 2, 2, 4), ALL)
    placed = (P(ALL, None), P(), P(ALL, None), P(), P(), P())
    return jax.shard_map(shards, mesh=fine, in_specs=placed, out_specs=P(ALL, None), check_vma=False)
```

```python
import functools

import jax
import jax.numpy as jnp
from jax import lax
from jax.experimental import pallas as pl
from jax.experimental.pallas import tpu as pltpu
from jax.sharding import Mesh, PartitionSpec as P

MEMBERS = 256
TILE = 512
NTILES = 2048
RADIUS = 4
WINDOW = 2 * RADIUS + 1
BATCH_OBS = 256
BATCHES = 4
NOBS = BATCH_OBS * BATCHES

ALL = ("y", "h", "l", "c", "x")
PEERS = ("c", "y", "l", "x")
CHIPS = ("y", "l", "x")
GROUP = 64
CORES = 2
GROUP_CHIPS = GROUP // CORES
SUMS = 4
RESIDUES = 16
SLICES = 4
LANES = 128
HALF = 64
OWN_TILES = NTILES // RESIDUES
PAIRS = OWN_TILES // 2
ROWS = NTILES * TILE // LANES
CHUNK = NOBS // 2 // SUMS

epsilon = 1e-06
f32 = jnp.float32
bf16 = jnp.bfloat16
i32 = jnp.int32

VMEM = pl.BlockSpec(memory_space=pltpu.VMEM)
SMEM = pl.BlockSpec(memory_space=pltpu.SMEM)


def kernel_params(mib):
    return pltpu.CompilerParams(vmem_limit_bytes=mib * 1024 * 1024)


def struct(shape, dtype=f32):
    return jax.ShapeDtypeStruct(shape, dtype)


def two_parts(value):
    high = value.astype(bf16)
    return high, (value - high.astype(f32)).astype(bf16)


def three_parts(value):
    high = value.astype(bf16)
    rest = value - high.astype(f32)
    middle = rest.astype(bf16)
    return high, middle, (rest - middle.astype(f32)).astype(bf16)


def dot(a, b):
    return lax.dot_general(a, b, (((1,), (0,)), ((), ())), preferred_element_type=f32)


def dot_parts(a_high, a_low, b_high, b_low):
    return dot(a_high, b_high) + dot(a_high, b_low) + dot(a_low, b_high)


def accurate_dot(a, b):
    return dot_parts(*two_parts(a), *two_parts(b))


def columns_kernel(plan_ref, locations_ref, state_ref, out_ref, picked_ref):
    lane = lax.broadcasted_iota(i32, (1, LANES), 1)

    def step(i, carry):
        base = pl.multiple_of(i * 8, 8)
        found = []
        for u in range(8):
            where = locations_ref[plan_ref[base + u]]
            row = state_ref[pl.ds(where >> 7, 1), :]
            found.append(jnp.where(lane == (where & (LANES - 1)), row, 0.0))
        picked_ref[pl.ds(base, 8), :] = jnp.concatenate(found, axis=0)
        return carry

    lax.fori_loop(0, NOBS // 8, step, 0, unroll=2)
    ones = jnp.ones((16, LANES), bf16)
    total = jnp.zeros((16, NOBS), f32)
    for part in three_parts(picked_ref[...]):
        total = total + lax.dot_general(ones, part, (((1,), (1,)), ((), ())), preferred_element_type=f32)
    for g in range(NOBS // LANES):
        out_ref[pl.ds(g, 1), :] = total[0:1, g * LANES : (g + 1) * LANES]


def own_columns(plan, locations, rows):
    return pl.pallas_call(
        columns_kernel,
        out_shape=struct((NOBS // LANES, LANES)),
        in_specs=[SMEM, SMEM, VMEM],
        out_specs=VMEM,
        scratch_shapes=[pltpu.VMEM((NOBS, LANES), f32)],
        compiler_params=kernel_params(24),
        cost_estimate=pl.CostEstimate(flops=10**6, bytes_accessed=8 * 2**20, transcendentals=0),
        name="own_columns",
    )(plan, locations, rows)


def spread_kernel(state_ref, first_ref, second_ref):
    low_lanes = lax.broadcasted_iota(i32, (PAIRS, LANES), 1) < HALF

    def step(d, carry):
        upper = state_ref[pl.ds(d, PAIRS, stride=GROUP), :]
        lower = state_ref[pl.ds(d + ROWS // 2, PAIRS, stride=GROUP), :]
        first_ref[d] = jnp.where(low_lanes, upper, lower)
        second_ref[d] = jnp.where(low_lanes, lower, upper)
        return carry

    lax.fori_loop(0, GROUP, step, 0)


def spread_out(rows):
    half = struct((GROUP, PAIRS, LANES))
    return pl.pallas_call(
        spread_kernel,
        out_shape=(half, half),
        in_specs=[VMEM],
        out_specs=(VMEM, VMEM),
        compiler_params=kernel_params(24),
        cost_estimate=pl.CostEstimate(flops=10**6, bytes_accessed=8 * 2**20, transcendentals=0),
        name="spread_out",
    )(rows)


def collect_kernel(first_ref, second_ref, state_ref):
    low_lanes = lax.broadcasted_iota(i32, (PAIRS, LANES), 1) < HALF

    def step(d, carry):
        first = first_ref[d]
        second = second_ref[d]
        state_ref[pl.ds(d, PAIRS, stride=GROUP), :] = jnp.where(low_lanes, first, second)
        state_ref[pl.ds(d + ROWS // 2, PAIRS, stride=GROUP), :] = jnp.where(low_lanes, second, first)
        return carry

    lax.fori_loop(0, GROUP, step, 0)


def collect(first, second):
    return pl.pallas_call(
        collect_kernel,
        out_shape=struct((ROWS, LANES)),
        in_specs=[VMEM, VMEM],
        out_specs=VMEM,
        compiler_params=kernel_params(24),
        cost_estimate=pl.CostEstimate(flops=10**6, bytes_accessed=8 * 2**20, transcendentals=0),
        name="collect",
    )(first, second)


def observation_kernel(
    position_ref, plan_ref, facts_ref, own_ref, other_ref,
    anomalies_high_ref, anomalies_low_ref, increments_high_ref, increments_low_ref,
    links_high_ref, links_low_ref, column_facts_ref, row_facts_ref,
    ensemble_ref, increments_ref, one_hot_ref, facts_scratch, in_columns_ref,
):
    core = position_ref[2]
    for d in range(SUMS):
        for gathered_ref, start in ((own_ref, core), (other_ref, 1 - core)):
            rows = pl.ds(pl.multiple_of(d * GROUP + start * GROUP_CHIPS, GROUP_CHIPS), GROUP_CHIPS)
            for g in range(NOBS // LANES):
                ensemble_ref[rows, g * LANES : (g + 1) * LANES] = gathered_ref[
                    pl.ds(d * 8 + g, GROUP_CHIPS, stride=40), :
                ]
    for g in range(NOBS // LANES):
        rows = pl.ds((g // 4) * 40 + 32 + g % 4, 16, stride=80)
        facts_scratch[0:16, g * LANES : (g + 1) * LANES] = own_ref[rows, :] + other_ref[rows, :]
    facts_scratch[16:24, :] = facts_ref[...]
    facts_scratch[24:128, :] = jnp.zeros((104, NOBS), f32)
    source = lax.broadcasted_iota(i32, (NOBS, NOBS), 0)
    one_hot_ref[...] = jnp.where(source == plan_ref[...], 1.0, 0.0).astype(bf16)
    high, middle, low = three_parts(facts_scratch[0:32, :])
    ordered = dot(high, one_hot_ref[...]) + dot(middle, one_hot_ref[...]) + dot(low, one_hot_ref[...])
    facts_scratch[0:32, :] = ordered
    for g in range(NOBS // LANES):
        in_columns_ref[g * LANES : (g + 1) * LANES, :] = facts_scratch[:, g * LANES : (g + 1) * LANES].T

    residue = position_ref[0]
    tile_row = facts_scratch[16:17, :].astype(i32)
    tile_column = in_columns_ref[:, 16:17].astype(i32)
    nth_row = (residue - tile_row + RADIUS) & (RESIDUES - 1)
    nth_column = (residue - tile_column + RADIUS) & (RESIDUES - 1)
    own_row = ((tile_row - RADIUS + nth_row) & (NTILES - 1)) >> 4
    own_column = ((tile_column - RADIUS + nth_column) & (NTILES - 1)) >> 4
    own_row = jnp.where(nth_row < WINDOW, own_row, -1)
    own_column = jnp.where(nth_column < WINDOW, own_column, -2)
    mask_column = jnp.zeros((NOBS, 1), f32)
    for n in range(WINDOW):
        mask_column = mask_column + jnp.where(nth_column == n, in_columns_ref[:, n : n + 1], 0.0)

    row_facts_ref[...] = jnp.broadcast_to(jnp.where(own_row < 0, -256, own_row & (PAIRS - 1)).astype(f32), (16, NOBS))
    lane = lax.broadcasted_iota(i32, (NOBS, LANES), 1)
    pair_column = jnp.where(own_column < 0, -256, own_column & (PAIRS - 1)).astype(f32)
    half_column = jnp.where(own_column >= PAIRS, 1.0, 0.0)

    for b in range(BATCHES):
        here = slice(b * BATCH_OBS, (b + 1) * BATCH_OBS)
        prior = ensemble_ref[:, here]
        average = jnp.sum(prior, axis=0, keepdims=True) / MEMBERS
        anomaly = prior - average
        spread = jnp.sum(anomaly * anomaly, axis=0, keepdims=True) / (MEMBERS - 1) + epsilon
        value = facts_scratch[17:18, here]
        error = facts_scratch[18:19, here]
        shrink = jnp.sqrt(error / (spread + error))
        moved = (average * error + value * spread) / (spread + error)
        increments = (shrink - 1.0) * anomaly + (moved - average)
        increments_ref[:, here] = increments
        turned = anomaly.T
        spread_column = jnp.sum(turned * turned, axis=1, keepdims=True) / (MEMBERS - 1) + epsilon
        gain_column = 1.0 / ((MEMBERS - 1) * spread_column)
        turned_high, turned_low = two_parts(turned)
        own_high = turned_high[:, 0:GROUP]
        own_low = turned_low[:, 0:GROUP]
        anomalies_high_ref[here, :] = jnp.concatenate([own_high] * 4, axis=1)
        anomalies_low_ref[here, :] = jnp.concatenate([own_low] * 4, axis=1)
        own_increments = two_parts(increments[0:GROUP, :])
        increments_high_ref[:, here] = own_increments[0]
        increments_low_ref[:, here] = own_increments[1]
        weight = mask_column[here] * gain_column
        column_facts_ref[here, :] = jnp.where(
            lane[here] == 0, weight, jnp.where(lane[here] == 1, pair_column[here], half_column[here])
        )
        if b > 0:
            before = b * BATCH_OBS
            links = accurate_dot(turned, increments_ref[:, 0:before])
            links = jnp.where(own_column[here] == own_row[:, 0:before], links * weight, 0.0)
            links_high, links_low = two_parts(links)
            links_high_ref[here, 0:before] = links_high
            links_low_ref[here, 0:before] = links_low
        if b < BATCHES - 1:
            after = slice((b + 1) * BATCH_OBS, NOBS)
            later = ensemble_ref[:, after]
            covariance = dot_parts(turned_high, turned_low, *two_parts(later))
            apart = (tile_row[:, after] - tile_column[here] + RADIUS) & (NTILES - 1)
            masks = jnp.zeros(apart.shape, f32)
            for n in range(WINDOW):
                masks = jnp.where(apart == n, in_columns_ref[here, n : n + 1], masks)
            ensemble_ref[:, after] = later + accurate_dot(increments, covariance * masks * gain_column)


def observations(position, plan, facts, own, other):
    wide = struct((NOBS, 4 * GROUP), bf16)
    narrow = struct((GROUP, NOBS), bf16)
    links = struct((NOBS, NOBS), bf16)
    return pl.pallas_call(
        observation_kernel,
        out_shape=(wide, wide, narrow, narrow, links, links, struct((NOBS, LANES)), struct((16, NOBS))),
        in_specs=[SMEM, VMEM, VMEM, VMEM, VMEM],
        out_specs=(VMEM,) * 8,
        scratch_shapes=[
            pltpu.VMEM((MEMBERS, NOBS), f32),
            pltpu.VMEM((MEMBERS, NOBS), f32),
            pltpu.VMEM((NOBS, NOBS), bf16),
            pltpu.VMEM((128, NOBS), f32),
            pltpu.VMEM((NOBS, 128), f32),
        ],
        compiler_params=kernel_params(40),
        cost_estimate=pl.CostEstimate(flops=12 * 10**9, bytes_accessed=8 * 2**20, transcendentals=10**5),
        name="observations",
    )(position, plan, facts, own, other)


def half_of(column_facts, second):
    half = column_facts[:, 2:3] > 0.5
    return jnp.logical_not(half) if second else half


def covariance_kernel(second, position_ref, block_ref, anomalies_high_ref, anomalies_low_ref, facts_ref, *refs):
    out_refs, (total_ref, pair_ref) = refs[:SUMS], refs[SUMS:]
    lane_block = lax.broadcasted_iota(i32, (NOBS, 4 * GROUP), 1) >> 6
    pair_ref[...] = (facts_ref[:, 1:2] - lane_block.astype(f32)).astype(bf16)
    total_ref[...] = jnp.zeros_like(total_ref)

    def step(g, carry):
        found = pair_ref[...] == jnp.full((NOBS, 4 * GROUP), (g * 4).astype(f32)).astype(bf16)
        zero = jnp.zeros((NOBS, 4 * GROUP), bf16)
        left_high = jnp.where(found, anomalies_high_ref[...], zero)
        left_low = jnp.where(found, anomalies_low_ref[...], zero)
        right = jnp.concatenate(
            [block_ref[pl.ds(g * 4 + u, GROUP, stride=PAIRS), :] for u in range(4)], axis=0
        )
        right_high, right_low = two_parts(right)
        both = dot(left_high, jnp.concatenate([right_high, right_low], axis=1))
        total_ref[...] += both[:, :LANES] + both[:, LANES:] + dot(left_low, right_high)
        return carry

    lax.fori_loop(0, PAIRS // 4, step, 0)
    total = total_ref[...]
    other = pltpu.roll(total, HALF, 1)
    half = half_of(facts_ref[...], second)
    low_lanes = lax.broadcasted_iota(i32, (NOBS // 2, LANES), 1) < HALF
    upper = jnp.where(half, other, total)[: NOBS // 2]
    lower = jnp.where(half, total, other)[NOBS // 2 :]
    total_ref[0 : NOBS // 2, :] = jnp.where(low_lanes, upper, lower)
    for d in range(SUMS):
        start = ((position_ref[1] + d) & (SUMS - 1)) * CHUNK
        out_refs[d][...] = total_ref[pl.ds(pl.multiple_of(start, CHUNK), CHUNK), :]


def covariances(second, position, block, anomalies_high, anomalies_low, facts):
    return pl.pallas_call(
        functools.partial(covariance_kernel, second),
        out_shape=(struct((CHUNK, LANES)),) * SUMS,
        in_specs=[SMEM] + [VMEM] * 4,
        out_specs=(VMEM,) * SUMS,
        scratch_shapes=[pltpu.VMEM((NOBS, LANES), f32), pltpu.VMEM((NOBS, 4 * GROUP), bf16)],
        compiler_params=kernel_params(24),
        cost_estimate=pl.CostEstimate(flops=3 * 10**9, bytes_accessed=4 * 2**20, transcendentals=0),
        name="covariances",
    )(position, block.reshape(GROUP * PAIRS, LANES), anomalies_high, anomalies_low, facts)


def update_kernel(
    second, position_ref, *refs
):
    sums_refs = refs[:SUMS]
    (block_ref, increments_high_ref, increments_low_ref, links_high_ref, links_low_ref,
     facts_ref, row_facts_ref, out_ref, sums_ref, coefficient_ref, right_ref) = refs[SUMS:]
    for d in range(SUMS):
        start = ((position_ref[1] - d) & (SUMS - 1)) * CHUNK
        sums_ref[pl.ds(pl.multiple_of(start, CHUNK), CHUNK), :] = sums_refs[d][...]
    packed = sums_ref[...]
    weight = facts_ref[:, 0:1]
    coefficient_ref[0 : NOBS // 2, :] = packed * weight[: NOBS // 2]
    coefficient_ref[NOBS // 2 :, :] = pltpu.roll(packed, HALF, 1) * weight[NOBS // 2 :]
    for b in range(1, BATCHES):
        here = slice(b * BATCH_OBS, (b + 1) * BATCH_OBS)
        before = slice(0, b * BATCH_OBS)
        coefficient_ref[here, :] += dot_parts(
            links_high_ref[here, before], links_low_ref[here, before], *two_parts(coefficient_ref[before, :])
        )
    coefficient = coefficient_ref[...]
    half = half_of(facts_ref[...], second)
    high_lanes = lax.broadcasted_iota(i32, (NOBS, LANES), 1) >= HALF
    placed = jnp.where(
        high_lanes,
        jnp.where(half, pltpu.roll(coefficient, HALF, 1), 0.0),
        jnp.where(half, 0.0, coefficient),
    )
    right_high, right_low = two_parts(placed)
    right_ref[:, :LANES] = right_high
    right_ref[:, LANES:] = right_low
    pair_row = row_facts_ref[...].astype(bf16)[0:1, :]

    def step(g, carry):
        highs, lows = [], []
        zero = jnp.zeros((GROUP, NOBS), bf16)
        for u in range(4):
            found = pair_row == jnp.full((1, NOBS), (g * 4 + u).astype(f32)).astype(bf16)
            found = jnp.broadcast_to(found, (GROUP, NOBS))
            highs.append(jnp.where(found, increments_high_ref[...], zero))
            lows.append(jnp.where(found, increments_low_ref[...], zero))
        both = dot(jnp.concatenate(highs, axis=0), right_ref[...])
        change = both[:, :LANES] + both[:, LANES:] + dot(jnp.concatenate(lows, axis=0), right_ref[:, :LANES])
        for u in range(4):
            rows = pl.ds(g * 4 + u, GROUP, stride=PAIRS)
            out_ref[rows, :] = block_ref[rows, :] + change[u * GROUP : (u + 1) * GROUP]
        return carry

    lax.fori_loop(0, PAIRS // 4, step, 0)


def updated(second, position, sums, block, increments_high, increments_low, links_high, links_low, facts, row_facts):
    out = pl.pallas_call(
        functools.partial(update_kernel, second),
        out_shape=struct((GROUP * PAIRS, LANES)),
        in_specs=[SMEM] + [VMEM] * (SUMS + 7),
        out_specs=VMEM,
        scratch_shapes=[
            pltpu.VMEM((NOBS // 2, LANES), f32),
            pltpu.VMEM((NOBS, LANES), f32),
            pltpu.VMEM((NOBS, 2 * LANES), bf16),
        ],
        compiler_params=kernel_params(32),
        cost_estimate=pl.CostEstimate(flops=4 * 10**9, bytes_accessed=8 * 2**20, transcendentals=0),
        name="updated",
    )(
        position, *sums, block.reshape(GROUP * PAIRS, LANES), increments_high, increments_low,
        links_high, links_low, facts, row_facts,
    )
    return out.reshape(GROUP, PAIRS, LANES)


def exchange(value, axes=PEERS):
    return lax.all_to_all(value, axes, 0, 0, tiled=True)


def passed_along(value, by):
    return lax.ppermute(value, "h", [(i, (i + by) % SUMS) for i in range(SUMS)])


def scattered(parts):
    total = parts[0]
    for by in range(1, SUMS):
        total = total + passed_along(parts[by], by)
    return total


def shared(total):
    return (total, *(passed_along(total, by) for by in range(1, SUMS)))


def shards(state, locations, tile_mask, plan, obs_value, obs_error):
    residue = lax.axis_index(PEERS) // SLICES
    position = jnp.stack([residue, lax.axis_index("h"), lax.axis_index("c")]).astype(i32)
    rows = state.reshape(ROWS, LANES)

    tiles_here = tile_mask.shape[0]
    tiles = locations // TILE
    nth = jnp.arange(16, dtype=i32)[:, None]
    local = (tiles[None, :] - RADIUS + nth - lax.axis_index(ALL) * tiles_here) & (NTILES - 1)
    masks = jnp.zeros((16, NOBS), i32)
    for i in range(tiles_here):
        masks = masks + jnp.where((local == i) & (nth < WINDOW), tile_mask[i][None, :], 0)
    masks = exchange(masks.astype(f32).reshape(GROUP_CHIPS, 4, LANES), CHIPS).sum(axis=0)

    columns = own_columns(plan, locations, rows)
    mine = jnp.concatenate([columns, masks], axis=0)
    all_four = [mine] + [passed_along(mine, by) for by in range(1, SUMS)]
    payload = jnp.concatenate(
        [*(each[0:8] for each in all_four), sum(each[8:12] for each in all_four), jnp.zeros((4, LANES), f32)], axis=0
    )
    first, second = spread_out(rows)
    first, _ = lax.optimization_barrier((first, masks))
    first = exchange(first)
    payload, first = lax.optimization_barrier((payload, first))
    gathered = exchange(jnp.broadcast_to(payload[None], (GROUP_CHIPS, 40, LANES)), CHIPS)
    second, gathered = lax.optimization_barrier((second, gathered))
    second = exchange(second)

    other = lax.ppermute(gathered, "c", [(0, 1), (1, 0)])
    facts = jnp.concatenate(
        [tiles.astype(f32)[None], obs_value[None], obs_error[None], jnp.zeros((5, NOBS), f32)], axis=0
    )
    (anomalies_high, anomalies_low, increments_high, increments_low, links_high, links_low, column_facts, row_facts) = (
        observations(
            position, plan[None], facts, gathered.reshape(-1, LANES), other.reshape(-1, LANES)
        )
    )

    def covariance_parts(is_second, block):
        return covariances(is_second, position, block, anomalies_high, anomalies_low, column_facts)

    def update(is_second, sums, block):
        return updated(
            is_second, position, sums, block,
            increments_high, increments_low, links_high, links_low, column_facts, row_facts,
        )

    first_sums = shared(scattered(covariance_parts(False, first)))
    second_parts = covariance_parts(True, second)
    first_sums, second_parts = lax.optimization_barrier((first_sums, second_parts))
    first = update(False, first_sums, first)
    first, second_total = lax.optimization_barrier((first, scattered(second_parts)))
    second_sums = shared(second_total)
    first = exchange(first)
    second = exchange(update(True, second_sums, second))
    return collect(first, second).reshape(state.shape)


def solution(mesh):
    fine = Mesh(mesh.devices.reshape(4, 4, 2, 2, 4), ALL)
    placed = (P(ALL, None), P(), P(ALL, None), P(), P(), P())
    return jax.shard_map(shards, mesh=fine, in_specs=placed, out_specs=P(ALL, None), check_vma=False)
```

```python
import functools

import jax
import jax.numpy as jnp
from jax import lax
from jax.experimental import pallas as pl
from jax.experimental.pallas import tpu as pltpu
from jax.sharding import Mesh, PartitionSpec as P

MEMBERS = 256
TILE = 512
NTILES = 2048
RADIUS = 4
WINDOW = 2 * RADIUS + 1
BATCH_OBS = 256
BATCHES = 4
NOBS = BATCH_OBS * BATCHES

ALL = ("y", "h", "l", "c", "x")
PEERS = ("c", "y", "l", "x")
CHIPS = ("y", "l", "x")
GROUP = 64
CORES = 2
GROUP_CHIPS = GROUP // CORES
SUMS = 4
RESIDUES = 16
SLICES = 4
LANES = 128
OWN_TILES = NTILES // RESIDUES
ROWS = NTILES * TILE // LANES
CHUNK = NOBS // SUMS
FOUR = 4
WIDE = FOUR * GROUP
GROUPS = OWN_TILES // FOUR
WINDOW_ROWS = 128
WINDOW_COLUMNS = 256
PADDED_ROWS = NOBS + WINDOW_ROWS
PADDED_COLUMNS = NOBS + WINDOW_COLUMNS
NOWHERE = -512
BLOCK_TILES = 16

epsilon = 1e-06
f32 = jnp.float32
bf16 = jnp.bfloat16
i32 = jnp.int32

VMEM = pl.BlockSpec(memory_space=pltpu.VMEM)
SMEM = pl.BlockSpec(memory_space=pltpu.SMEM)


def kernel_params(mib):
    return pltpu.CompilerParams(vmem_limit_bytes=mib * 1024 * 1024)


def struct(shape, dtype=f32):
    return jax.ShapeDtypeStruct(shape, dtype)


def two_parts(value):
    high = value.astype(bf16)
    return high, (value - high.astype(f32)).astype(bf16)


def three_parts(value):
    high = value.astype(bf16)
    rest = value - high.astype(f32)
    middle = rest.astype(bf16)
    return high, middle, (rest - middle.astype(f32)).astype(bf16)


def dot(a, b):
    return lax.dot_general(a, b, (((1,), (0,)), ((), ())), preferred_element_type=f32)


def dot_parts(a_high, a_low, b_high, b_low):
    return dot(a_high, b_high) + dot(a_high, b_low) + dot(a_low, b_high)


def accurate_dot(a, b):
    return dot_parts(*two_parts(a), *two_parts(b))


def columns_kernel(plan_ref, locations_ref, state_ref, out_ref, picked_ref):
    lane = lax.broadcasted_iota(i32, (1, LANES), 1)

    def step(i, carry):
        base = pl.multiple_of(i * 8, 8)
        found = []
        for u in range(8):
            where = locations_ref[plan_ref[base + u]]
            row = state_ref[pl.ds(where >> 7, 1), :]
            found.append(jnp.where(lane == (where & (LANES - 1)), row, 0.0))
        picked_ref[pl.ds(base, 8), :] = jnp.concatenate(found, axis=0)
        return carry

    lax.fori_loop(0, NOBS // 8, step, 0, unroll=2)
    ones = jnp.ones((16, LANES), bf16)
    total = jnp.zeros((16, NOBS), f32)
    for part in three_parts(picked_ref[...]):
        total = total + lax.dot_general(ones, part, (((1,), (1,)), ((), ())), preferred_element_type=f32)
    for g in range(NOBS // LANES):
        out_ref[pl.ds(g, 1), :] = total[0:1, g * LANES : (g + 1) * LANES]


def own_columns(plan, locations, rows):
    return pl.pallas_call(
        columns_kernel,
        out_shape=struct((NOBS // LANES, LANES)),
        in_specs=[SMEM, SMEM, VMEM],
        out_specs=VMEM,
        scratch_shapes=[pltpu.VMEM((NOBS, LANES), f32)],
        compiler_params=kernel_params(24),
        cost_estimate=pl.CostEstimate(flops=10**6, bytes_accessed=8 * 2**20, transcendentals=0),
        name="own_columns",
    )(plan, locations, rows)


def spread_kernel(state_ref, out_ref):
    for d in range(GROUP):
        out_ref[d] = state_ref[pl.ds(d, BLOCK_TILES, stride=GROUP), :]


def collect_kernel(in_ref, state_ref):
    for d in range(GROUP):
        state_ref[pl.ds(d, BLOCK_TILES, stride=GROUP), :] = in_ref[d]


def reordered(kernel, value, out_shape, name):
    by_device = pl.BlockSpec((GROUP, BLOCK_TILES, LANES), lambda i: (0, i, 0))
    by_row = pl.BlockSpec((GROUP * BLOCK_TILES, LANES), lambda i: (i, 0))
    specs = (by_row, by_device) if value.ndim == 2 else (by_device, by_row)
    return pl.pallas_call(
        kernel,
        grid=(OWN_TILES // BLOCK_TILES,),
        out_shape=struct(out_shape),
        in_specs=[specs[0]],
        out_specs=specs[1],
        compiler_params=kernel_params(16),
        cost_estimate=pl.CostEstimate(flops=10**6, bytes_accessed=8 * 2**20, transcendentals=0),
        name=name,
    )(value)


def spread_out(rows):
    return reordered(spread_kernel, rows, (GROUP, OWN_TILES, LANES), "spread_out")


def collect(blocks):
    return reordered(collect_kernel, blocks, (ROWS, LANES), "collect")


def observation_kernel(
    position_ref, plan_ref, facts_ref, own_ref, other_ref,
    anomalies_high_ref, anomalies_low_ref, tiles_ref, factors_high_ref, factors_low_ref, tile_rows_ref,
    ensemble_ref, increments_ref, one_hot_ref, facts_scratch, in_columns_ref,
    turned_ref, links_high_ref, links_low_ref, sort_ref, sort_back_ref,
):
    core = position_ref[2]
    for d in range(SUMS):
        for gathered_ref, start in ((own_ref, core), (other_ref, 1 - core)):
            rows = pl.ds(pl.multiple_of(d * GROUP + start * GROUP_CHIPS, GROUP_CHIPS), GROUP_CHIPS)
            for g in range(NOBS // LANES):
                ensemble_ref[rows, g * LANES : (g + 1) * LANES] = gathered_ref[
                    pl.ds(d * 8 + g, GROUP_CHIPS, stride=40), :
                ]
    for g in range(NOBS // LANES):
        rows = pl.ds((g // 4) * 40 + 32 + g % 4, 16, stride=80)
        facts_scratch[0:16, g * LANES : (g + 1) * LANES] = own_ref[rows, :] + other_ref[rows, :]
    facts_scratch[16:24, :] = facts_ref[...]
    facts_scratch[24:128, :] = jnp.zeros((104, NOBS), f32)
    source = lax.broadcasted_iota(i32, (NOBS, NOBS), 0)
    one_hot_ref[...] = jnp.where(source == plan_ref[...], 1.0, 0.0).astype(bf16)
    high, middle, low = three_parts(facts_scratch[0:32, :])
    ordered = dot(high, one_hot_ref[...]) + dot(middle, one_hot_ref[...]) + dot(low, one_hot_ref[...])
    facts_scratch[0:32, :] = ordered
    for g in range(NOBS // LANES):
        in_columns_ref[g * LANES : (g + 1) * LANES, :] = facts_scratch[:, g * LANES : (g + 1) * LANES].T

    residue = position_ref[0]
    tile_row = facts_scratch[16:17, :].astype(i32)
    tile_column = in_columns_ref[:, 16:17].astype(i32)
    nth_row = (residue - tile_row + RADIUS) & (RESIDUES - 1)
    nth_column = (residue - tile_column + RADIUS) & (RESIDUES - 1)
    own_row = ((tile_row - RADIUS + nth_row) & (NTILES - 1)) >> 4
    own_column = ((tile_column - RADIUS + nth_column) & (NTILES - 1)) >> 4
    own_row = jnp.where(nth_row < WINDOW, own_row, -1)
    own_column = jnp.where(nth_column < WINDOW, own_column, -2)
    mask_column = jnp.zeros((NOBS, 1), f32)
    for n in range(WINDOW):
        mask_column = mask_column + jnp.where(nth_column == n, in_columns_ref[:, n : n + 1], 0.0)

    mask_row = jnp.zeros((1, NOBS), f32)
    for n in range(WINDOW):
        mask_row = mask_row + jnp.where(nth_row == n, facts_scratch[n : n + 1, :], 0.0)

    key_row = jnp.where(own_row < 0, OWN_TILES, own_row) * NOBS + lax.broadcasted_iota(i32, (1, NOBS), 1)
    key_column = jnp.where(own_column < 0, OWN_TILES, own_column) * NOBS + lax.broadcasted_iota(i32, (NOBS, 1), 0)
    rank_row = jnp.sum(jnp.where(key_column < key_row, 1.0, 0.0), axis=0, keepdims=True).astype(i32)
    rank_column = jnp.sum(jnp.where(key_row < key_column, 1.0, 0.0), axis=1, keepdims=True).astype(i32)
    sort_ref[...] = jnp.where(source == rank_row, 1.0, 0.0).astype(bf16)
    to = lax.broadcasted_iota(i32, (NOBS, NOBS), 1)
    sort_back_ref[...] = jnp.where(to == rank_column, 1.0, 0.0).astype(bf16)

    gain_rows = []
    for b in range(BATCHES):
        here = slice(b * BATCH_OBS, (b + 1) * BATCH_OBS)
        prior = ensemble_ref[:, here]
        average = jnp.sum(prior, axis=0, keepdims=True) / MEMBERS
        anomaly = prior - average
        spread = jnp.sum(anomaly * anomaly, axis=0, keepdims=True) / (MEMBERS - 1) + epsilon
        value = facts_scratch[17:18, here]
        error = facts_scratch[18:19, here]
        shrink = jnp.sqrt(error / (spread + error))
        moved = (average * error + value * spread) / (spread + error)
        increments = (shrink - 1.0) * anomaly + (moved - average)
        increments_ref[:, here] = increments
        turned = anomaly.T
        spread_column = jnp.sum(turned * turned, axis=1, keepdims=True) / (MEMBERS - 1) + epsilon
        gain_column = 1.0 / ((MEMBERS - 1) * spread_column)
        turned_high, turned_low = two_parts(turned)
        turned_ref[here, :] = jnp.concatenate([turned_high[:, 0:GROUP], turned_low[:, 0:GROUP]], axis=1)
        gain_rows.append(1.0 / ((MEMBERS - 1) * spread))
        weight = mask_column[here] * gain_column
        if b > 0:
            before = b * BATCH_OBS
            links = accurate_dot(turned, increments_ref[:, 0:before])
            links = jnp.where(own_column[here] == own_row[:, 0:before], links * weight, 0.0)
            links_high, links_low = two_parts(links)
            links_high_ref[here, 0:before] = links_high
            links_low_ref[here, 0:before] = links_low
        if b < BATCHES - 1:
            after = slice((b + 1) * BATCH_OBS, NOBS)
            later = ensemble_ref[:, after]
            covariance = dot_parts(turned_high, turned_low, *two_parts(later))
            apart = (tile_row[:, after] - tile_column[here] + RADIUS) & (NTILES - 1)
            masks = jnp.zeros(apart.shape, f32)
            for n in range(WINDOW):
                masks = jnp.where(apart == n, in_columns_ref[here, n : n + 1], masks)
            ensemble_ref[:, after] = later + accurate_dot(increments, covariance * masks * gain_column)

    for b in reversed(range(BATCHES - 1)):
        here = slice(b * BATCH_OBS, (b + 1) * BATCH_OBS)
        after = slice((b + 1) * BATCH_OBS, NOBS)
        increments_ref[0:GROUP, here] += dot_parts(
            *two_parts(increments_ref[0:GROUP, after]), links_high_ref[after, here], links_low_ref[after, here]
        )
    factors = increments_ref[0:GROUP, :] * (mask_row * jnp.concatenate(gain_rows, axis=1))

    tile_here = jnp.where(own_column < 0, NOWHERE, own_column).astype(f32)
    tile_here = jnp.broadcast_to(tile_here, (NOBS, LANES)).astype(bf16)
    sorted_columns = dot(sort_ref[...], jnp.concatenate([turned_ref[...], tile_here], axis=1))
    high = sorted_columns[:, 0:GROUP].astype(bf16)
    low = sorted_columns[:, GROUP : 2 * GROUP].astype(bf16)
    anomalies_high_ref[0:NOBS, :] = jnp.concatenate([high] * FOUR, axis=1)
    anomalies_low_ref[0:NOBS, :] = jnp.concatenate([low] * FOUR, axis=1)
    nth_of_four = (lax.broadcasted_iota(i32, (NOBS, WIDE), 1) >> 6).astype(f32)
    tiles_ref[0:NOBS, :] = (sorted_columns[:, LANES : LANES + 1] - nth_of_four).astype(bf16)
    padding = slice(NOBS, PADDED_ROWS)
    anomalies_high_ref[padding, :] = jnp.zeros((WINDOW_ROWS, WIDE), bf16)
    anomalies_low_ref[padding, :] = jnp.zeros((WINDOW_ROWS, WIDE), bf16)
    tiles_ref[padding, :] = jnp.full((WINDOW_ROWS, WIDE), NOWHERE, bf16)

    factors_high, factors_low = two_parts(factors)
    tile_there = jnp.where(own_row < 0, NOWHERE, own_row).astype(f32)
    tile_there = jnp.broadcast_to(tile_there, (GROUP, NOBS)).astype(bf16)
    sorted_rows = dot(jnp.concatenate([factors_high, factors_low, tile_there], axis=0), sort_back_ref[...]).astype(bf16)
    factors_high_ref[:, 0:NOBS] = sorted_rows[0:GROUP]
    factors_low_ref[:, 0:NOBS] = sorted_rows[GROUP : 2 * GROUP]
    tile_rows_ref[:, 0:NOBS] = sorted_rows[2 * GROUP : 3 * GROUP]
    padding = slice(NOBS, PADDED_COLUMNS)
    factors_high_ref[:, padding] = jnp.zeros((GROUP, WINDOW_COLUMNS), bf16)
    factors_low_ref[:, padding] = jnp.zeros((GROUP, WINDOW_COLUMNS), bf16)
    tile_rows_ref[:, padding] = jnp.full((GROUP, WINDOW_COLUMNS), NOWHERE, bf16)


def observations(position, plan, facts, own, other):
    columns = struct((PADDED_ROWS, WIDE), bf16)
    factors = struct((GROUP, PADDED_COLUMNS), bf16)
    square = pltpu.VMEM((NOBS, NOBS), bf16)
    return pl.pallas_call(
        observation_kernel,
        out_shape=(columns, columns, columns, factors, factors, factors),
        in_specs=[SMEM, VMEM, VMEM, VMEM, VMEM],
        out_specs=(VMEM,) * 6,
        scratch_shapes=[
            pltpu.VMEM((MEMBERS, NOBS), f32),
            pltpu.VMEM((MEMBERS, NOBS), f32),
            square,
            pltpu.VMEM((128, NOBS), f32),
            pltpu.VMEM((NOBS, 128), f32),
            pltpu.VMEM((NOBS, 2 * GROUP), bf16),
            square,
            square,
            square,
            square,
        ],
        compiler_params=kernel_params(44),
        cost_estimate=pl.CostEstimate(flops=20 * 10**9, bytes_accessed=8 * 2**20, transcendentals=10**5),
        name="observations",
    )(position, plan, facts, own, other)


def for_windows(starts_ref, size, align, visit):
    def first(g):
        return starts_ref[g] & -align

    for g in range(GROUPS):
        visit(g, pl.multiple_of(first(g), align), True)

    def rest(g, carry):
        count = (starts_ref[g + 1] - first(g) + size - 1) // size

        def step(i, carry):
            visit(g, pl.multiple_of(first(g) + i * size, align), False)
            return carry

        return lax.fori_loop(1, count, step, carry)

    lax.fori_loop(0, GROUPS, rest, 0)


def number(value, shape):
    if isinstance(value, int):
        return jnp.full(shape, value, bf16)
    return jnp.full(shape, value.astype(f32)).astype(bf16)


def covariance_kernel(
    position_ref, starts_ref, block_ref, anomalies_high_ref, anomalies_low_ref, tiles_ref, *refs
):
    out_refs, (total_ref,) = refs[:SUMS], refs[SUMS:]
    total_ref[...] = jnp.zeros_like(total_ref)
    zero = jnp.zeros((WINDOW_ROWS, WIDE), bf16)

    def visit(g, start, is_first):
        rows = pl.ds(start, WINDOW_ROWS)
        found = tiles_ref[rows, :] == number(g * FOUR, (WINDOW_ROWS, WIDE))
        left = jnp.concatenate(
            [jnp.where(found, anomalies_high_ref[rows, :], zero), jnp.where(found, anomalies_low_ref[rows, :], zero)],
            axis=0,
        )
        right = jnp.concatenate(
            [block_ref[pl.ds(g * FOUR + u, GROUP, stride=OWN_TILES), :] for u in range(FOUR)], axis=0
        )
        both = dot(left, jnp.concatenate(two_parts(right), axis=1))
        both = both[:WINDOW_ROWS] + both[WINDOW_ROWS:]
        total_ref[rows, :] += both[:, :LANES] + both[:, LANES:]

    for_windows(starts_ref, WINDOW_ROWS, 16, visit)
    for d in range(SUMS):
        start = ((position_ref[1] + d) & (SUMS - 1)) * CHUNK
        out_refs[d][...] = total_ref[pl.ds(pl.multiple_of(start, CHUNK), CHUNK), :]


def covariances(position, starts, block, anomalies_high, anomalies_low, tiles):
    return pl.pallas_call(
        covariance_kernel,
        out_shape=(struct((CHUNK, LANES)),) * SUMS,
        in_specs=[SMEM, SMEM] + [VMEM] * 4,
        out_specs=(VMEM,) * SUMS,
        scratch_shapes=[pltpu.VMEM((PADDED_ROWS, LANES), f32)],
        compiler_params=kernel_params(24),
        cost_estimate=pl.CostEstimate(flops=3 * 10**9, bytes_accessed=4 * 2**20, transcendentals=0),
        name="covariances",
    )(position, starts, block.reshape(GROUP * OWN_TILES, LANES), anomalies_high, anomalies_low, tiles)


def update_kernel(position_ref, starts_ref, *refs):
    sums_refs = refs[:SUMS]
    block_ref, factors_high_ref, factors_low_ref, tile_rows_ref, out_ref, right_ref = refs[SUMS:]
    for d in range(SUMS):
        start = ((position_ref[1] - d) & (SUMS - 1)) * CHUNK
        right_ref[pl.ds(pl.multiple_of(start, CHUNK), CHUNK), :] = jnp.concatenate(two_parts(sums_refs[d][...]), axis=1)
    right_ref[NOBS:, :] = jnp.zeros((WINDOW_COLUMNS, 2 * LANES), bf16)
    zero = jnp.zeros((GROUP, WINDOW_COLUMNS), bf16)

    def visit(g, start, is_first):
        columns = pl.ds(start, WINDOW_COLUMNS)
        tiles = tile_rows_ref[:, columns]
        high = factors_high_ref[:, columns]
        low = factors_low_ref[:, columns]
        found = [tiles == number(g * FOUR + u, (GROUP, WINDOW_COLUMNS)) for u in range(FOUR)]
        left = [jnp.where(f, high, zero) for f in found] + [jnp.where(f, low, zero) for f in found]
        both = dot(jnp.concatenate(left, axis=0), right_ref[columns, :])
        both = both[:WIDE] + both[WIDE:]
        change = both[:, :LANES] + both[:, LANES:]
        for u in range(FOUR):
            rows = pl.ds(g * FOUR + u, GROUP, stride=OWN_TILES)
            before = block_ref if is_first else out_ref
            out_ref[rows, :] = before[rows, :] + change[u * GROUP : (u + 1) * GROUP]

    for_windows(starts_ref, WINDOW_COLUMNS, LANES, visit)


def updated(position, starts, sums, block, factors_high, factors_low, tile_rows):
    out = pl.pallas_call(
        update_kernel,
        out_shape=struct((GROUP * OWN_TILES, LANES)),
        in_specs=[SMEM, SMEM] + [VMEM] * (SUMS + 4),
        out_specs=VMEM,
        scratch_shapes=[pltpu.VMEM((PADDED_COLUMNS, 2 * LANES), bf16)],
        compiler_params=kernel_params(32),
        cost_estimate=pl.CostEstimate(flops=4 * 10**9, bytes_accessed=8 * 2**20, transcendentals=0),
        name="updated",
    )(position, starts, *sums, block.reshape(GROUP * OWN_TILES, LANES), factors_high, factors_low, tile_rows)
    return out.reshape(GROUP, OWN_TILES, LANES)


def exchange(value, axes=PEERS):
    return lax.all_to_all(value, axes, 0, 0, tiled=True)


def passed_along(value, by):
    return lax.ppermute(value, "h", [(i, (i + by) % SUMS) for i in range(SUMS)])


def shards(state, locations, tile_mask, plan, obs_value, obs_error):
    residue = lax.axis_index(PEERS) // SLICES
    position = jnp.stack([residue, lax.axis_index("h"), lax.axis_index("c")]).astype(i32)
    rows = state.reshape(ROWS, LANES)

    tiles_here = tile_mask.shape[0]
    tiles = locations // TILE
    nth = jnp.arange(16, dtype=i32)[:, None]
    local = (tiles[None, :] - RADIUS + nth - lax.axis_index(ALL) * tiles_here) & (NTILES - 1)
    masks = jnp.zeros((16, NOBS), i32)
    for i in range(tiles_here):
        masks = masks + jnp.where((local == i) & (nth < WINDOW), tile_mask[i][None, :], 0)
    masks = exchange(masks.astype(f32).reshape(GROUP_CHIPS, 4, LANES), CHIPS).sum(axis=0)

    columns = own_columns(plan, locations, rows)
    mine = jnp.concatenate([columns, masks], axis=0)
    all_four = [mine] + [passed_along(mine, by) for by in range(1, SUMS)]
    payload = jnp.concatenate(
        [*(each[0:8] for each in all_four), sum(each[8:12] for each in all_four), jnp.zeros((4, LANES), f32)], axis=0
    )
    gathered = exchange(jnp.broadcast_to(payload[None], (GROUP_CHIPS, 40, LANES)), CHIPS)
    other = lax.ppermute(gathered, "c", [(0, 1), (1, 0)])
    block, other = lax.optimization_barrier((spread_out(rows), other))
    block = exchange(block)

    facts = jnp.concatenate(
        [tiles.astype(f32)[None], obs_value[None], obs_error[None], jnp.zeros((5, NOBS), f32)], axis=0
    )
    anomalies_high, anomalies_low, sorted_tiles, factors_high, factors_low, tile_rows = observations(
        position, plan[None], facts, gathered.reshape(-1, LANES), other.reshape(-1, LANES)
    )
    nth_own = (residue - tiles + RADIUS) & (RESIDUES - 1)
    own_tile = jnp.where(nth_own < WINDOW, ((tiles - RADIUS + nth_own) & (NTILES - 1)) // RESIDUES, OWN_TILES)
    starts = jnp.sum(own_tile[None, :] < FOUR * jnp.arange(GROUPS + 1, dtype=i32)[:, None], axis=1, dtype=i32)

    parts = covariances(position, starts, block, anomalies_high, anomalies_low, sorted_tiles)
    total = parts[0]
    for by in range(1, SUMS):
        total = total + passed_along(parts[by], by)
    sums = [total] + [passed_along(total, by) for by in range(1, SUMS)]
    block = exchange(updated(position, starts, sums, block, factors_high, factors_low, tile_rows))
    return collect(block).reshape(state.shape)


def solution(mesh):
    fine = Mesh(mesh.devices.reshape(4, 4, 2, 2, 4), ALL)
    placed = (P(ALL, None), P(), P(ALL, None), P(), P(), P())
    return jax.shard_map(shards, mesh=fine, in_specs=placed, out_specs=P(ALL, None), check_vma=False)
```

```python
import functools

import jax
import jax.numpy as jnp
from jax import lax
from jax.experimental import pallas as pl
from jax.experimental.pallas import tpu as pltpu
from jax.sharding import Mesh, PartitionSpec as P

MEMBERS = 256
TILE = 512
NTILES = 2048
RADIUS = 4
WINDOW = 2 * RADIUS + 1
BATCH_OBS = 256
BATCHES = 4
NOBS = BATCH_OBS * BATCHES

ALL = ("y", "h", "l", "c", "x")
PEERS = ("c", "y", "l", "x")
CHIPS = ("y", "l", "x")
GROUP = 64
CORES = 2
GROUP_CHIPS = GROUP // CORES
SUMS = 4
RESIDUES = 16
SLICES = 4
LANES = 128
OWN_TILES = NTILES // RESIDUES
ROWS = NTILES * TILE // LANES
EIGHT = 8
WIDE = EIGHT * GROUP
GROUPS = OWN_TILES // EIGHT
WINDOW_ROWS = 128
WINDOW_COLUMNS = 256
PADDED_ROWS = NOBS + WINDOW_ROWS
PADDED_COLUMNS = NOBS + WINDOW_COLUMNS
NOWHERE = -512
BLOCK_TILES = 16
FIRST = 640
FIRST_CHUNK = FIRST // SUMS
REST_CHUNK = (NOBS - FIRST) // SUMS

epsilon = 1e-06
f32 = jnp.float32
bf16 = jnp.bfloat16
i32 = jnp.int32

VMEM = pl.BlockSpec(memory_space=pltpu.VMEM)
SMEM = pl.BlockSpec(memory_space=pltpu.SMEM)


def kernel_params(mib):
    return pltpu.CompilerParams(vmem_limit_bytes=mib * 1024 * 1024)


def struct(shape, dtype=f32):
    return jax.ShapeDtypeStruct(shape, dtype)


def two_parts(value):
    high = value.astype(bf16)
    return high, (value - high.astype(f32)).astype(bf16)


def three_parts(value):
    high = value.astype(bf16)
    rest = value - high.astype(f32)
    middle = rest.astype(bf16)
    return high, middle, (rest - middle.astype(f32)).astype(bf16)


def dot(a, b):
    return lax.dot_general(a, b, (((1,), (0,)), ((), ())), preferred_element_type=f32)


def dot_parts(a_high, a_low, b_high, b_low):
    return dot(a_high, b_high) + dot(a_high, b_low) + dot(a_low, b_high)


def accurate_dot(a, b):
    return dot_parts(*two_parts(a), *two_parts(b))


def columns_kernel(plan_ref, locations_ref, state_ref, out_ref, picked_ref):
    lane = lax.broadcasted_iota(i32, (1, LANES), 1)

    def step(i, carry):
        base = pl.multiple_of(i * 8, 8)
        found = []
        for u in range(8):
            where = locations_ref[plan_ref[base + u]]
            row = state_ref[pl.ds(where >> 7, 1), :]
            found.append(jnp.where(lane == (where & (LANES - 1)), row, 0.0))
        picked_ref[pl.ds(base, 8), :] = jnp.concatenate(found, axis=0)
        return carry

    lax.fori_loop(0, NOBS // 8, step, 0, unroll=2)
    ones = jnp.ones((16, LANES), bf16)
    total = jnp.zeros((16, NOBS), f32)
    for part in three_parts(picked_ref[...]):
        total = total + lax.dot_general(ones, part, (((1,), (1,)), ((), ())), preferred_element_type=f32)
    for g in range(NOBS // LANES):
        out_ref[pl.ds(g, 1), :] = total[0:1, g * LANES : (g + 1) * LANES]


def own_columns(plan, locations, rows):
    return pl.pallas_call(
        columns_kernel,
        out_shape=struct((NOBS // LANES, LANES)),
        in_specs=[SMEM, SMEM, VMEM],
        out_specs=VMEM,
        scratch_shapes=[pltpu.VMEM((NOBS, LANES), f32)],
        compiler_params=kernel_params(24),
        cost_estimate=pl.CostEstimate(flops=10**6, bytes_accessed=8 * 2**20, transcendentals=0),
        name="own_columns",
    )(plan, locations, rows)


def spread_kernel(state_ref, out_ref):
    for d in range(GROUP):
        out_ref[d] = state_ref[pl.ds(d, BLOCK_TILES, stride=GROUP), :]


def collect_kernel(in_ref, state_ref):
    for a in range(BLOCK_TILES):
        state_ref[a * GROUP : (a + 1) * GROUP, :] = in_ref[:, a, :]


def reordered(kernel, value, out_shape, name):
    by_device = pl.BlockSpec((GROUP, BLOCK_TILES, LANES), lambda i: (0, i, 0))
    by_row = pl.BlockSpec((GROUP * BLOCK_TILES, LANES), lambda i: (i, 0))
    specs = (by_row, by_device) if value.ndim == 2 else (by_device, by_row)
    return pl.pallas_call(
        kernel,
        grid=(OWN_TILES // BLOCK_TILES,),
        out_shape=struct(out_shape),
        in_specs=[specs[0]],
        out_specs=specs[1],
        compiler_params=kernel_params(16),
        cost_estimate=pl.CostEstimate(flops=10**6, bytes_accessed=8 * 2**20, transcendentals=0),
        name=name,
    )(value)


def spread_out(rows):
    return reordered(spread_kernel, rows, (GROUP, OWN_TILES, LANES), "spread_out")


def collect(blocks):
    return reordered(collect_kernel, blocks, (ROWS, LANES), "collect")


def observation_kernel(
    position_ref, plan_ref, facts_ref, own_ref, other_ref,
    anomalies_high_ref, anomalies_low_ref, tiles_ref, factors_high_ref, factors_low_ref, tile_rows_ref,
    ensemble_ref, increments_ref, one_hot_ref, facts_scratch, in_columns_ref,
    turned_ref, links_high_ref, links_low_ref, sort_ref, sort_back_ref,
):
    core = position_ref[2]
    for d in range(SUMS):
        for gathered_ref, start in ((own_ref, core), (other_ref, 1 - core)):
            rows = pl.ds(pl.multiple_of(d * GROUP + start * GROUP_CHIPS, GROUP_CHIPS), GROUP_CHIPS)
            for g in range(NOBS // LANES):
                ensemble_ref[rows, g * LANES : (g + 1) * LANES] = gathered_ref[
                    pl.ds(d * 8 + g, GROUP_CHIPS, stride=40), :
                ]
    for g in range(NOBS // LANES):
        rows = pl.ds((g // 4) * 40 + 32 + g % 4, 16, stride=80)
        facts_scratch[0:16, g * LANES : (g + 1) * LANES] = own_ref[rows, :] + other_ref[rows, :]
    facts_scratch[16:24, :] = facts_ref[...]
    facts_scratch[24:128, :] = jnp.zeros((104, NOBS), f32)
    source = lax.broadcasted_iota(i32, (NOBS, NOBS), 0)
    one_hot_ref[...] = jnp.where(source == plan_ref[...], 1.0, 0.0).astype(bf16)
    high, middle, low = three_parts(facts_scratch[0:32, :])
    ordered = dot(high, one_hot_ref[...]) + dot(middle, one_hot_ref[...]) + dot(low, one_hot_ref[...])
    facts_scratch[0:32, :] = ordered
    for g in range(NOBS // LANES):
        in_columns_ref[g * LANES : (g + 1) * LANES, :] = facts_scratch[:, g * LANES : (g + 1) * LANES].T

    residue = position_ref[0]
    tile_row = facts_scratch[16:17, :].astype(i32)
    tile_column = in_columns_ref[:, 16:17].astype(i32)
    nth_row = (residue - tile_row + RADIUS) & (RESIDUES - 1)
    nth_column = (residue - tile_column + RADIUS) & (RESIDUES - 1)
    own_row = ((tile_row - RADIUS + nth_row) & (NTILES - 1)) >> 4
    own_column = ((tile_column - RADIUS + nth_column) & (NTILES - 1)) >> 4
    own_row = jnp.where(nth_row < WINDOW, own_row, -1)
    own_column = jnp.where(nth_column < WINDOW, own_column, -2)
    mask_column = jnp.zeros((NOBS, 1), f32)
    for n in range(WINDOW):
        mask_column = mask_column + jnp.where(nth_column == n, in_columns_ref[:, n : n + 1], 0.0)

    mask_row = jnp.zeros((1, NOBS), f32)
    for n in range(WINDOW):
        mask_row = mask_row + jnp.where(nth_row == n, facts_scratch[n : n + 1, :], 0.0)

    key_row = jnp.where(own_row < 0, OWN_TILES, own_row) * NOBS + lax.broadcasted_iota(i32, (1, NOBS), 1)
    key_column = jnp.where(own_column < 0, OWN_TILES, own_column) * NOBS + lax.broadcasted_iota(i32, (NOBS, 1), 0)
    rank_row = jnp.sum(jnp.where(key_column < key_row, 1.0, 0.0), axis=0, keepdims=True).astype(i32)
    rank_column = jnp.sum(jnp.where(key_row < key_column, 1.0, 0.0), axis=1, keepdims=True).astype(i32)
    sort_ref[...] = jnp.where(source == rank_row, 1.0, 0.0).astype(bf16)
    to = lax.broadcasted_iota(i32, (NOBS, NOBS), 1)
    sort_back_ref[...] = jnp.where(to == rank_column, 1.0, 0.0).astype(bf16)

    gain_rows = []
    for b in range(BATCHES):
        here = slice(b * BATCH_OBS, (b + 1) * BATCH_OBS)
        prior = ensemble_ref[:, here]
        average = jnp.sum(prior, axis=0, keepdims=True) / MEMBERS
        anomaly = prior - average
        spread = jnp.sum(anomaly * anomaly, axis=0, keepdims=True) / (MEMBERS - 1) + epsilon
        value = facts_scratch[17:18, here]
        error = facts_scratch[18:19, here]
        shrink = jnp.sqrt(error / (spread + error))
        moved = (average * error + value * spread) / (spread + error)
        increments = (shrink - 1.0) * anomaly + (moved - average)
        increments_ref[:, here] = increments
        turned = anomaly.T
        spread_column = jnp.sum(turned * turned, axis=1, keepdims=True) / (MEMBERS - 1) + epsilon
        gain_column = 1.0 / ((MEMBERS - 1) * spread_column)
        turned_high, turned_low = two_parts(turned)
        turned_ref[here, :] = jnp.concatenate([turned_high[:, 0:GROUP], turned_low[:, 0:GROUP]], axis=1)
        gain_rows.append(1.0 / ((MEMBERS - 1) * spread))
        weight = mask_column[here] * gain_column
        if b > 0:
            before = b * BATCH_OBS
            links = accurate_dot(turned, increments_ref[:, 0:before])
            links = jnp.where(own_column[here] == own_row[:, 0:before], links * weight, 0.0)
            links_high, links_low = two_parts(links)
            links_high_ref[here, 0:before] = links_high
            links_low_ref[here, 0:before] = links_low
        if b < BATCHES - 1:
            after = slice((b + 1) * BATCH_OBS, NOBS)
            later = ensemble_ref[:, after]
            covariance = dot_parts(turned_high, turned_low, *two_parts(later))
            apart = (tile_row[:, after] - tile_column[here] + RADIUS) & (NTILES - 1)
            masks = jnp.zeros(apart.shape, f32)
            for n in range(WINDOW):
                masks = jnp.where(apart == n, in_columns_ref[here, n : n + 1], masks)
            ensemble_ref[:, after] = later + accurate_dot(increments, covariance * masks * gain_column)

    for b in reversed(range(BATCHES - 1)):
        here = slice(b * BATCH_OBS, (b + 1) * BATCH_OBS)
        after = slice((b + 1) * BATCH_OBS, NOBS)
        increments_ref[0:GROUP, here] += dot_parts(
            *two_parts(increments_ref[0:GROUP, after]), links_high_ref[after, here], links_low_ref[after, here]
        )
    factors = increments_ref[0:GROUP, :] * (mask_row * jnp.concatenate(gain_rows, axis=1))

    tile_here = jnp.where(own_column < 0, NOWHERE, own_column).astype(f32)
    tile_here = jnp.broadcast_to(tile_here, (NOBS, LANES)).astype(bf16)
    sorted_columns = dot(sort_ref[...], jnp.concatenate([turned_ref[...], tile_here], axis=1))
    high = sorted_columns[:, 0:GROUP].astype(bf16)
    low = sorted_columns[:, GROUP : 2 * GROUP].astype(bf16)
    replicate = jnp.where(
        lax.broadcasted_iota(i32, (GROUP, WIDE), 1) >> 3 == lax.broadcasted_iota(i32, (GROUP, WIDE), 0), 1.0, 0.0
    ).astype(bf16)
    anomalies_high_ref[0:NOBS, :] = dot(high, replicate).astype(bf16)
    anomalies_low_ref[0:NOBS, :] = dot(low, replicate).astype(bf16)
    nth_of_eight = (lax.broadcasted_iota(i32, (NOBS, WIDE), 1) & (EIGHT - 1)).astype(f32)
    tiles_ref[0:NOBS, :] = (sorted_columns[:, LANES : LANES + 1] - nth_of_eight).astype(bf16)
    padding = slice(NOBS, PADDED_ROWS)
    anomalies_high_ref[padding, :] = jnp.zeros((WINDOW_ROWS, WIDE), bf16)
    anomalies_low_ref[padding, :] = jnp.zeros((WINDOW_ROWS, WIDE), bf16)
    tiles_ref[padding, :] = jnp.full((WINDOW_ROWS, WIDE), NOWHERE, bf16)

    factors_high, factors_low = two_parts(factors)
    tile_there = jnp.where(own_row < 0, NOWHERE, own_row).astype(f32)
    tile_there = jnp.broadcast_to(tile_there, (GROUP, NOBS)).astype(bf16)
    sorted_rows = dot(jnp.concatenate([factors_high, factors_low, tile_there], axis=0), sort_back_ref[...])
    replicate = jnp.where(
        lax.broadcasted_iota(i32, (WIDE, GROUP), 0) >> 3 == lax.broadcasted_iota(i32, (WIDE, GROUP), 1), 1.0, 0.0
    ).astype(bf16)
    factors_high_ref[:, 0:NOBS] = dot(replicate, sorted_rows[0:GROUP].astype(bf16)).astype(bf16)
    factors_low_ref[:, 0:NOBS] = dot(replicate, sorted_rows[GROUP : 2 * GROUP].astype(bf16)).astype(bf16)
    nth_of_eight = (lax.broadcasted_iota(i32, (16, NOBS), 0) & (EIGHT - 1)).astype(f32)
    tile_rows_ref[:, 0:NOBS] = (sorted_rows[2 * GROUP : 2 * GROUP + 16] - nth_of_eight).astype(bf16)
    padding = slice(NOBS, PADDED_COLUMNS)
    factors_high_ref[:, padding] = jnp.zeros((WIDE, WINDOW_COLUMNS), bf16)
    factors_low_ref[:, padding] = jnp.zeros((WIDE, WINDOW_COLUMNS), bf16)
    tile_rows_ref[:, padding] = jnp.full((16, WINDOW_COLUMNS), NOWHERE, bf16)


def observations(position, plan, facts, own, other):
    columns = struct((PADDED_ROWS, WIDE), bf16)
    factors = struct((WIDE, PADDED_COLUMNS), bf16)
    square = pltpu.VMEM((NOBS, NOBS), bf16)
    return pl.pallas_call(
        observation_kernel,
        out_shape=(columns, columns, columns, factors, factors, struct((16, PADDED_COLUMNS), bf16)),
        in_specs=[SMEM, VMEM, VMEM, VMEM, VMEM],
        out_specs=(VMEM,) * 6,
        scratch_shapes=[
            pltpu.VMEM((MEMBERS, NOBS), f32),
            pltpu.VMEM((MEMBERS, NOBS), f32),
            square,
            pltpu.VMEM((128, NOBS), f32),
            pltpu.VMEM((NOBS, 128), f32),
            pltpu.VMEM((NOBS, 2 * GROUP), bf16),
            square,
            square,
            square,
            square,
        ],
        compiler_params=kernel_params(44),
        cost_estimate=pl.CostEstimate(flops=20 * 10**9, bytes_accessed=8 * 2**20, transcendentals=10**5),
        name="observations",
    )(position, plan, facts, own, other)


def for_windows(starts_ref, groups, size, align, visit):
    def start(g, i):
        return pl.multiple_of((starts_ref[g] & -align) + i * size, align)

    first_group = pl.program_id(0) * groups
    for n in range(groups):
        visit(n, first_group + n, start(first_group + n, 0), True)
    for n in range(groups):
        g = first_group + n
        count = (starts_ref[g + 1] - (starts_ref[g] & -align) + size - 1) // size

        def step(i, carry, n=n, g=g):
            visit(n, g, start(g, i), False)
            return carry

        lax.fori_loop(1, count, step, 0)


def first_tile(g, shape):
    return jnp.full(shape, (g * EIGHT).astype(f32)).astype(bf16)


COVARIANCE_GROUPS = 4


def covariance_kernel(position_ref, starts_ref, block_ref, anomalies_high_ref, anomalies_low_ref, tiles_ref, *refs):
    out_refs, (total_ref,) = refs[: 2 * SUMS], refs[2 * SUMS :]

    @pl.when(pl.program_id(0) == 0)
    def _():
        total_ref[...] = jnp.zeros_like(total_ref)

    zero = jnp.zeros((WINDOW_ROWS, WIDE), bf16)

    def visit(n, g, start, is_first):
        rows = pl.ds(start, WINDOW_ROWS)
        found = tiles_ref[rows, :] == first_tile(g, (WINDOW_ROWS, WIDE))
        left = jnp.concatenate(
            [jnp.where(found, anomalies_high_ref[rows, :], zero), jnp.where(found, anomalies_low_ref[rows, :], zero)],
            axis=0,
        )
        right = block_ref[:, n * EIGHT : (n + 1) * EIGHT, :].reshape(WIDE, LANES)
        both = dot(left, jnp.concatenate(two_parts(right), axis=1))
        both = both[:WINDOW_ROWS] + both[WINDOW_ROWS:]
        total_ref[rows, :] += both[:, :LANES] + both[:, LANES:]

    for_windows(starts_ref, COVARIANCE_GROUPS, WINDOW_ROWS, 16, visit)

    @pl.when(pl.program_id(0) == pl.num_programs(0) - 1)
    def _():
        for d in range(SUMS):
            to = (position_ref[1] + d) & (SUMS - 1)
            start = pl.multiple_of(to * FIRST_CHUNK, 16)
            out_refs[d][...] = total_ref[pl.ds(start, FIRST_CHUNK), :]
            start = pl.multiple_of(FIRST + to * REST_CHUNK, 16)
            out_refs[SUMS + d][...] = total_ref[pl.ds(start, REST_CHUNK), :]


def covariances(position, starts, block, anomalies_high, anomalies_low, tiles):
    steps = GROUPS // COVARIANCE_GROUPS
    return pl.pallas_call(
        covariance_kernel,
        grid=(steps,),
        out_shape=(struct((FIRST_CHUNK, LANES)),) * SUMS + (struct((REST_CHUNK, LANES)),) * SUMS,
        in_specs=[SMEM, SMEM, pl.BlockSpec((GROUP, OWN_TILES // steps, LANES), lambda i: (0, i, 0))] + [VMEM] * 3,
        out_specs=(VMEM,) * (2 * SUMS),
        scratch_shapes=[pltpu.VMEM((PADDED_ROWS, LANES), f32)],
        compiler_params=kernel_params(24),
        cost_estimate=pl.CostEstimate(flops=3 * 10**9, bytes_accessed=4 * 2**20, transcendentals=0),
        name="covariances",
    )(position, starts, block, anomalies_high, anomalies_low, tiles)


UPDATE_GROUPS = 2


def update_kernel(position_ref, starts_ref, *refs):
    sums_refs = refs[: 2 * SUMS]
    block_ref, factors_high_ref, factors_low_ref, tile_rows_ref, out_ref, right_ref = refs[2 * SUMS :]

    @pl.when(pl.program_id(0) == 0)
    def _():
        for d in range(SUMS):
            of = (position_ref[1] - d) & (SUMS - 1)
            start = pl.multiple_of(of * FIRST_CHUNK, 16)
            right_ref[pl.ds(start, FIRST_CHUNK), :] = jnp.concatenate(two_parts(sums_refs[d][...]), axis=1)
            start = pl.multiple_of(FIRST + of * REST_CHUNK, 16)
            right_ref[pl.ds(start, REST_CHUNK), :] = jnp.concatenate(two_parts(sums_refs[SUMS + d][...]), axis=1)
        right_ref[NOBS:, :] = jnp.zeros((WINDOW_COLUMNS, 2 * LANES), bf16)

    def visit(n, g, start, is_first):
        columns = pl.ds(start, WINDOW_COLUMNS)
        found = tile_rows_ref[:, columns] == first_tile(g, (16, WINDOW_COLUMNS))
        found = jnp.where(found, jnp.ones((16, WINDOW_COLUMNS), bf16), jnp.zeros((16, WINDOW_COLUMNS), bf16))
        left = [
            (ref[:, columns].reshape(WIDE // 16, 16, WINDOW_COLUMNS) * found[None]).reshape(WIDE, WINDOW_COLUMNS)
            for ref in (factors_high_ref, factors_low_ref)
        ]
        both = dot(jnp.concatenate(left, axis=0), right_ref[columns, :])
        both = both[:WIDE] + both[WIDE:]
        change = (both[:, :LANES] + both[:, LANES:]).reshape(GROUP, EIGHT, LANES)
        here = slice(n * EIGHT, (n + 1) * EIGHT)
        out_ref[:, here, :] = (block_ref if is_first else out_ref)[:, here, :] + change

    for_windows(starts_ref, UPDATE_GROUPS, WINDOW_COLUMNS, LANES, visit)


def updated(position, starts, sums, block, factors_high, factors_low, tile_rows):
    steps = GROUPS // UPDATE_GROUPS
    by_tiles = pl.BlockSpec((GROUP, OWN_TILES // steps, LANES), lambda i: (0, i, 0))
    return pl.pallas_call(
        update_kernel,
        grid=(steps,),
        out_shape=struct((GROUP, OWN_TILES, LANES)),
        in_specs=[SMEM, SMEM] + [VMEM] * (2 * SUMS) + [by_tiles] + [VMEM] * 3,
        out_specs=by_tiles,
        scratch_shapes=[pltpu.VMEM((PADDED_COLUMNS, 2 * LANES), bf16)],
        compiler_params=kernel_params(24),
        cost_estimate=pl.CostEstimate(flops=4 * 10**9, bytes_accessed=8 * 2**20, transcendentals=0),
        name="updated",
    )(position, starts, *sums, block, factors_high, factors_low, tile_rows)


def exchange(value, axes=PEERS):
    return lax.all_to_all(value, axes, 0, 0, tiled=True)


def passed_along(value, by):
    return lax.ppermute(value, "h", [(i, (i + by) % SUMS) for i in range(SUMS)])


def summed(parts):
    total = parts[0]
    for by in range(1, SUMS):
        total = total + passed_along(parts[by], by)
    return (total, *(passed_along(total, by) for by in range(1, SUMS)))


def shards(state, locations, tile_mask, plan, obs_value, obs_error):
    residue = lax.axis_index(PEERS) // SLICES
    position = jnp.stack([residue, lax.axis_index("h"), lax.axis_index("c")]).astype(i32)
    rows = state.reshape(ROWS, LANES)

    tiles_here = tile_mask.shape[0]
    tiles = locations // TILE
    nth = jnp.arange(16, dtype=i32)[:, None]
    local = (tiles[None, :] - RADIUS + nth - lax.axis_index(ALL) * tiles_here) & (NTILES - 1)
    masks = jnp.zeros((16, NOBS), i32)
    for i in range(tiles_here):
        masks = masks + jnp.where((local == i) & (nth < WINDOW), tile_mask[i][None, :], 0)
    masks = exchange(masks.astype(f32).reshape(GROUP_CHIPS, 4, LANES), CHIPS).sum(axis=0)

    columns = own_columns(plan, locations, rows)
    mine = jnp.concatenate([columns, masks], axis=0)
    all_four = [mine] + [passed_along(mine, by) for by in range(1, SUMS)]
    payload = jnp.concatenate(
        [*(each[0:8] for each in all_four), sum(each[8:12] for each in all_four), jnp.zeros((4, LANES), f32)], axis=0
    )
    block, payload = lax.optimization_barrier((spread_out(rows), payload))
    gathered = exchange(jnp.broadcast_to(payload[None], (GROUP_CHIPS, 40, LANES)), CHIPS)
    other = lax.ppermute(gathered, "c", [(0, 1), (1, 0)])
    block, other = lax.optimization_barrier((block, other))
    block = exchange(block)

    facts = jnp.concatenate(
        [tiles.astype(f32)[None], obs_value[None], obs_error[None], jnp.zeros((5, NOBS), f32)], axis=0
    )
    anomalies_high, anomalies_low, sorted_tiles, factors_high, factors_low, tile_rows = observations(
        position, plan[None], facts, gathered.reshape(-1, LANES), other.reshape(-1, LANES)
    )
    nth_own = (residue - tiles + RADIUS) & (RESIDUES - 1)
    own_tile = jnp.where(nth_own < WINDOW, ((tiles - RADIUS + nth_own) & (NTILES - 1)) // RESIDUES, OWN_TILES)
    starts = jnp.sum(own_tile[None, :] < EIGHT * jnp.arange(GROUPS + 1, dtype=i32)[:, None], axis=1, dtype=i32)
    nth_all = (jnp.arange(RESIDUES, dtype=i32)[:, None] - tiles[None, :] + RADIUS) & (RESIDUES - 1)
    most = jnp.max(jnp.sum(nth_all < WINDOW, axis=1, dtype=i32))

    parts = covariances(position, starts, block, anomalies_high, anomalies_low, sorted_tiles)
    rest = lax.cond(most > FIRST, summed, lambda parts: parts, parts[SUMS:])
    sums = summed(parts[:SUMS]) + tuple(rest)
    block = exchange(updated(position, starts, sums, block, factors_high, factors_low, tile_rows))
    return collect(block).reshape(state.shape)


def solution(mesh):
    fine = Mesh(mesh.devices.reshape(4, 4, 2, 2, 4), ALL)
    placed = (P(ALL, None), P(), P(ALL, None), P(), P(), P())
    return jax.shard_map(shards, mesh=fine, in_specs=placed, out_specs=P(ALL, None), check_vma=False)
```

```python
import functools

import jax
import jax.numpy as jnp
from jax import lax
from jax.experimental import pallas as pl
from jax.experimental.pallas import tpu as pltpu
from jax.sharding import Mesh, PartitionSpec as P

MEMBERS = 256
TILE = 512
NTILES = 2048
RADIUS = 4
WINDOW = 2 * RADIUS + 1
BATCH_OBS = 256
BATCHES = 4
NOBS = BATCH_OBS * BATCHES

ALL = ("y", "h", "l", "c", "x")
PEERS = ("c", "y", "l", "x")
CHIPS = ("y", "l", "x")
GROUP = 64
CORES = 2
GROUP_CHIPS = GROUP // CORES
SUMS = 4
RESIDUES = 16
SLICES = 4
LANES = 128
OWN_TILES = NTILES // RESIDUES
ROWS = NTILES * TILE // LANES
EIGHT = 8
WIDE = EIGHT * GROUP
GROUPS = OWN_TILES // EIGHT
WINDOW_ROWS = 128
WINDOW_COLUMNS = 256
PADDED_ROWS = NOBS + WINDOW_ROWS
PADDED_COLUMNS = NOBS + WINDOW_COLUMNS
LOW = slice(WIDE, 2 * WIDE)
TILES = slice(2 * WIDE, 2 * WIDE + LANES)
TILE_ROWS = slice(2 * WIDE, 2 * WIDE + 16)
NOWHERE = -512
BLOCK_TILES = 16
FIRST = 640
FIRST_CHUNK = FIRST // SUMS
REST_CHUNK = (NOBS - FIRST) // SUMS

epsilon = 1e-06
f32 = jnp.float32
bf16 = jnp.bfloat16
i32 = jnp.int32

VMEM = pl.BlockSpec(memory_space=pltpu.VMEM)
SMEM = pl.BlockSpec(memory_space=pltpu.SMEM)


def kernel_params(mib):
    return pltpu.CompilerParams(vmem_limit_bytes=mib * 1024 * 1024)


def struct(shape, dtype=f32):
    return jax.ShapeDtypeStruct(shape, dtype)


def two_parts(value):
    high = value.astype(bf16)
    return high, (value - high.astype(f32)).astype(bf16)


def three_parts(value):
    high = value.astype(bf16)
    rest = value - high.astype(f32)
    middle = rest.astype(bf16)
    return high, middle, (rest - middle.astype(f32)).astype(bf16)


def dot(a, b):
    return lax.dot_general(a, b, (((1,), (0,)), ((), ())), preferred_element_type=f32)


def dot_parts(a_high, a_low, b_high, b_low):
    return dot(a_high, b_high) + dot(a_high, b_low) + dot(a_low, b_high)


def accurate_dot(a, b):
    return dot_parts(*two_parts(a), *two_parts(b))


def masks_kernel(position_ref, locations_ref, tile_mask_ref, out_ref):
    tiles_here = tile_mask_ref.shape[0]
    first = position_ref[3] * tiles_here
    per_row = NOBS // LANES
    relative = (locations_ref[...] >> 9) - RADIUS - first
    masks = [
        jnp.concatenate([tile_mask_ref[i : i + 1, g * LANES : (g + 1) * LANES] for g in range(per_row)], axis=0)
        for i in range(tiles_here)
    ]
    for n in range(16):
        local = (relative + n) & (NTILES - 1)
        found = jnp.zeros((per_row, LANES), i32)
        if n < WINDOW:
            for i in range(tiles_here):
                found = jnp.where(local == i, masks[i], found)
        out_ref[n * per_row : (n + 1) * per_row, :] = found.astype(f32)


def own_masks(position, locations, tile_mask):
    return pl.pallas_call(
        masks_kernel,
        out_shape=struct((16 * NOBS // LANES, LANES)),
        in_specs=[SMEM, VMEM, VMEM],
        out_specs=VMEM,
        compiler_params=kernel_params(4),
        cost_estimate=pl.CostEstimate(flops=10**5, bytes_accessed=10**5, transcendentals=0),
        name="own_masks",
    )(position, locations, tile_mask)


def columns_kernel(plan_ref, locations_ref, state_ref, out_ref, picked_ref):
    lane = lax.broadcasted_iota(i32, (1, LANES), 1)

    def step(i, carry):
        base = pl.multiple_of(i * 8, 8)
        found = []
        for u in range(8):
            where = locations_ref[plan_ref[base + u]]
            row = state_ref[pl.ds(where >> 7, 1), :]
            found.append(jnp.where(lane == (where & (LANES - 1)), row, 0.0))
        picked_ref[pl.ds(base, 8), :] = jnp.concatenate(found, axis=0)
        return carry

    lax.fori_loop(0, NOBS // 8, step, 0, unroll=2)
    ones = jnp.ones((16, LANES), bf16)
    total = jnp.zeros((16, NOBS), f32)
    for part in three_parts(picked_ref[...]):
        total = total + lax.dot_general(ones, part, (((1,), (1,)), ((), ())), preferred_element_type=f32)
    for g in range(NOBS // LANES):
        out_ref[pl.ds(g, 1), :] = total[0:1, g * LANES : (g + 1) * LANES]


def own_columns(plan, locations, rows):
    return pl.pallas_call(
        columns_kernel,
        out_shape=struct((NOBS // LANES, LANES)),
        in_specs=[SMEM, SMEM, VMEM],
        out_specs=VMEM,
        scratch_shapes=[pltpu.VMEM((NOBS, LANES), f32)],
        compiler_params=kernel_params(24),
        cost_estimate=pl.CostEstimate(flops=10**6, bytes_accessed=8 * 2**20, transcendentals=0),
        name="own_columns",
    )(plan, locations, rows)


def spread_kernel(state_ref, out_ref):
    for d in range(GROUP):
        out_ref[d] = state_ref[pl.ds(d, BLOCK_TILES, stride=GROUP), :]


def collect_kernel(in_ref, state_ref):
    rows_ref = in_ref.reshape(GROUP * BLOCK_TILES, LANES)
    for a in range(BLOCK_TILES):
        state_ref[a * GROUP : (a + 1) * GROUP, :] = rows_ref[pl.ds(a, GROUP, stride=BLOCK_TILES), :]


def reordered(kernel, value, out_shape, name):
    by_device = pl.BlockSpec((GROUP, BLOCK_TILES, LANES), lambda i: (0, i, 0))
    by_row = pl.BlockSpec((GROUP * BLOCK_TILES, LANES), lambda i: (i, 0))
    specs = (by_row, by_device) if value.ndim == 2 else (by_device, by_row)
    return pl.pallas_call(
        kernel,
        grid=(OWN_TILES // BLOCK_TILES,),
        out_shape=struct(out_shape),
        in_specs=[specs[0]],
        out_specs=specs[1],
        compiler_params=kernel_params(16),
        cost_estimate=pl.CostEstimate(flops=10**6, bytes_accessed=8 * 2**20, transcendentals=0),
        name=name,
    )(value)


def spread_out(rows):
    return reordered(spread_kernel, rows, (GROUP, OWN_TILES, LANES), "spread_out")


def collect(blocks):
    return reordered(collect_kernel, blocks, (ROWS, LANES), "collect")


def observation_kernel(
    position_ref, plan_ref, facts_ref, own_ref, other_ref,
    columns_ref, factors_ref,
    ensemble_ref, increments_ref, one_hot_ref, facts_scratch, in_columns_ref,
    turned_ref, links_high_ref, links_low_ref, sort_ref, sort_back_ref,
):
    core = position_ref[2]
    for d in range(SUMS):
        for gathered_ref, start in ((own_ref, core), (other_ref, 1 - core)):
            rows = pl.ds(pl.multiple_of(d * GROUP + start * GROUP_CHIPS, GROUP_CHIPS), GROUP_CHIPS)
            for g in range(NOBS // LANES):
                ensemble_ref[rows, g * LANES : (g + 1) * LANES] = gathered_ref[
                    pl.ds(d * 8 + g, GROUP_CHIPS, stride=40), :
                ]
    for g in range(NOBS // LANES):
        rows = pl.ds((g // 4) * 40 + 32 + g % 4, 16, stride=80)
        facts_scratch[0:16, g * LANES : (g + 1) * LANES] = own_ref[rows, :] + other_ref[rows, :]
    facts_scratch[16:24, :] = facts_ref[...]
    facts_scratch[24:128, :] = jnp.zeros((104, NOBS), f32)
    source = lax.broadcasted_iota(i32, (NOBS, NOBS), 0)
    one_hot_ref[...] = jnp.where(source == plan_ref[...], 1.0, 0.0).astype(bf16)
    high, middle, low = three_parts(facts_scratch[0:32, :])
    ordered = dot(high, one_hot_ref[...]) + dot(middle, one_hot_ref[...]) + dot(low, one_hot_ref[...])
    facts_scratch[0:32, :] = ordered
    for g in range(NOBS // LANES):
        in_columns_ref[g * LANES : (g + 1) * LANES, :] = facts_scratch[:, g * LANES : (g + 1) * LANES].T

    residue = position_ref[0]
    tile_row = facts_scratch[16:17, :].astype(i32)
    tile_column = in_columns_ref[:, 16:17].astype(i32)
    nth_row = (residue - tile_row + RADIUS) & (RESIDUES - 1)
    nth_column = (residue - tile_column + RADIUS) & (RESIDUES - 1)
    own_row = ((tile_row - RADIUS + nth_row) & (NTILES - 1)) >> 4
    own_column = ((tile_column - RADIUS + nth_column) & (NTILES - 1)) >> 4
    own_row = jnp.where(nth_row < WINDOW, own_row, -1)
    own_column = jnp.where(nth_column < WINDOW, own_column, -2)
    mask_column = jnp.zeros((NOBS, 1), f32)
    for n in range(WINDOW):
        mask_column = mask_column + jnp.where(nth_column == n, in_columns_ref[:, n : n + 1], 0.0)

    mask_row = jnp.zeros((1, NOBS), f32)
    for n in range(WINDOW):
        mask_row = mask_row + jnp.where(nth_row == n, facts_scratch[n : n + 1, :], 0.0)

    key_row = jnp.where(own_row < 0, OWN_TILES, own_row) * NOBS + lax.broadcasted_iota(i32, (1, NOBS), 1)
    key_column = jnp.where(own_column < 0, OWN_TILES, own_column) * NOBS + lax.broadcasted_iota(i32, (NOBS, 1), 0)
    rank_row = jnp.sum(jnp.where(key_column < key_row, 1.0, 0.0), axis=0, keepdims=True).astype(i32)
    rank_column = jnp.sum(jnp.where(key_row < key_column, 1.0, 0.0), axis=1, keepdims=True).astype(i32)
    sort_ref[...] = jnp.where(source == rank_row, 1.0, 0.0).astype(bf16)
    to = lax.broadcasted_iota(i32, (NOBS, NOBS), 1)
    sort_back_ref[...] = jnp.where(to == rank_column, 1.0, 0.0).astype(bf16)

    gain_rows = []
    for b in range(BATCHES):
        here = slice(b * BATCH_OBS, (b + 1) * BATCH_OBS)
        prior = ensemble_ref[:, here]
        average = jnp.sum(prior, axis=0, keepdims=True) / MEMBERS
        anomaly = prior - average
        spread = jnp.sum(anomaly * anomaly, axis=0, keepdims=True) / (MEMBERS - 1) + epsilon
        value = facts_scratch[17:18, here]
        error = facts_scratch[18:19, here]
        shrink = jnp.sqrt(error / (spread + error))
        moved = (average * error + value * spread) / (spread + error)
        increments = (shrink - 1.0) * anomaly + (moved - average)
        increments_ref[:, here] = increments
        turned = anomaly.T
        spread_column = jnp.sum(turned * turned, axis=1, keepdims=True) / (MEMBERS - 1) + epsilon
        gain_column = 1.0 / ((MEMBERS - 1) * spread_column)
        turned_high, turned_low = two_parts(turned)
        turned_ref[here, :] = jnp.concatenate([turned_high[:, 0:GROUP], turned_low[:, 0:GROUP]], axis=1)
        gain_rows.append(1.0 / ((MEMBERS - 1) * spread))
        weight = mask_column[here] * gain_column
        if b > 0:
            before = b * BATCH_OBS
            links = accurate_dot(turned, increments_ref[:, 0:before])
            links = jnp.where(own_column[here] == own_row[:, 0:before], links * weight, 0.0)
            links_high, links_low = two_parts(links)
            links_high_ref[here, 0:before] = links_high
            links_low_ref[here, 0:before] = links_low
        if b < BATCHES - 1:
            after = slice((b + 1) * BATCH_OBS, NOBS)
            later = ensemble_ref[:, after]
            covariance = dot_parts(turned_high, turned_low, *two_parts(later))
            apart = (tile_row[:, after] - tile_column[here] + RADIUS) & (NTILES - 1)
            masks = jnp.zeros(apart.shape, f32)
            for n in range(WINDOW):
                masks = jnp.where(apart == n, in_columns_ref[here, n : n + 1], masks)
            ensemble_ref[:, after] = later + accurate_dot(increments, covariance * masks * gain_column)

    for b in reversed(range(BATCHES - 1)):
        here = slice(b * BATCH_OBS, (b + 1) * BATCH_OBS)
        after = slice((b + 1) * BATCH_OBS, NOBS)
        increments_ref[0:GROUP, here] += dot_parts(
            *two_parts(increments_ref[0:GROUP, after]), links_high_ref[after, here], links_low_ref[after, here]
        )
    factors = increments_ref[0:GROUP, :] * (mask_row * jnp.concatenate(gain_rows, axis=1))

    tile_here = jnp.where(own_column < 0, NOWHERE, own_column).astype(f32)
    tile_here = jnp.broadcast_to(tile_here, (NOBS, LANES)).astype(bf16)
    sorted_columns = dot(sort_ref[...], jnp.concatenate([turned_ref[...], tile_here], axis=1))
    high = sorted_columns[:, 0:GROUP].astype(bf16)
    low = sorted_columns[:, GROUP : 2 * GROUP].astype(bf16)
    replicate = jnp.where(
        lax.broadcasted_iota(i32, (GROUP, WIDE), 1) >> 3 == lax.broadcasted_iota(i32, (GROUP, WIDE), 0), 1.0, 0.0
    ).astype(bf16)
    columns_ref[0:NOBS, 0:WIDE] = dot(high, replicate).astype(bf16)
    columns_ref[0:NOBS, LOW] = dot(low, replicate).astype(bf16)
    nth_of_eight = (lax.broadcasted_iota(i32, (NOBS, LANES), 1) & (EIGHT - 1)).astype(f32)
    columns_ref[0:NOBS, TILES] = (sorted_columns[:, LANES : LANES + 1] - nth_of_eight).astype(bf16)
    columns_ref[NOBS:, 0 : 2 * WIDE] = jnp.zeros((WINDOW_ROWS, 2 * WIDE), bf16)
    columns_ref[NOBS:, TILES] = jnp.full((WINDOW_ROWS, LANES), NOWHERE, bf16)

    factors_high, factors_low = two_parts(factors)
    tile_there = jnp.where(own_row < 0, NOWHERE, own_row).astype(f32)
    tile_there = jnp.broadcast_to(tile_there, (GROUP, NOBS)).astype(bf16)
    sorted_rows = dot(jnp.concatenate([factors_high, factors_low, tile_there], axis=0), sort_back_ref[...])
    replicate = jnp.where(
        lax.broadcasted_iota(i32, (WIDE, GROUP), 0) >> 3 == lax.broadcasted_iota(i32, (WIDE, GROUP), 1), 1.0, 0.0
    ).astype(bf16)
    factors_ref[0:WIDE, 0:NOBS] = dot(replicate, sorted_rows[0:GROUP].astype(bf16)).astype(bf16)
    factors_ref[LOW, 0:NOBS] = dot(replicate, sorted_rows[GROUP : 2 * GROUP].astype(bf16)).astype(bf16)
    nth_of_eight = (lax.broadcasted_iota(i32, (16, NOBS), 0) & (EIGHT - 1)).astype(f32)
    factors_ref[TILE_ROWS, 0:NOBS] = (sorted_rows[2 * GROUP : 2 * GROUP + 16] - nth_of_eight).astype(bf16)
    factors_ref[0 : 2 * WIDE, NOBS:] = jnp.zeros((2 * WIDE, WINDOW_COLUMNS), bf16)
    factors_ref[TILE_ROWS, NOBS:] = jnp.full((16, WINDOW_COLUMNS), NOWHERE, bf16)


def observations(position, plan, facts, own, other):
    columns = struct((PADDED_ROWS, 2 * WIDE + LANES), bf16)
    factors = struct((2 * WIDE + 16, PADDED_COLUMNS), bf16)
    square = pltpu.VMEM((NOBS, NOBS), bf16)
    return pl.pallas_call(
        observation_kernel,
        out_shape=(columns, factors),
        in_specs=[SMEM, VMEM, VMEM, VMEM, VMEM],
        out_specs=(VMEM,) * 2,
        scratch_shapes=[
            pltpu.VMEM((MEMBERS, NOBS), f32),
            pltpu.VMEM((MEMBERS, NOBS), f32),
            square,
            pltpu.VMEM((128, NOBS), f32),
            pltpu.VMEM((NOBS, 128), f32),
            pltpu.VMEM((NOBS, 2 * GROUP), bf16),
            square,
            square,
            square,
            square,
        ],
        compiler_params=kernel_params(44),
        cost_estimate=pl.CostEstimate(flops=20 * 10**9, bytes_accessed=8 * 2**20, transcendentals=10**5),
        name="observations",
    )(position, plan, facts, own, other)


def for_windows(starts_ref, groups, size, align, visit):
    def start(g, i):
        return pl.multiple_of((starts_ref[g] & -align) + i * size, align)

    first_group = pl.program_id(0) * groups
    for n in range(groups):
        visit(n, first_group + n, start(first_group + n, 0), True)
    for n in range(groups):
        g = first_group + n
        count = (starts_ref[g + 1] - (starts_ref[g] & -align) + size - 1) // size

        def step(i, carry, n=n, g=g):
            visit(n, g, start(g, i), False)
            return carry

        lax.fori_loop(1, count, step, 0)


def first_tile(g, shape):
    return jnp.full(shape, (g * EIGHT).astype(f32)).astype(bf16)


COVARIANCE_GROUPS = 4


def covariance_kernel(position_ref, starts_ref, block_ref, columns_ref, *refs):
    out_refs, (total_ref,) = refs[: 2 * SUMS], refs[2 * SUMS :]

    @pl.when(pl.program_id(0) == 0)
    def _():
        total_ref[...] = jnp.zeros_like(total_ref)

    zero = jnp.zeros((WINDOW_ROWS, LANES), bf16)

    def visit(n, g, start, is_first):
        rows = pl.ds(start, WINDOW_ROWS)
        found = columns_ref[rows, TILES] == first_tile(g, (WINDOW_ROWS, LANES))
        left = [
            jnp.concatenate(
                [
                    jnp.where(found, columns_ref[rows, part * WIDE + n * LANES : part * WIDE + (n + 1) * LANES], zero)
                    for n in range(WIDE // LANES)
                ],
                axis=1,
            )
            for part in range(2)
        ]
        right = block_ref[:, n * EIGHT : (n + 1) * EIGHT, :].reshape(WIDE, LANES)
        both = dot(jnp.concatenate(left, axis=0), jnp.concatenate(two_parts(right), axis=1))
        both = both[:WINDOW_ROWS] + both[WINDOW_ROWS:]
        total_ref[rows, :] += both[:, :LANES] + both[:, LANES:]

    for_windows(starts_ref, COVARIANCE_GROUPS, WINDOW_ROWS, 16, visit)

    @pl.when(pl.program_id(0) == pl.num_programs(0) - 1)
    def _():
        for d in range(SUMS):
            to = (position_ref[1] + d) & (SUMS - 1)
            start = pl.multiple_of(to * FIRST_CHUNK, 16)
            out_refs[d][...] = total_ref[pl.ds(start, FIRST_CHUNK), :]
            start = pl.multiple_of(FIRST + to * REST_CHUNK, 16)
            out_refs[SUMS + d][...] = total_ref[pl.ds(start, REST_CHUNK), :]


def covariances(position, starts, block, columns):
    steps = GROUPS // COVARIANCE_GROUPS
    return pl.pallas_call(
        covariance_kernel,
        grid=(steps,),
        out_shape=(struct((FIRST_CHUNK, LANES)),) * SUMS + (struct((REST_CHUNK, LANES)),) * SUMS,
        in_specs=[SMEM, SMEM, pl.BlockSpec((GROUP, OWN_TILES // steps, LANES), lambda i: (0, i, 0)), VMEM],
        out_specs=(VMEM,) * (2 * SUMS),
        scratch_shapes=[pltpu.VMEM((PADDED_ROWS, LANES), f32)],
        compiler_params=kernel_params(24),
        cost_estimate=pl.CostEstimate(flops=3 * 10**9, bytes_accessed=4 * 2**20, transcendentals=0),
        name="covariances",
    )(position, starts, block, columns)


UPDATE_GROUPS = 2


def update_kernel(position_ref, starts_ref, *refs):
    sums_refs = refs[: 2 * SUMS]
    block_ref, factors_ref, out_ref, right_ref = refs[2 * SUMS :]

    @pl.when(pl.program_id(0) == 0)
    def _():
        for d in range(SUMS):
            of = (position_ref[1] - d) & (SUMS - 1)
            start = pl.multiple_of(of * FIRST_CHUNK, 16)
            right_ref[pl.ds(start, FIRST_CHUNK), :] = jnp.concatenate(two_parts(sums_refs[d][...]), axis=1)
            start = pl.multiple_of(FIRST + of * REST_CHUNK, 16)
            right_ref[pl.ds(start, REST_CHUNK), :] = jnp.concatenate(two_parts(sums_refs[SUMS + d][...]), axis=1)
        right_ref[NOBS:, :] = jnp.zeros((WINDOW_COLUMNS, 2 * LANES), bf16)

    def visit(n, g, start, is_first):
        columns = pl.ds(start, WINDOW_COLUMNS)
        found = factors_ref[TILE_ROWS, columns] == first_tile(g, (16, WINDOW_COLUMNS))
        found = jnp.where(found, jnp.ones((16, WINDOW_COLUMNS), bf16), jnp.zeros((16, WINDOW_COLUMNS), bf16))
        left = [
            (factors_ref[part, columns].reshape(WIDE // 16, 16, WINDOW_COLUMNS) * found[None]).reshape(WIDE, WINDOW_COLUMNS)
            for part in (slice(0, WIDE), LOW)
        ]
        both = dot(jnp.concatenate(left, axis=0), right_ref[columns, :])
        both = both[:WIDE] + both[WIDE:]
        change = (both[:, :LANES] + both[:, LANES:]).reshape(GROUP, EIGHT, LANES)
        here = slice(n * EIGHT, (n + 1) * EIGHT)
        out_ref[:, here, :] = (block_ref if is_first else out_ref)[:, here, :] + change

    for_windows(starts_ref, UPDATE_GROUPS, WINDOW_COLUMNS, LANES, visit)


def updated(position, starts, sums, block, factors):
    steps = GROUPS // UPDATE_GROUPS
    by_tiles = pl.BlockSpec((GROUP, OWN_TILES // steps, LANES), lambda i: (0, i, 0))
    return pl.pallas_call(
        update_kernel,
        grid=(steps,),
        out_shape=struct((GROUP, OWN_TILES, LANES)),
        in_specs=[SMEM, SMEM] + [VMEM] * (2 * SUMS) + [by_tiles, VMEM],
        out_specs=by_tiles,
        scratch_shapes=[pltpu.VMEM((PADDED_COLUMNS, 2 * LANES), bf16)],
        compiler_params=kernel_params(24),
        cost_estimate=pl.CostEstimate(flops=4 * 10**9, bytes_accessed=8 * 2**20, transcendentals=0),
        name="updated",
    )(position, starts, *sums, block, factors)


def exchange(value, axes=PEERS):
    return lax.all_to_all(value, axes, 0, 0, tiled=True)


def passed_along(value, by):
    return lax.ppermute(value, "h", [(i, (i + by) % SUMS) for i in range(SUMS)])


def summed(parts):
    total = parts[0]
    for by in range(1, SUMS):
        total = total + passed_along(parts[by], by)
    return (total, *(passed_along(total, by) for by in range(1, SUMS)))


def shards(state, locations, tile_mask, plan, obs_value, obs_error):
    residue = lax.axis_index(PEERS) // SLICES
    position = jnp.stack([residue, lax.axis_index("h"), lax.axis_index("c"), lax.axis_index(ALL)]).astype(i32)
    rows = state.reshape(ROWS, LANES)

    masks = own_masks(position, locations.reshape(-1, LANES), tile_mask)
    masks = exchange(masks.reshape(GROUP_CHIPS, 4, LANES), CHIPS).sum(axis=0)
    tiles = locations // TILE

    observed = own_columns(plan, locations, rows)
    mine = jnp.concatenate([observed, masks], axis=0)
    all_four = [mine] + [passed_along(mine, by) for by in range(1, SUMS)]
    payload = jnp.concatenate(
        [*(each[0:8] for each in all_four), sum(each[8:12] for each in all_four), jnp.zeros((4, LANES), f32)], axis=0
    )
    gathered = exchange(jnp.broadcast_to(payload[None], (GROUP_CHIPS, 40, LANES)), CHIPS)
    block, gathered = lax.optimization_barrier((spread_out(rows), gathered))
    other = lax.ppermute(gathered, "c", [(0, 1), (1, 0)])
    block, other = lax.optimization_barrier((block, other))
    block = exchange(block)

    facts = jnp.concatenate(
        [tiles.astype(f32)[None], obs_value[None], obs_error[None], jnp.zeros((5, NOBS), f32)], axis=0
    )
    columns, factors = observations(
        position, plan[None], facts, gathered.reshape(-1, LANES), other.reshape(-1, LANES)
    )
    nth_own = (residue - tiles + RADIUS) & (RESIDUES - 1)
    own_tile = jnp.where(nth_own < WINDOW, ((tiles - RADIUS + nth_own) & (NTILES - 1)) // RESIDUES, OWN_TILES)
    starts = jnp.sum(own_tile[None, :] < EIGHT * jnp.arange(GROUPS + 1, dtype=i32)[:, None], axis=1, dtype=i32)
    nth_all = (jnp.arange(RESIDUES, dtype=i32)[:, None] - tiles[None, :] + RADIUS) & (RESIDUES - 1)
    most = jnp.max(jnp.sum(nth_all < WINDOW, axis=1, dtype=i32))

    parts = covariances(position, starts, block, columns)
    rest = lax.cond(most > FIRST, summed, lambda parts: parts, parts[SUMS:])
    sums = summed(parts[:SUMS]) + tuple(rest)
    block = exchange(updated(position, starts, sums, block, factors))
    return collect(block).reshape(state.shape)


def solution(mesh):
    fine = Mesh(mesh.devices.reshape(4, 4, 2, 2, 4), ALL)
    placed = (P(ALL, None), P(), P(ALL, None), P(), P(), P())
    return jax.shard_map(shards, mesh=fine, in_specs=placed, out_specs=P(ALL, None), check_vma=False)
```

```python
import functools

import jax
import jax.numpy as jnp
from jax import lax
from jax.experimental import pallas as pl
from jax.experimental.pallas import tpu as pltpu
from jax.sharding import Mesh, PartitionSpec as P

MEMBERS = 256
TILE = 512
NTILES = 2048
RADIUS = 4
WINDOW = 2 * RADIUS + 1
BATCH_OBS = 256
BATCHES = 4
NOBS = BATCH_OBS * BATCHES

ALL = ("y", "h", "l", "c", "x")
PEERS = ("c", "y", "l", "x")
CHIPS = ("y", "l", "x")
GROUP = 64
CORES = 2
GROUP_CHIPS = GROUP // CORES
SUMS = 4
RESIDUES = 16
SLICES = 4
LANES = 128
OWN_TILES = NTILES // RESIDUES
ROWS = NTILES * TILE // LANES
EIGHT = 8
WIDE = EIGHT * GROUP
GROUPS = OWN_TILES // EIGHT
WINDOW_ROWS = 128
WINDOW_COLUMNS = 256
PADDED_ROWS = NOBS + WINDOW_ROWS
PADDED_COLUMNS = NOBS + WINDOW_COLUMNS
LOW = slice(WIDE, 2 * WIDE)
TILES = slice(2 * WIDE, 2 * WIDE + LANES)
TILE_ROWS = slice(2 * WIDE, 2 * WIDE + 16)
NOWHERE = -512
BLOCK_TILES = 16
FIRST = 640
FIRST_CHUNK = FIRST // SUMS
REST_CHUNK = (NOBS - FIRST) // SUMS

epsilon = 1e-06
f32 = jnp.float32
bf16 = jnp.bfloat16
i32 = jnp.int32

VMEM = pl.BlockSpec(memory_space=pltpu.VMEM)
SMEM = pl.BlockSpec(memory_space=pltpu.SMEM)


def kernel_params(mib):
    return pltpu.CompilerParams(vmem_limit_bytes=mib * 1024 * 1024)


def struct(shape, dtype=f32):
    return jax.ShapeDtypeStruct(shape, dtype)


def two_parts(value):
    high = value.astype(bf16)
    return high, (value - high.astype(f32)).astype(bf16)


def three_parts(value):
    high = value.astype(bf16)
    rest = value - high.astype(f32)
    middle = rest.astype(bf16)
    return high, middle, (rest - middle.astype(f32)).astype(bf16)


def dot(a, b):
    return lax.dot_general(a, b, (((1,), (0,)), ((), ())), preferred_element_type=f32)


def dot_parts(a_high, a_low, b_high, b_low):
    return dot(a_high, b_high) + dot(a_high, b_low) + dot(a_low, b_high)


def accurate_dot(a, b):
    return dot_parts(*two_parts(a), *two_parts(b))


def masks_kernel(position_ref, locations_ref, tile_mask_ref, out_ref):
    tiles_here = tile_mask_ref.shape[0]
    first = position_ref[3] * tiles_here
    per_row = NOBS // LANES
    relative = (locations_ref[...] >> 9) - RADIUS - first
    masks = [
        jnp.concatenate([tile_mask_ref[i : i + 1, g * LANES : (g + 1) * LANES] for g in range(per_row)], axis=0)
        for i in range(tiles_here)
    ]
    for n in range(16):
        local = (relative + n) & (NTILES - 1)
        found = jnp.zeros((per_row, LANES), i32)
        if n < WINDOW:
            for i in range(tiles_here):
                found = jnp.where(local == i, masks[i], found)
        out_ref[n * per_row : (n + 1) * per_row, :] = found.astype(f32)


def own_masks(position, locations, tile_mask):
    return pl.pallas_call(
        masks_kernel,
        out_shape=struct((16 * NOBS // LANES, LANES)),
        in_specs=[SMEM, VMEM, VMEM],
        out_specs=VMEM,
        compiler_params=kernel_params(4),
        cost_estimate=pl.CostEstimate(flops=10**5, bytes_accessed=10**5, transcendentals=0),
        name="own_masks",
    )(position, locations, tile_mask)


def columns_kernel(plan_ref, locations_ref, state_ref, out_ref, picked_ref):
    lane = lax.broadcasted_iota(i32, (1, LANES), 1)

    def step(i, carry):
        base = pl.multiple_of(i * 8, 8)
        found = []
        for u in range(8):
            where = locations_ref[plan_ref[base + u]]
            row = state_ref[pl.ds(where >> 7, 1), :]
            found.append(jnp.where(lane == (where & (LANES - 1)), row, 0.0))
        picked_ref[pl.ds(base, 8), :] = jnp.concatenate(found, axis=0)
        return carry

    lax.fori_loop(0, NOBS // 8, step, 0, unroll=2)
    ones = jnp.ones((16, LANES), bf16)
    total = jnp.zeros((16, NOBS), f32)
    for part in three_parts(picked_ref[...]):
        total = total + lax.dot_general(ones, part, (((1,), (1,)), ((), ())), preferred_element_type=f32)
    for g in range(NOBS // LANES):
        out_ref[pl.ds(g, 1), :] = total[0:1, g * LANES : (g + 1) * LANES]


def own_columns(plan, locations, rows):
    return pl.pallas_call(
        columns_kernel,
        out_shape=struct((NOBS // LANES, LANES)),
        in_specs=[SMEM, SMEM, VMEM],
        out_specs=VMEM,
        scratch_shapes=[pltpu.VMEM((NOBS, LANES), f32)],
        compiler_params=kernel_params(24),
        cost_estimate=pl.CostEstimate(flops=10**6, bytes_accessed=8 * 2**20, transcendentals=0),
        name="own_columns",
    )(plan, locations, rows)


def spread_kernel(state_ref, out_ref):
    for d in range(GROUP):
        out_ref[d] = state_ref[pl.ds(d, BLOCK_TILES, stride=GROUP), :]


def collect_kernel(in_ref, state_ref):
    rows_ref = in_ref.reshape(GROUP * BLOCK_TILES, LANES)
    for a in range(BLOCK_TILES):
        state_ref[a * GROUP : (a + 1) * GROUP, :] = rows_ref[pl.ds(a, GROUP, stride=BLOCK_TILES), :]


def reordered(kernel, value, out_shape, name):
    by_device = pl.BlockSpec((GROUP, BLOCK_TILES, LANES), lambda i: (0, i, 0))
    by_row = pl.BlockSpec((GROUP * BLOCK_TILES, LANES), lambda i: (i, 0))
    specs = (by_row, by_device) if value.ndim == 2 else (by_device, by_row)
    return pl.pallas_call(
        kernel,
        grid=(OWN_TILES // BLOCK_TILES,),
        out_shape=struct(out_shape),
        in_specs=[specs[0]],
        out_specs=specs[1],
        compiler_params=kernel_params(16),
        cost_estimate=pl.CostEstimate(flops=10**6, bytes_accessed=8 * 2**20, transcendentals=0),
        name=name,
    )(value)


def spread_out(rows):
    return reordered(spread_kernel, rows, (GROUP, OWN_TILES, LANES), "spread_out")


def collect(blocks):
    return reordered(collect_kernel, blocks, (ROWS, LANES), "collect")


def observation_kernel(
    position_ref, plan_ref, facts_ref, own_ref, other_ref,
    columns_ref, turned_high_ref, turned_low_ref, increments_ref, column_facts_ref, row_facts_ref,
    ensemble_ref, one_hot_ref, facts_scratch, in_columns_ref, own_turned_ref,
):
    core = position_ref[2]
    for d in range(SUMS):
        for gathered_ref, start in ((own_ref, core), (other_ref, 1 - core)):
            rows = pl.ds(pl.multiple_of(d * GROUP + start * GROUP_CHIPS, GROUP_CHIPS), GROUP_CHIPS)
            for g in range(NOBS // LANES):
                ensemble_ref[rows, g * LANES : (g + 1) * LANES] = gathered_ref[
                    pl.ds(d * 8 + g, GROUP_CHIPS, stride=40), :
                ]
    for g in range(NOBS // LANES):
        rows = pl.ds((g // 4) * 40 + 32 + g % 4, 16, stride=80)
        facts_scratch[0:16, g * LANES : (g + 1) * LANES] = own_ref[rows, :] + other_ref[rows, :]
    facts_scratch[16:24, :] = facts_ref[...]
    facts_scratch[24:128, :] = jnp.zeros((104, NOBS), f32)
    source = lax.broadcasted_iota(i32, (NOBS, NOBS), 0)
    one_hot_ref[...] = jnp.where(source == plan_ref[...], 1.0, 0.0).astype(bf16)
    high, middle, low = three_parts(facts_scratch[0:32, :])
    ordered = dot(high, one_hot_ref[...]) + dot(middle, one_hot_ref[...]) + dot(low, one_hot_ref[...])
    facts_scratch[0:32, :] = ordered
    for g in range(NOBS // LANES):
        in_columns_ref[g * LANES : (g + 1) * LANES, :] = facts_scratch[:, g * LANES : (g + 1) * LANES].T

    residue = position_ref[0]
    tile_row = facts_scratch[16:17, :].astype(i32)
    tile_column = in_columns_ref[:, 16:17].astype(i32)
    nth_row = (residue - tile_row + RADIUS) & (RESIDUES - 1)
    nth_column = (residue - tile_column + RADIUS) & (RESIDUES - 1)
    own_row = ((tile_row - RADIUS + nth_row) & (NTILES - 1)) >> 4
    own_column = ((tile_column - RADIUS + nth_column) & (NTILES - 1)) >> 4
    own_row = jnp.where(nth_row < WINDOW, own_row, -1)
    own_column = jnp.where(nth_column < WINDOW, own_column, -2)
    mask_column = jnp.zeros((NOBS, 1), f32)
    for n in range(WINDOW):
        mask_column = mask_column + jnp.where(nth_column == n, in_columns_ref[:, n : n + 1], 0.0)

    mask_row = jnp.zeros((1, NOBS), f32)
    for n in range(WINDOW):
        mask_row = mask_row + jnp.where(nth_row == n, facts_scratch[n : n + 1, :], 0.0)

    key_row = jnp.where(own_row < 0, OWN_TILES, own_row) * NOBS + lax.broadcasted_iota(i32, (1, NOBS), 1)
    key_column = jnp.where(own_column < 0, OWN_TILES, own_column) * NOBS + lax.broadcasted_iota(i32, (NOBS, 1), 0)
    lane = lax.broadcasted_iota(i32, (NOBS, LANES), 1)
    rank_row = jnp.sum(jnp.where(key_column < key_row, 1.0, 0.0), axis=0, keepdims=True).astype(i32)
    sort_ref = one_hot_ref
    sort_ref[...] = jnp.where(source == rank_row, 1.0, 0.0).astype(bf16)

    gain_rows = []
    for b in range(BATCHES):
        here = slice(b * BATCH_OBS, (b + 1) * BATCH_OBS)
        prior = ensemble_ref[:, here]
        average = jnp.sum(prior, axis=0, keepdims=True) / MEMBERS
        anomaly = prior - average
        spread = jnp.sum(anomaly * anomaly, axis=0, keepdims=True) / (MEMBERS - 1) + epsilon
        value = facts_scratch[17:18, here]
        error = facts_scratch[18:19, here]
        shrink = jnp.sqrt(error / (spread + error))
        moved = (average * error + value * spread) / (spread + error)
        increments = (shrink - 1.0) * anomaly + (moved - average)
        increments_ref[:, here] = increments
        turned = anomaly.T
        spread_column = jnp.sum(turned * turned, axis=1, keepdims=True) / (MEMBERS - 1) + epsilon
        gain_column = 1.0 / ((MEMBERS - 1) * spread_column)
        turned_high, turned_low = two_parts(turned)
        turned_high_ref[here, :] = turned_high
        turned_low_ref[here, :] = turned_low
        own_turned_ref[here, :] = jnp.concatenate([turned_high[:, 0:GROUP], turned_low[:, 0:GROUP]], axis=1)
        gain_rows.append(1.0 / ((MEMBERS - 1) * spread))
        column_facts_ref[here, :] = jnp.where(
            lane[here] == 0, mask_column[here] * gain_column, own_column[here].astype(f32)
        )
        if b < BATCHES - 1:
            after = slice((b + 1) * BATCH_OBS, NOBS)
            later = ensemble_ref[:, after]
            covariance = dot_parts(turned_high, turned_low, *two_parts(later))
            apart = (tile_row[:, after] - tile_column[here] + RADIUS) & (NTILES - 1)
            masks = jnp.zeros(apart.shape, f32)
            for n in range(WINDOW):
                masks = jnp.where(apart == n, in_columns_ref[here, n : n + 1], masks)
            ensemble_ref[:, after] = later + accurate_dot(increments, covariance * masks * gain_column)

    row_facts_ref[0:8, :] = jnp.broadcast_to(mask_row * jnp.concatenate(gain_rows, axis=1), (8, NOBS))
    row_facts_ref[8:16, :] = jnp.broadcast_to(own_row.astype(f32), (8, NOBS))

    tile_here = jnp.where(own_column < 0, NOWHERE, own_column).astype(f32)
    tile_here = jnp.broadcast_to(tile_here, (NOBS, LANES)).astype(bf16)
    sorted_columns = dot(sort_ref[...], jnp.concatenate([own_turned_ref[...], tile_here], axis=1))
    high = sorted_columns[:, 0:GROUP].astype(bf16)
    low = sorted_columns[:, GROUP : 2 * GROUP].astype(bf16)
    replicate = jnp.where(
        lax.broadcasted_iota(i32, (GROUP, WIDE), 1) >> 3 == lax.broadcasted_iota(i32, (GROUP, WIDE), 0), 1.0, 0.0
    ).astype(bf16)
    columns_ref[0:NOBS, 0:WIDE] = dot(high, replicate).astype(bf16)
    columns_ref[0:NOBS, LOW] = dot(low, replicate).astype(bf16)
    nth_of_eight = (lax.broadcasted_iota(i32, (NOBS, LANES), 1) & (EIGHT - 1)).astype(f32)
    columns_ref[0:NOBS, TILES] = (sorted_columns[:, LANES : LANES + 1] - nth_of_eight).astype(bf16)
    columns_ref[NOBS:, 0 : 2 * WIDE] = jnp.zeros((WINDOW_ROWS, 2 * WIDE), bf16)
    columns_ref[NOBS:, TILES] = jnp.full((WINDOW_ROWS, LANES), NOWHERE, bf16)


def observations(position, plan, facts, own, other):
    turned = struct((NOBS, MEMBERS), bf16)
    return pl.pallas_call(
        observation_kernel,
        out_shape=(
            struct((PADDED_ROWS, 2 * WIDE + LANES), bf16), turned, turned,
            struct((MEMBERS, NOBS)), struct((NOBS, LANES)), struct((16, NOBS)),
        ),
        in_specs=[SMEM, VMEM, VMEM, VMEM, VMEM],
        out_specs=(VMEM,) * 6,
        scratch_shapes=[
            pltpu.VMEM((MEMBERS, NOBS), f32),
            pltpu.VMEM((NOBS, NOBS), bf16),
            pltpu.VMEM((128, NOBS), f32),
            pltpu.VMEM((NOBS, 128), f32),
            pltpu.VMEM((NOBS, 2 * GROUP), bf16),
        ],
        compiler_params=kernel_params(32),
        cost_estimate=pl.CostEstimate(flops=8 * 10**9, bytes_accessed=8 * 2**20, transcendentals=10**5),
        name="observations",
    )(position, plan, facts, own, other)


def factors_kernel(
    turned_high_ref, turned_low_ref, all_increments_ref, column_facts_ref, row_facts_ref,
    factors_ref,
    increments_ref, links_high_ref, links_low_ref, sort_back_ref,
):
    own_row = row_facts_ref[8:9, :].astype(i32)
    own_column = column_facts_ref[:, 1:2].astype(i32)
    for b in range(1, BATCHES):
        here = slice(b * BATCH_OBS, (b + 1) * BATCH_OBS)
        before = slice(0, b * BATCH_OBS)
        links = dot_parts(turned_high_ref[here, :], turned_low_ref[here, :], *two_parts(all_increments_ref[:, before]))
        links = jnp.where(own_column[here] == own_row[:, before], links * column_facts_ref[here, 0:1], 0.0)
        links_high, links_low = two_parts(links)
        links_high_ref[here, before] = links_high
        links_low_ref[here, before] = links_low
    increments_ref[...] = all_increments_ref[0:GROUP, :]
    for b in reversed(range(BATCHES - 1)):
        here = slice(b * BATCH_OBS, (b + 1) * BATCH_OBS)
        after = slice((b + 1) * BATCH_OBS, NOBS)
        increments_ref[:, here] += dot_parts(
            *two_parts(increments_ref[:, after]), links_high_ref[after, here], links_low_ref[after, here]
        )
    factors = increments_ref[...] * row_facts_ref[0:1, :]
    key_row = jnp.where(own_row < 0, OWN_TILES, own_row) * NOBS + lax.broadcasted_iota(i32, (1, NOBS), 1)
    key_column = jnp.where(own_column < 0, OWN_TILES, own_column) * NOBS + lax.broadcasted_iota(i32, (NOBS, 1), 0)
    rank_column = jnp.sum(jnp.where(key_row < key_column, 1.0, 0.0), axis=1, keepdims=True).astype(i32)
    to = lax.broadcasted_iota(i32, (NOBS, NOBS), 1)
    sort_back_ref[...] = jnp.where(to == rank_column, 1.0, 0.0).astype(bf16)

    factors_high, factors_low = two_parts(factors)
    tile_there = jnp.where(own_row < 0, NOWHERE, own_row).astype(f32)
    tile_there = jnp.broadcast_to(tile_there, (GROUP, NOBS)).astype(bf16)
    sorted_rows = dot(jnp.concatenate([factors_high, factors_low, tile_there], axis=0), sort_back_ref[...])
    replicate = jnp.where(
        lax.broadcasted_iota(i32, (WIDE, GROUP), 0) >> 3 == lax.broadcasted_iota(i32, (WIDE, GROUP), 1), 1.0, 0.0
    ).astype(bf16)
    factors_ref[0:WIDE, 0:NOBS] = dot(replicate, sorted_rows[0:GROUP].astype(bf16)).astype(bf16)
    factors_ref[LOW, 0:NOBS] = dot(replicate, sorted_rows[GROUP : 2 * GROUP].astype(bf16)).astype(bf16)
    nth_of_eight = (lax.broadcasted_iota(i32, (16, NOBS), 0) & (EIGHT - 1)).astype(f32)
    factors_ref[TILE_ROWS, 0:NOBS] = (sorted_rows[2 * GROUP : 2 * GROUP + 16] - nth_of_eight).astype(bf16)
    factors_ref[0 : 2 * WIDE, NOBS:] = jnp.zeros((2 * WIDE, WINDOW_COLUMNS), bf16)
    factors_ref[TILE_ROWS, NOBS:] = jnp.full((16, WINDOW_COLUMNS), NOWHERE, bf16)


def factors_of(turned_high, turned_low, increments, column_facts, row_facts):
    square = pltpu.VMEM((NOBS, NOBS), bf16)
    return pl.pallas_call(
        factors_kernel,
        out_shape=struct((2 * WIDE + 16, PADDED_COLUMNS), bf16),
        in_specs=[VMEM] * 5,
        out_specs=VMEM,
        scratch_shapes=[pltpu.VMEM((GROUP, NOBS), f32), square, square, square],
        compiler_params=kernel_params(32),
        cost_estimate=pl.CostEstimate(flops=8 * 10**9, bytes_accessed=6 * 2**20, transcendentals=0),
        name="factors",
    )(turned_high, turned_low, increments, column_facts, row_facts)


def for_windows(starts_ref, groups, size, align, visit):
    def start(g, i):
        return pl.multiple_of((starts_ref[g] & -align) + i * size, align)

    first_group = pl.program_id(0) * groups
    for n in range(groups):
        visit(n, first_group + n, start(first_group + n, 0), True)
    for n in range(groups):
        g = first_group + n
        count = (starts_ref[g + 1] - (starts_ref[g] & -align) + size - 1) // size

        def step(i, carry, n=n, g=g):
            visit(n, g, start(g, i), False)
            return carry

        lax.fori_loop(1, count, step, 0)


def first_tile(g, shape):
    return jnp.full(shape, (g * EIGHT).astype(f32)).astype(bf16)


COVARIANCE_GROUPS = 4


def covariance_kernel(position_ref, starts_ref, block_ref, columns_ref, *refs):
    out_refs, (total_ref,) = refs[: 2 * SUMS], refs[2 * SUMS :]

    @pl.when(pl.program_id(0) == 0)
    def _():
        total_ref[...] = jnp.zeros_like(total_ref)

    zero = jnp.zeros((WINDOW_ROWS, LANES), bf16)

    def visit(n, g, start, is_first):
        rows = pl.ds(start, WINDOW_ROWS)
        found = columns_ref[rows, TILES] == first_tile(g, (WINDOW_ROWS, LANES))
        left = [
            jnp.concatenate(
                [
                    jnp.where(found, columns_ref[rows, part * WIDE + n * LANES : part * WIDE + (n + 1) * LANES], zero)
                    for n in range(WIDE // LANES)
                ],
                axis=1,
            )
            for part in range(2)
        ]
        right = block_ref[:, n * EIGHT : (n + 1) * EIGHT, :].reshape(WIDE, LANES)
        both = dot(jnp.concatenate(left, axis=0), jnp.concatenate(two_parts(right), axis=1))
        both = both[:WINDOW_ROWS] + both[WINDOW_ROWS:]
        total_ref[rows, :] += both[:, :LANES] + both[:, LANES:]

    for_windows(starts_ref, COVARIANCE_GROUPS, WINDOW_ROWS, 16, visit)

    @pl.when(pl.program_id(0) == pl.num_programs(0) - 1)
    def _():
        for d in range(SUMS):
            to = (position_ref[1] + d) & (SUMS - 1)
            start = pl.multiple_of(to * FIRST_CHUNK, 16)
            out_refs[d][...] = total_ref[pl.ds(start, FIRST_CHUNK), :]
            start = pl.multiple_of(FIRST + to * REST_CHUNK, 16)
            out_refs[SUMS + d][...] = total_ref[pl.ds(start, REST_CHUNK), :]


def covariances(position, starts, block, columns):
    steps = GROUPS // COVARIANCE_GROUPS
    return pl.pallas_call(
        covariance_kernel,
        grid=(steps,),
        out_shape=(struct((FIRST_CHUNK, LANES)),) * SUMS + (struct((REST_CHUNK, LANES)),) * SUMS,
        in_specs=[SMEM, SMEM, pl.BlockSpec((GROUP, OWN_TILES // steps, LANES), lambda i: (0, i, 0)), VMEM],
        out_specs=(VMEM,) * (2 * SUMS),
        scratch_shapes=[pltpu.VMEM((PADDED_ROWS, LANES), f32)],
        compiler_params=kernel_params(24),
        cost_estimate=pl.CostEstimate(flops=3 * 10**9, bytes_accessed=4 * 2**20, transcendentals=0),
        name="covariances",
    )(position, starts, block, columns)


UPDATE_GROUPS = 2


def update_kernel(position_ref, starts_ref, *refs):
    sums_refs = refs[: 2 * SUMS]
    block_ref, factors_ref, out_ref, right_ref = refs[2 * SUMS :]

    @pl.when(pl.program_id(0) == 0)
    def _():
        for d in range(SUMS):
            of = (position_ref[1] - d) & (SUMS - 1)
            start = pl.multiple_of(of * FIRST_CHUNK, 16)
            right_ref[pl.ds(start, FIRST_CHUNK), :] = jnp.concatenate(two_parts(sums_refs[d][...]), axis=1)
            start = pl.multiple_of(FIRST + of * REST_CHUNK, 16)
            right_ref[pl.ds(start, REST_CHUNK), :] = jnp.concatenate(two_parts(sums_refs[SUMS + d][...]), axis=1)
        right_ref[NOBS:, :] = jnp.zeros((WINDOW_COLUMNS, 2 * LANES), bf16)

    def visit(n, g, start, is_first):
        columns = pl.ds(start, WINDOW_COLUMNS)
        found = factors_ref[TILE_ROWS, columns] == first_tile(g, (16, WINDOW_COLUMNS))
        found = jnp.where(found, jnp.ones((16, WINDOW_COLUMNS), bf16), jnp.zeros((16, WINDOW_COLUMNS), bf16))
        left = [
            (factors_ref[part, columns].reshape(WIDE // 16, 16, WINDOW_COLUMNS) * found[None]).reshape(WIDE, WINDOW_COLUMNS)
            for part in (slice(0, WIDE), LOW)
        ]
        both = dot(jnp.concatenate(left, axis=0), right_ref[columns, :])
        both = both[:WIDE] + both[WIDE:]
        change = (both[:, :LANES] + both[:, LANES:]).reshape(GROUP, EIGHT, LANES)
        here = slice(n * EIGHT, (n + 1) * EIGHT)
        out_ref[:, here, :] = (block_ref if is_first else out_ref)[:, here, :] + change

    for_windows(starts_ref, UPDATE_GROUPS, WINDOW_COLUMNS, LANES, visit)


def updated(position, starts, sums, block, factors):
    steps = GROUPS // UPDATE_GROUPS
    by_tiles = pl.BlockSpec((GROUP, OWN_TILES // steps, LANES), lambda i: (0, i, 0))
    return pl.pallas_call(
        update_kernel,
        grid=(steps,),
        out_shape=struct((GROUP, OWN_TILES, LANES)),
        in_specs=[SMEM, SMEM] + [VMEM] * (2 * SUMS) + [by_tiles, VMEM],
        out_specs=by_tiles,
        scratch_shapes=[pltpu.VMEM((PADDED_COLUMNS, 2 * LANES), bf16)],
        compiler_params=kernel_params(24),
        cost_estimate=pl.CostEstimate(flops=4 * 10**9, bytes_accessed=8 * 2**20, transcendentals=0),
        name="updated",
    )(position, starts, *sums, block, factors)


def exchange(value, axes=PEERS):
    return lax.all_to_all(value, axes, 0, 0, tiled=True)


def passed_along(value, by):
    return lax.ppermute(value, "h", [(i, (i + by) % SUMS) for i in range(SUMS)])


def summed(parts):
    total = parts[0]
    for by in range(1, SUMS):
        total = total + passed_along(parts[by], by)
    return (total, *(passed_along(total, by) for by in range(1, SUMS)))


def shards(state, locations, tile_mask, plan, obs_value, obs_error):
    residue = lax.axis_index(PEERS) // SLICES
    position = jnp.stack([residue, lax.axis_index("h"), lax.axis_index("c"), lax.axis_index(ALL)]).astype(i32)
    rows = state.reshape(ROWS, LANES)

    masks = own_masks(position, locations.reshape(-1, LANES), tile_mask)
    masks = exchange(masks.reshape(GROUP_CHIPS, 4, LANES), CHIPS).sum(axis=0)
    tiles = locations // TILE

    block, masks = lax.optimization_barrier((spread_out(rows), masks))
    block = exchange(block)
    mine = jnp.concatenate([own_columns(plan, locations, rows), masks], axis=0)
    all_four = [mine] + [passed_along(mine, by) for by in range(1, SUMS)]
    payload = jnp.concatenate(
        [*(each[0:8] for each in all_four), sum(each[8:12] for each in all_four), jnp.zeros((4, LANES), f32)], axis=0
    )
    block, payload = lax.optimization_barrier((block, payload))
    gathered = exchange(jnp.broadcast_to(payload[None], (GROUP_CHIPS, 40, LANES)), CHIPS)
    other = lax.ppermute(gathered, "c", [(0, 1), (1, 0)])

    facts = jnp.concatenate(
        [tiles.astype(f32)[None], obs_value[None], obs_error[None], jnp.zeros((5, NOBS), f32)], axis=0
    )
    columns, *for_factors = observations(
        position, plan[None], facts, gathered.reshape(-1, LANES), other.reshape(-1, LANES)
    )
    nth_own = (residue - tiles + RADIUS) & (RESIDUES - 1)
    own_tile = jnp.where(nth_own < WINDOW, ((tiles - RADIUS + nth_own) & (NTILES - 1)) // RESIDUES, OWN_TILES)
    starts = jnp.sum(own_tile[None, :] < EIGHT * jnp.arange(GROUPS + 1, dtype=i32)[:, None], axis=1, dtype=i32)
    nth_all = (jnp.arange(RESIDUES, dtype=i32)[:, None] - tiles[None, :] + RADIUS) & (RESIDUES - 1)
    most = jnp.max(jnp.sum(nth_all < WINDOW, axis=1, dtype=i32))

    parts = covariances(position, starts, block, columns)
    rest = lax.cond(most > FIRST, summed, lambda parts: parts, parts[SUMS:])
    sums = summed(parts[:SUMS]) + tuple(rest)
    block = exchange(updated(position, starts, sums, block, factors_of(*for_factors)))
    return collect(block).reshape(state.shape)


def solution(mesh):
    fine = Mesh(mesh.devices.reshape(4, 4, 2, 2, 4), ALL)
    placed = (P(ALL, None), P(), P(ALL, None), P(), P(), P())
    return jax.shard_map(shards, mesh=fine, in_specs=placed, out_specs=P(ALL, None), check_vma=False)
```

```python
import functools

import jax
import jax.numpy as jnp
from jax import lax
from jax.experimental import pallas as pl
from jax.experimental.pallas import tpu as pltpu
from jax.sharding import Mesh, PartitionSpec as P

MEMBERS = 256
TILE = 512
NTILES = 2048
RADIUS = 4
WINDOW = 2 * RADIUS + 1
BATCH_OBS = 256
BATCHES = 4
NOBS = BATCH_OBS * BATCHES

ALL = ("y", "h", "l", "c", "x")
PEERS = ("c", "y", "l", "x")
CHIPS = ("y", "l", "x")
GROUP = 64
CORES = 2
GROUP_CHIPS = GROUP // CORES
SUMS = 4
RESIDUES = 16
SLICES = 4
LANES = 128
OWN_TILES = NTILES // RESIDUES
ROWS = NTILES * TILE // LANES
EIGHT = 8
WIDE = EIGHT * GROUP
GROUPS = OWN_TILES // EIGHT
WINDOW_ROWS = 128
WINDOW_COLUMNS = 256
PADDED_ROWS = NOBS + WINDOW_ROWS
PADDED_COLUMNS = NOBS + WINDOW_COLUMNS
LOW = slice(WIDE, 2 * WIDE)
TILES = slice(2 * WIDE, 2 * WIDE + LANES)
TILE_ROWS = slice(2 * WIDE, 2 * WIDE + 16)
NOWHERE = -512
BLOCK_TILES = 16
FIRST = 640
FIRST_CHUNK = FIRST // SUMS
REST_CHUNK = (NOBS - FIRST) // SUMS

epsilon = 1e-06
f32 = jnp.float32
bf16 = jnp.bfloat16
i32 = jnp.int32

VMEM = pl.BlockSpec(memory_space=pltpu.VMEM)
SMEM = pl.BlockSpec(memory_space=pltpu.SMEM)
ANY = pl.BlockSpec(memory_space=pl.ANY)


def kernel_params(mib):
    return pltpu.CompilerParams(vmem_limit_bytes=mib * 1024 * 1024)


def struct(shape, dtype=f32):
    return jax.ShapeDtypeStruct(shape, dtype)


def two_parts(value):
    high = value.astype(bf16)
    return high, (value - high.astype(f32)).astype(bf16)


def three_parts(value):
    high = value.astype(bf16)
    rest = value - high.astype(f32)
    middle = rest.astype(bf16)
    return high, middle, (rest - middle.astype(f32)).astype(bf16)


def dot(a, b):
    return lax.dot_general(a, b, (((1,), (0,)), ((), ())), preferred_element_type=f32)


def dot_parts(a_high, a_low, b_high, b_low):
    return dot(a_high, b_high) + dot(a_high, b_low) + dot(a_low, b_high)


def accurate_dot(a, b):
    return dot_parts(*two_parts(a), *two_parts(b))


def masks_kernel(position_ref, locations_ref, tile_mask_ref, out_ref):
    tiles_here = tile_mask_ref.shape[0]
    first = position_ref[3] * tiles_here
    per_row = NOBS // LANES
    relative = (locations_ref[...] >> 9) - RADIUS - first
    masks = [
        jnp.concatenate([tile_mask_ref[i : i + 1, g * LANES : (g + 1) * LANES] for g in range(per_row)], axis=0)
        for i in range(tiles_here)
    ]
    for n in range(16):
        local = (relative + n) & (NTILES - 1)
        found = jnp.zeros((per_row, LANES), i32)
        if n < WINDOW:
            for i in range(tiles_here):
                found = jnp.where(local == i, masks[i], found)
        out_ref[n * per_row : (n + 1) * per_row, :] = found.astype(f32)


def own_masks(position, locations, tile_mask):
    return pl.pallas_call(
        masks_kernel,
        out_shape=struct((16 * NOBS // LANES, LANES)),
        in_specs=[SMEM, VMEM, VMEM],
        out_specs=VMEM,
        compiler_params=kernel_params(4),
        cost_estimate=pl.CostEstimate(flops=10**5, bytes_accessed=10**5, transcendentals=0),
        name="own_masks",
    )(position, locations, tile_mask)


def columns_kernel(plan_ref, locations_ref, state_ref, out_ref, picked_ref):
    lane = lax.broadcasted_iota(i32, (1, LANES), 1)

    def step(i, carry):
        base = pl.multiple_of(i * 8, 8)
        found = []
        for u in range(8):
            where = locations_ref[plan_ref[base + u]]
            row = state_ref[pl.ds(where >> 7, 1), :]
            found.append(jnp.where(lane == (where & (LANES - 1)), row, 0.0))
        picked_ref[pl.ds(base, 8), :] = jnp.concatenate(found, axis=0)
        return carry

    lax.fori_loop(0, NOBS // 8, step, 0, unroll=2)
    ones = jnp.ones((16, LANES), bf16)
    total = jnp.zeros((16, NOBS), f32)
    for part in three_parts(picked_ref[...]):
        total = total + lax.dot_general(ones, part, (((1,), (1,)), ((), ())), preferred_element_type=f32)
    for g in range(NOBS // LANES):
        out_ref[pl.ds(g, 1), :] = total[0:1, g * LANES : (g + 1) * LANES]


def own_columns(plan, locations, rows):
    return pl.pallas_call(
        columns_kernel,
        out_shape=struct((NOBS // LANES, LANES)),
        in_specs=[SMEM, SMEM, VMEM],
        out_specs=VMEM,
        scratch_shapes=[pltpu.VMEM((NOBS, LANES), f32)],
        compiler_params=kernel_params(24),
        cost_estimate=pl.CostEstimate(flops=10**6, bytes_accessed=8 * 2**20, transcendentals=0),
        name="own_columns",
    )(plan, locations, rows)


def spread_kernel(state_ref, out_ref):
    for d in range(GROUP):
        out_ref[d] = state_ref[pl.ds(d, BLOCK_TILES, stride=GROUP), :]


def spread_out(rows):
    return pl.pallas_call(
        spread_kernel,
        grid=(OWN_TILES // BLOCK_TILES,),
        out_shape=struct((GROUP, OWN_TILES, LANES)),
        in_specs=[pl.BlockSpec((GROUP * BLOCK_TILES, LANES), lambda i: (i, 0))],
        out_specs=pl.BlockSpec((GROUP, BLOCK_TILES, LANES), lambda i: (0, i, 0)),
        compiler_params=kernel_params(16),
        cost_estimate=pl.CostEstimate(flops=10**6, bytes_accessed=8 * 2**20, transcendentals=0),
        name="spread_out",
    )(rows)


PIECES = 8


def collect_kernel(in_ref, state_ref, held_ref, in_sems, out_sems):
    devices = GROUP // PIECES
    arriving = [
        pltpu.make_async_copy(
            in_ref.at[pl.ds(n * devices, devices)], held_ref.at[pl.ds(n * devices, devices)], in_sems.at[n]
        )
        for n in range(PIECES)
    ]
    leaving = [
        pltpu.make_async_copy(held_ref.at[d], state_ref.at[:, d, :], out_sems.at[d]) for d in range(GROUP)
    ]
    for copy in arriving:
        copy.start()
    for n in range(PIECES):
        arriving[n].wait()
        for copy in leaving[n * devices : (n + 1) * devices]:
            copy.start()
    for copy in leaving:
        copy.wait()


def collect(blocks):
    return pl.pallas_call(
        collect_kernel,
        out_shape=struct((OWN_TILES, GROUP, LANES)),
        in_specs=[ANY],
        out_specs=ANY,
        scratch_shapes=[
            pltpu.VMEM((GROUP, OWN_TILES, LANES), f32),
            pltpu.SemaphoreType.DMA((PIECES,)),
            pltpu.SemaphoreType.DMA((GROUP,)),
        ],
        compiler_params=kernel_params(60),
        cost_estimate=pl.CostEstimate(flops=10**6, bytes_accessed=8 * 2**20, transcendentals=0),
        name="collect",
    )(blocks)


def observation_kernel(
    position_ref, plan_ref, facts_ref, own_ref, other_ref,
    columns_ref, factors_ref,
    ensemble_ref, increments_ref, one_hot_ref, facts_scratch, in_columns_ref,
    turned_ref, links_high_ref, links_low_ref, sort_ref, sort_back_ref,
):
    core = position_ref[2]
    for d in range(SUMS):
        for gathered_ref, start in ((own_ref, core), (other_ref, 1 - core)):
            rows = pl.ds(pl.multiple_of(d * GROUP + start * GROUP_CHIPS, GROUP_CHIPS), GROUP_CHIPS)
            for g in range(NOBS // LANES):
                ensemble_ref[rows, g * LANES : (g + 1) * LANES] = gathered_ref[
                    pl.ds(d * 8 + g, GROUP_CHIPS, stride=40), :
                ]
    for g in range(NOBS // LANES):
        rows = pl.ds((g // 4) * 40 + 32 + g % 4, 16, stride=80)
        facts_scratch[0:16, g * LANES : (g + 1) * LANES] = own_ref[rows, :] + other_ref[rows, :]
    facts_scratch[16:24, :] = facts_ref[...]
    facts_scratch[24:128, :] = jnp.zeros((104, NOBS), f32)
    source = lax.broadcasted_iota(i32, (NOBS, NOBS), 0)
    one_hot_ref[...] = jnp.where(source == plan_ref[...], 1.0, 0.0).astype(bf16)
    high, middle, low = three_parts(facts_scratch[0:32, :])
    ordered = dot(high, one_hot_ref[...]) + dot(middle, one_hot_ref[...]) + dot(low, one_hot_ref[...])
    facts_scratch[0:32, :] = ordered
    for g in range(NOBS // LANES):
        in_columns_ref[g * LANES : (g + 1) * LANES, :] = facts_scratch[:, g * LANES : (g + 1) * LANES].T

    residue = position_ref[0]
    tile_row = facts_scratch[16:17, :].astype(i32)
    tile_column = in_columns_ref[:, 16:17].astype(i32)
    nth_row = (residue - tile_row + RADIUS) & (RESIDUES - 1)
    nth_column = (residue - tile_column + RADIUS) & (RESIDUES - 1)
    own_row = ((tile_row - RADIUS + nth_row) & (NTILES - 1)) >> 4
    own_column = ((tile_column - RADIUS + nth_column) & (NTILES - 1)) >> 4
    own_row = jnp.where(nth_row < WINDOW, own_row, -1)
    own_column = jnp.where(nth_column < WINDOW, own_column, -2)
    mask_column = jnp.zeros((NOBS, 1), f32)
    for n in range(WINDOW):
        mask_column = mask_column + jnp.where(nth_column == n, in_columns_ref[:, n : n + 1], 0.0)

    mask_row = jnp.zeros((1, NOBS), f32)
    for n in range(WINDOW):
        mask_row = mask_row + jnp.where(nth_row == n, facts_scratch[n : n + 1, :], 0.0)

    key_row = jnp.where(own_row < 0, OWN_TILES, own_row) * NOBS + lax.broadcasted_iota(i32, (1, NOBS), 1)
    key_column = jnp.where(own_column < 0, OWN_TILES, own_column) * NOBS + lax.broadcasted_iota(i32, (NOBS, 1), 0)
    rank_row = jnp.sum(jnp.where(key_column < key_row, 1.0, 0.0), axis=0, keepdims=True).astype(i32)
    rank_column = jnp.sum(jnp.where(key_row < key_column, 1.0, 0.0), axis=1, keepdims=True).astype(i32)
    sort_ref[...] = jnp.where(source == rank_row, 1.0, 0.0).astype(bf16)
    to = lax.broadcasted_iota(i32, (NOBS, NOBS), 1)
    sort_back_ref[...] = jnp.where(to == rank_column, 1.0, 0.0).astype(bf16)

    gain_rows = []
    for b in range(BATCHES):
        here = slice(b * BATCH_OBS, (b + 1) * BATCH_OBS)
        prior = ensemble_ref[:, here]
        average = jnp.sum(prior, axis=0, keepdims=True) / MEMBERS
        anomaly = prior - average
        spread = jnp.sum(anomaly * anomaly, axis=0, keepdims=True) / (MEMBERS - 1) + epsilon
        value = facts_scratch[17:18, here]
        error = facts_scratch[18:19, here]
        shrink = jnp.sqrt(error / (spread + error))
        moved = (average * error + value * spread) / (spread + error)
        increments = (shrink - 1.0) * anomaly + (moved - average)
        increments_ref[:, here] = increments
        turned = anomaly.T
        spread_column = jnp.sum(turned * turned, axis=1, keepdims=True) / (MEMBERS - 1) + epsilon
        gain_column = 1.0 / ((MEMBERS - 1) * spread_column)
        turned_high, turned_low = two_parts(turned)
        turned_ref[here, :] = jnp.concatenate([turned_high[:, 0:GROUP], turned_low[:, 0:GROUP]], axis=1)
        gain_rows.append(1.0 / ((MEMBERS - 1) * spread))
        weight = mask_column[here] * gain_column
        if b > 0:
            before = b * BATCH_OBS
            links = accurate_dot(turned, increments_ref[:, 0:before])
            links = jnp.where(own_column[here] == own_row[:, 0:before], links * weight, 0.0)
            links_high, links_low = two_parts(links)
            links_high_ref[here, 0:before] = links_high
            links_low_ref[here, 0:before] = links_low
        if b < BATCHES - 1:
            after = slice((b + 1) * BATCH_OBS, NOBS)
            later = ensemble_ref[:, after]
            covariance = dot_parts(turned_high, turned_low, *two_parts(later))
            apart = (tile_row[:, after] - tile_column[here] + RADIUS) & (NTILES - 1)
            masks = jnp.zeros(apart.shape, f32)
            for n in range(WINDOW):
                masks = jnp.where(apart == n, in_columns_ref[here, n : n + 1], masks)
            ensemble_ref[:, after] = later + accurate_dot(increments, covariance * masks * gain_column)

    for b in reversed(range(BATCHES - 1)):
        here = slice(b * BATCH_OBS, (b + 1) * BATCH_OBS)
        after = slice((b + 1) * BATCH_OBS, NOBS)
        increments_ref[0:GROUP, here] += dot_parts(
            *two_parts(increments_ref[0:GROUP, after]), links_high_ref[after, here], links_low_ref[after, here]
        )
    factors = increments_ref[0:GROUP, :] * (mask_row * jnp.concatenate(gain_rows, axis=1))

    tile_here = jnp.where(own_column < 0, NOWHERE, own_column).astype(f32)
    tile_here = jnp.broadcast_to(tile_here, (NOBS, LANES)).astype(bf16)
    sorted_columns = dot(sort_ref[...], jnp.concatenate([turned_ref[...], tile_here], axis=1))
    high = sorted_columns[:, 0:GROUP].astype(bf16)
    low = sorted_columns[:, GROUP : 2 * GROUP].astype(bf16)
    replicate = jnp.where(
        lax.broadcasted_iota(i32, (GROUP, WIDE), 1) >> 3 == lax.broadcasted_iota(i32, (GROUP, WIDE), 0), 1.0, 0.0
    ).astype(bf16)
    columns_ref[0:NOBS, 0:WIDE] = dot(high, replicate).astype(bf16)
    columns_ref[0:NOBS, LOW] = dot(low, replicate).astype(bf16)
    nth_of_eight = (lax.broadcasted_iota(i32, (NOBS, LANES), 1) & (EIGHT - 1)).astype(f32)
    columns_ref[0:NOBS, TILES] = (sorted_columns[:, LANES : LANES + 1] - nth_of_eight).astype(bf16)
    columns_ref[NOBS:, 0 : 2 * WIDE] = jnp.zeros((WINDOW_ROWS, 2 * WIDE), bf16)
    columns_ref[NOBS:, TILES] = jnp.full((WINDOW_ROWS, LANES), NOWHERE, bf16)

    factors_high, factors_low = two_parts(factors)
    tile_there = jnp.where(own_row < 0, NOWHERE, own_row).astype(f32)
    tile_there = jnp.broadcast_to(tile_there, (GROUP, NOBS)).astype(bf16)
    sorted_rows = dot(jnp.concatenate([factors_high, factors_low, tile_there], axis=0), sort_back_ref[...])
    replicate = jnp.where(
        lax.broadcasted_iota(i32, (WIDE, GROUP), 0) >> 3 == lax.broadcasted_iota(i32, (WIDE, GROUP), 1), 1.0, 0.0
    ).astype(bf16)
    factors_ref[0:WIDE, 0:NOBS] = dot(replicate, sorted_rows[0:GROUP].astype(bf16)).astype(bf16)
    factors_ref[LOW, 0:NOBS] = dot(replicate, sorted_rows[GROUP : 2 * GROUP].astype(bf16)).astype(bf16)
    nth_of_eight = (lax.broadcasted_iota(i32, (16, NOBS), 0) & (EIGHT - 1)).astype(f32)
    factors_ref[TILE_ROWS, 0:NOBS] = (sorted_rows[2 * GROUP : 2 * GROUP + 16] - nth_of_eight).astype(bf16)
    factors_ref[0 : 2 * WIDE, NOBS:] = jnp.zeros((2 * WIDE, WINDOW_COLUMNS), bf16)
    factors_ref[TILE_ROWS, NOBS:] = jnp.full((16, WINDOW_COLUMNS), NOWHERE, bf16)


def observations(position, plan, facts, own, other):
    columns = struct((PADDED_ROWS, 2 * WIDE + LANES), bf16)
    factors = struct((2 * WIDE + 16, PADDED_COLUMNS), bf16)
    square = pltpu.VMEM((NOBS, NOBS), bf16)
    return pl.pallas_call(
        observation_kernel,
        out_shape=(columns, factors),
        in_specs=[SMEM, VMEM, VMEM, VMEM, VMEM],
        out_specs=(VMEM,) * 2,
        scratch_shapes=[
            pltpu.VMEM((MEMBERS, NOBS), f32),
            pltpu.VMEM((MEMBERS, NOBS), f32),
            square,
            pltpu.VMEM((128, NOBS), f32),
            pltpu.VMEM((NOBS, 128), f32),
            pltpu.VMEM((NOBS, 2 * GROUP), bf16),
            square,
            square,
            square,
            square,
        ],
        compiler_params=kernel_params(44),
        cost_estimate=pl.CostEstimate(flops=20 * 10**9, bytes_accessed=8 * 2**20, transcendentals=10**5),
        name="observations",
    )(position, plan, facts, own, other)


def for_windows(starts_ref, groups, size, align, visit):
    def start(g, i):
        return pl.multiple_of((starts_ref[g] & -align) + i * size, align)

    for g in groups:
        visit(g, start(g, 0))
    return functools.partial(for_rest, starts_ref, groups, size, align, visit, start)


def for_rest(starts_ref, groups, size, align, visit, start):
    for g in groups:
        count = (starts_ref[g + 1] - (starts_ref[g] & -align) + size - 1) // size

        def step(i, carry, g=g):
            visit(g, start(g, i))
            return carry

        lax.fori_loop(1, count, step, 0)


COVARIANCE_PIECES = 2
UPDATE_PIECES = 4


def piece_copies(pieces, from_ref, to_ref, sems):
    tiles = OWN_TILES // pieces
    return [
        pltpu.make_async_copy(
            from_ref.at[:, pl.ds(n * tiles, tiles), :], to_ref.at[:, pl.ds(n * tiles, tiles), :], sems.at[n]
        )
        for n in range(pieces)
    ]


def piece_groups(pieces, n):
    groups = GROUPS // pieces
    return range(n * groups, (n + 1) * groups)


def covariance_kernel(position_ref, starts_ref, block_ref, columns_in_ref, *refs):
    out_refs, (total_ref, held_ref, columns_ref, sems, columns_sems) = refs[: 2 * SUMS], refs[2 * SUMS :]
    usual = FIRST + WINDOW_ROWS
    columns_copy, more_copy = (
        pltpu.make_async_copy(columns_in_ref.at[rows], columns_ref.at[rows], columns_sems.at[n])
        for n, rows in enumerate((pl.ds(0, usual), pl.ds(usual, PADDED_ROWS - usual)))
    )
    columns_copy.start()
    arriving = piece_copies(COVARIANCE_PIECES, block_ref, held_ref, sems)
    for copy in arriving:
        copy.start()
    total_ref[...] = jnp.zeros_like(total_ref)
    zero = jnp.zeros((WINDOW_ROWS, LANES), bf16)

    def visit(g, start):
        rows = pl.ds(start, WINDOW_ROWS)
        found = columns_ref[rows, TILES] == jnp.full((WINDOW_ROWS, LANES), g * EIGHT, bf16)
        left = [
            jnp.concatenate(
                [
                    jnp.where(found, columns_ref[rows, part * WIDE + n * LANES : part * WIDE + (n + 1) * LANES], zero)
                    for n in range(WIDE // LANES)
                ],
                axis=1,
            )
            for part in range(2)
        ]
        right = held_ref[:, g * EIGHT : (g + 1) * EIGHT, :].reshape(WIDE, LANES)
        both = dot(jnp.concatenate(left, axis=0), jnp.concatenate(two_parts(right), axis=1))
        both = both[:WINDOW_ROWS] + both[WINDOW_ROWS:]
        total_ref[rows, :] += both[:, :LANES] + both[:, LANES:]

    columns_copy.wait()

    @pl.when(starts_ref[GROUPS] > FIRST)
    def _():
        more_copy.start()
        more_copy.wait()

    rest = []
    for n in range(COVARIANCE_PIECES):
        arriving[n].wait()
        rest.append(for_windows(starts_ref, piece_groups(COVARIANCE_PIECES, n), WINDOW_ROWS, 16, visit))
    for windows in rest:
        windows()
    for d in range(SUMS):
        to = (position_ref[1] + d) & (SUMS - 1)
        start = pl.multiple_of(to * FIRST_CHUNK, 16)
        out_refs[d][...] = total_ref[pl.ds(start, FIRST_CHUNK), :]
        start = pl.multiple_of(FIRST + to * REST_CHUNK, 16)
        out_refs[SUMS + d][...] = total_ref[pl.ds(start, REST_CHUNK), :]


def covariances(position, starts, block, columns):
    return pl.pallas_call(
        covariance_kernel,
        out_shape=(struct((FIRST_CHUNK, LANES)),) * SUMS + (struct((REST_CHUNK, LANES)),) * SUMS,
        in_specs=[SMEM, SMEM, ANY, ANY],
        out_specs=(VMEM,) * (2 * SUMS),
        scratch_shapes=[
            pltpu.VMEM((PADDED_ROWS, LANES), f32),
            pltpu.VMEM((GROUP, OWN_TILES, LANES), f32),
            pltpu.VMEM((PADDED_ROWS, 2 * WIDE + LANES), bf16),
            pltpu.SemaphoreType.DMA((COVARIANCE_PIECES,)),
            pltpu.SemaphoreType.DMA((2,)),
        ],
        compiler_params=kernel_params(60),
        cost_estimate=pl.CostEstimate(flops=3 * 10**9, bytes_accessed=7 * 2**20, transcendentals=0),
        name="covariances",
    )(position, starts, block, columns)


def update_kernel(position_ref, starts_ref, *refs):
    sums_refs = refs[: 2 * SUMS]
    block_ref, factors_ref, out_ref, right_ref, held_ref, in_sems, out_sems = refs[2 * SUMS :]
    arriving = piece_copies(UPDATE_PIECES, block_ref, held_ref, in_sems)
    leaving = piece_copies(UPDATE_PIECES, held_ref, out_ref, out_sems)
    for copy in arriving:
        copy.start()
    for d in range(SUMS):
        of = (position_ref[1] - d) & (SUMS - 1)
        start = pl.multiple_of(of * FIRST_CHUNK, 16)
        right_ref[pl.ds(start, FIRST_CHUNK), :] = jnp.concatenate(two_parts(sums_refs[d][...]), axis=1)
        start = pl.multiple_of(FIRST + of * REST_CHUNK, 16)
        right_ref[pl.ds(start, REST_CHUNK), :] = jnp.concatenate(two_parts(sums_refs[SUMS + d][...]), axis=1)
    right_ref[NOBS:, :] = jnp.zeros((WINDOW_COLUMNS, 2 * LANES), bf16)

    def visit(g, start):
        columns = pl.ds(start, WINDOW_COLUMNS)
        shape = (16, WINDOW_COLUMNS)
        found = factors_ref[TILE_ROWS, columns] == jnp.full(shape, g * EIGHT, bf16)
        found = jnp.where(found, jnp.ones(shape, bf16), jnp.zeros(shape, bf16))
        left = [
            (factors_ref[part, columns].reshape(WIDE // 16, 16, WINDOW_COLUMNS) * found[None]).reshape(WIDE, WINDOW_COLUMNS)
            for part in (slice(0, WIDE), LOW)
        ]
        both = dot(jnp.concatenate(left, axis=0), right_ref[columns, :])
        both = both[:WIDE] + both[WIDE:]
        held_ref[:, g * EIGHT : (g + 1) * EIGHT, :] += (both[:, :LANES] + both[:, LANES:]).reshape(GROUP, EIGHT, LANES)

    for n in range(UPDATE_PIECES):
        arriving[n].wait()
        for_windows(starts_ref, piece_groups(UPDATE_PIECES, n), WINDOW_COLUMNS, LANES, visit)()
        leaving[n].start()
    for copy in leaving:
        copy.wait()


def updated(position, starts, sums, block, factors):
    return pl.pallas_call(
        update_kernel,
        out_shape=struct((GROUP, OWN_TILES, LANES)),
        in_specs=[SMEM, SMEM] + [VMEM] * (2 * SUMS) + [ANY, VMEM],
        out_specs=ANY,
        scratch_shapes=[
            pltpu.VMEM((PADDED_COLUMNS, 2 * LANES), bf16),
            pltpu.VMEM((GROUP, OWN_TILES, LANES), f32),
            pltpu.SemaphoreType.DMA((UPDATE_PIECES,)),
            pltpu.SemaphoreType.DMA((UPDATE_PIECES,)),
        ],
        compiler_params=kernel_params(24),
        cost_estimate=pl.CostEstimate(flops=4 * 10**9, bytes_accessed=8 * 2**20, transcendentals=0),
        name="updated",
    )(position, starts, *sums, block, factors)


def exchange(value, axes=PEERS):
    return lax.all_to_all(value, axes, 0, 0, tiled=True)


def passed_along(value, by):
    return lax.ppermute(value, "h", [(i, (i + by) % SUMS) for i in range(SUMS)])


def summed(parts):
    total = parts[0]
    for by in range(1, SUMS):
        total = total + passed_along(parts[by], by)
    return (total, *(passed_along(total, by) for by in range(1, SUMS)))


def shards(state, locations, tile_mask, plan, obs_value, obs_error):
    residue = lax.axis_index(PEERS) // SLICES
    position = jnp.stack([residue, lax.axis_index("h"), lax.axis_index("c"), lax.axis_index(ALL)]).astype(i32)
    rows = state.reshape(ROWS, LANES)

    masks = own_masks(position, locations.reshape(-1, LANES), tile_mask)
    masks = exchange(masks.reshape(GROUP_CHIPS, 4, LANES), CHIPS).sum(axis=0)
    tiles = locations // TILE

    observed = own_columns(plan, locations, rows)
    mine = jnp.concatenate([observed, masks], axis=0)
    all_four = [mine] + [passed_along(mine, by) for by in range(1, SUMS)]
    payload = jnp.concatenate(
        [*(each[0:8] for each in all_four), sum(each[8:12] for each in all_four), jnp.zeros((4, LANES), f32)], axis=0
    )
    gathered = exchange(jnp.broadcast_to(payload[None], (GROUP_CHIPS, 40, LANES)), CHIPS)
    block, gathered = lax.optimization_barrier((spread_out(rows), gathered))
    other = lax.ppermute(gathered, "c", [(0, 1), (1, 0)])
    block, other = lax.optimization_barrier((block, other))
    block = exchange(block)

    facts = jnp.concatenate(
        [tiles.astype(f32)[None], obs_value[None], obs_error[None], jnp.zeros((5, NOBS), f32)], axis=0
    )
    columns, factors = observations(
        position, plan[None], facts, gathered.reshape(-1, LANES), other.reshape(-1, LANES)
    )
    nth_own = (residue - tiles + RADIUS) & (RESIDUES - 1)
    own_tile = jnp.where(nth_own < WINDOW, ((tiles - RADIUS + nth_own) & (NTILES - 1)) // RESIDUES, OWN_TILES)
    starts = jnp.sum(own_tile[None, :] < EIGHT * jnp.arange(GROUPS + 1, dtype=i32)[:, None], axis=1, dtype=i32)
    nth_all = (jnp.arange(RESIDUES, dtype=i32)[:, None] - tiles[None, :] + RADIUS) & (RESIDUES - 1)
    most = jnp.max(jnp.sum(nth_all < WINDOW, axis=1, dtype=i32))

    parts = covariances(position, starts, block, columns)
    rest = lax.cond(most > FIRST, summed, lambda parts: parts, parts[SUMS:])
    sums = summed(parts[:SUMS]) + tuple(rest)
    block = exchange(updated(position, starts, sums, block, factors))
    return collect(block).reshape(state.shape)


def solution(mesh):
    fine = Mesh(mesh.devices.reshape(4, 4, 2, 2, 4), ALL)
    placed = (P(ALL, None), P(), P(ALL, None), P(), P(), P())
    return jax.shard_map(shards, mesh=fine, in_specs=placed, out_specs=P(ALL, None), check_vma=False)
```

```python
import functools

import jax
import jax.numpy as jnp
from jax import lax
from jax.experimental import pallas as pl
from jax.experimental.pallas import tpu as pltpu
from jax.sharding import Mesh, PartitionSpec as P

MEMBERS = 256
TILE = 512
NTILES = 2048
RADIUS = 4
WINDOW = 2 * RADIUS + 1
BATCH_OBS = 256
BATCHES = 4
NOBS = BATCH_OBS * BATCHES

ALL = ("y", "h", "l", "c", "x")
PEERS = ("c", "y", "l", "x")
CHIPS = ("y", "l", "x")
GROUP = 64
CORES = 2
GROUP_CHIPS = GROUP // CORES
SUMS = 4
RESIDUES = 16
SLICES = 4
LANES = 128
OWN_TILES = NTILES // RESIDUES
ROWS = NTILES * TILE // LANES
EIGHT = 8
WIDE = EIGHT * GROUP
GROUPS = OWN_TILES // EIGHT
WINDOW_ROWS = 128
WINDOW_COLUMNS = 256
PADDED_ROWS = NOBS + WINDOW_ROWS
PADDED_COLUMNS = NOBS + WINDOW_COLUMNS
LOW = slice(WIDE, 2 * WIDE)
TILES = slice(2 * WIDE, 2 * WIDE + LANES)
TILE_ROWS = slice(2 * WIDE, 2 * WIDE + 16)
NOWHERE = -512
BLOCK_TILES = 16
FIRST = 640
FIRST_CHUNK = FIRST // SUMS
REST_CHUNK = (NOBS - FIRST) // SUMS

epsilon = 1e-06
f32 = jnp.float32
bf16 = jnp.bfloat16
i32 = jnp.int32

VMEM = pl.BlockSpec(memory_space=pltpu.VMEM)
SMEM = pl.BlockSpec(memory_space=pltpu.SMEM)
ANY = pl.BlockSpec(memory_space=pl.ANY)


def kernel_params(mib):
    return pltpu.CompilerParams(vmem_limit_bytes=mib * 1024 * 1024)


def struct(shape, dtype=f32):
    return jax.ShapeDtypeStruct(shape, dtype)


def two_parts(value):
    high = value.astype(bf16)
    return high, (value - high.astype(f32)).astype(bf16)


def three_parts(value):
    high = value.astype(bf16)
    rest = value - high.astype(f32)
    middle = rest.astype(bf16)
    return high, middle, (rest - middle.astype(f32)).astype(bf16)


def dot(a, b):
    return lax.dot_general(a, b, (((1,), (0,)), ((), ())), preferred_element_type=f32)


def dot_parts(a_high, a_low, b_high, b_low):
    return dot(a_high, b_high) + dot(a_high, b_low) + dot(a_low, b_high)


def accurate_dot(a, b):
    return dot_parts(*two_parts(a), *two_parts(b))


def masks_kernel(position_ref, locations_ref, tile_mask_ref, out_ref):
    tiles_here = tile_mask_ref.shape[0]
    first = position_ref[3] * tiles_here
    per_row = NOBS // LANES
    relative = (locations_ref[...] >> 9) - RADIUS - first
    masks = [
        jnp.concatenate([tile_mask_ref[i : i + 1, g * LANES : (g + 1) * LANES] for g in range(per_row)], axis=0)
        for i in range(tiles_here)
    ]
    for n in range(16):
        local = (relative + n) & (NTILES - 1)
        found = jnp.zeros((per_row, LANES), i32)
        if n < WINDOW:
            for i in range(tiles_here):
                found = jnp.where(local == i, masks[i], found)
        out_ref[n * per_row : (n + 1) * per_row, :] = found.astype(f32)


def own_masks(position, locations, tile_mask):
    return pl.pallas_call(
        masks_kernel,
        out_shape=struct((16 * NOBS // LANES, LANES)),
        in_specs=[SMEM, VMEM, VMEM],
        out_specs=VMEM,
        compiler_params=kernel_params(4),
        cost_estimate=pl.CostEstimate(flops=10**5, bytes_accessed=10**5, transcendentals=0),
        name="own_masks",
    )(position, locations, tile_mask)


def columns_kernel(plan_ref, locations_ref, state_ref, out_ref, picked_ref):
    lane = lax.broadcasted_iota(i32, (1, LANES), 1)

    def step(i, carry):
        base = pl.multiple_of(i * 8, 8)
        found = []
        for u in range(8):
            where = locations_ref[plan_ref[base + u]]
            row = state_ref[pl.ds(where >> 7, 1), :]
            found.append(jnp.where(lane == (where & (LANES - 1)), row, 0.0))
        picked_ref[pl.ds(base, 8), :] = jnp.concatenate(found, axis=0)
        return carry

    lax.fori_loop(0, NOBS // 8, step, 0, unroll=2)
    ones = jnp.ones((16, LANES), bf16)
    total = jnp.zeros((16, NOBS), f32)
    for part in three_parts(picked_ref[...]):
        total = total + lax.dot_general(ones, part, (((1,), (1,)), ((), ())), preferred_element_type=f32)
    for g in range(NOBS // LANES):
        out_ref[pl.ds(g, 1), :] = total[0:1, g * LANES : (g + 1) * LANES]


def own_columns(plan, locations, rows):
    return pl.pallas_call(
        columns_kernel,
        out_shape=struct((NOBS // LANES, LANES)),
        in_specs=[SMEM, SMEM, VMEM],
        out_specs=VMEM,
        scratch_shapes=[pltpu.VMEM((NOBS, LANES), f32)],
        compiler_params=kernel_params(24),
        cost_estimate=pl.CostEstimate(flops=10**6, bytes_accessed=8 * 2**20, transcendentals=0),
        name="own_columns",
    )(plan, locations, rows)


def spread_kernel(state_ref, out_ref):
    for d in range(GROUP):
        out_ref[d] = state_ref[pl.ds(d, BLOCK_TILES, stride=GROUP), :]


def spread_out(rows):
    return pl.pallas_call(
        spread_kernel,
        grid=(OWN_TILES // BLOCK_TILES,),
        out_shape=struct((GROUP, OWN_TILES, LANES)),
        in_specs=[pl.BlockSpec((GROUP * BLOCK_TILES, LANES), lambda i: (i, 0))],
        out_specs=pl.BlockSpec((GROUP, BLOCK_TILES, LANES), lambda i: (0, i, 0)),
        compiler_params=kernel_params(16),
        cost_estimate=pl.CostEstimate(flops=10**6, bytes_accessed=8 * 2**20, transcendentals=0),
        name="spread_out",
    )(rows)


PIECES = 8


def collect_kernel(in_ref, state_ref, held_ref, in_sems, out_sems):
    devices = GROUP // PIECES
    arriving = [
        pltpu.make_async_copy(
            in_ref.at[pl.ds(n * devices, devices)], held_ref.at[pl.ds(n * devices, devices)], in_sems.at[n]
        )
        for n in range(PIECES)
    ]
    leaving = [
        pltpu.make_async_copy(held_ref.at[d], state_ref.at[:, d, :], out_sems.at[d]) for d in range(GROUP)
    ]
    for copy in arriving:
        copy.start()
    for n in range(PIECES):
        arriving[n].wait()
        for copy in leaving[n * devices : (n + 1) * devices]:
            copy.start()
    for copy in leaving:
        copy.wait()


def collect(blocks):
    return pl.pallas_call(
        collect_kernel,
        out_shape=struct((OWN_TILES, GROUP, LANES)),
        in_specs=[ANY],
        out_specs=ANY,
        scratch_shapes=[
            pltpu.VMEM((GROUP, OWN_TILES, LANES), f32),
            pltpu.SemaphoreType.DMA((PIECES,)),
            pltpu.SemaphoreType.DMA((GROUP,)),
        ],
        compiler_params=kernel_params(60),
        cost_estimate=pl.CostEstimate(flops=10**6, bytes_accessed=8 * 2**20, transcendentals=0),
        name="collect",
    )(blocks)


def observation_kernel(
    position_ref, plan_ref, facts_ref, own_ref, other_ref,
    columns_ref, factors_ref,
    ensemble_ref, increments_ref, one_hot_ref, facts_scratch, in_columns_ref,
    turned_ref, links_high_ref, links_low_ref, sort_ref, sort_back_ref,
):
    core = position_ref[2]
    for d in range(SUMS):
        for gathered_ref, start in ((own_ref, core), (other_ref, 1 - core)):
            rows = pl.ds(pl.multiple_of(d * GROUP + start * GROUP_CHIPS, GROUP_CHIPS), GROUP_CHIPS)
            for g in range(NOBS // LANES):
                ensemble_ref[rows, g * LANES : (g + 1) * LANES] = gathered_ref[
                    pl.ds(d * 8 + g, GROUP_CHIPS, stride=40), :
                ]
    for g in range(NOBS // LANES):
        rows = pl.ds((g // 4) * 40 + 32 + g % 4, 16, stride=80)
        facts_scratch[0:16, g * LANES : (g + 1) * LANES] = own_ref[rows, :] + other_ref[rows, :]
    facts_scratch[16:24, :] = facts_ref[...]
    facts_scratch[24:128, :] = jnp.zeros((104, NOBS), f32)
    source = lax.broadcasted_iota(i32, (NOBS, NOBS), 0)
    one_hot_ref[...] = jnp.where(source == plan_ref[...], 1.0, 0.0).astype(bf16)
    high, middle, low = three_parts(facts_scratch[0:32, :])
    ordered = dot(high, one_hot_ref[...]) + dot(middle, one_hot_ref[...]) + dot(low, one_hot_ref[...])
    facts_scratch[0:32, :] = ordered
    for g in range(NOBS // LANES):
        in_columns_ref[g * LANES : (g + 1) * LANES, :] = facts_scratch[:, g * LANES : (g + 1) * LANES].T

    residue = position_ref[0]
    tile_row = facts_scratch[16:17, :].astype(i32)
    tile_column = in_columns_ref[:, 16:17].astype(i32)
    nth_row = (residue - tile_row + RADIUS) & (RESIDUES - 1)
    nth_column = (residue - tile_column + RADIUS) & (RESIDUES - 1)
    own_row = ((tile_row - RADIUS + nth_row) & (NTILES - 1)) >> 4
    own_column = ((tile_column - RADIUS + nth_column) & (NTILES - 1)) >> 4
    own_row = jnp.where(nth_row < WINDOW, own_row, -1)
    own_column = jnp.where(nth_column < WINDOW, own_column, -2)
    mask_column = jnp.zeros((NOBS, 1), f32)
    for n in range(WINDOW):
        mask_column = mask_column + jnp.where(nth_column == n, in_columns_ref[:, n : n + 1], 0.0)

    mask_row = jnp.zeros((1, NOBS), f32)
    for n in range(WINDOW):
        mask_row = mask_row + jnp.where(nth_row == n, facts_scratch[n : n + 1, :], 0.0)

    key_row = jnp.where(own_row < 0, OWN_TILES, own_row) * NOBS + lax.broadcasted_iota(i32, (1, NOBS), 1)
    key_column = jnp.where(own_column < 0, OWN_TILES, own_column) * NOBS + lax.broadcasted_iota(i32, (NOBS, 1), 0)
    rank_row = jnp.sum(jnp.where(key_column < key_row, 1.0, 0.0), axis=0, keepdims=True).astype(i32)
    rank_column = jnp.sum(jnp.where(key_row < key_column, 1.0, 0.0), axis=1, keepdims=True).astype(i32)
    sort_ref[...] = jnp.where(source == rank_row, 1.0, 0.0).astype(bf16)
    to = lax.broadcasted_iota(i32, (NOBS, NOBS), 1)
    sort_back_ref[...] = jnp.where(to == rank_column, 1.0, 0.0).astype(bf16)

    gain_rows = []
    for b in range(BATCHES):
        here = slice(b * BATCH_OBS, (b + 1) * BATCH_OBS)
        prior = ensemble_ref[:, here]
        average = jnp.sum(prior, axis=0, keepdims=True) / MEMBERS
        anomaly = prior - average
        spread = jnp.sum(anomaly * anomaly, axis=0, keepdims=True) / (MEMBERS - 1) + epsilon
        value = facts_scratch[17:18, here]
        error = facts_scratch[18:19, here]
        shrink = jnp.sqrt(error / (spread + error))
        moved = (average * error + value * spread) / (spread + error)
        increments = (shrink - 1.0) * anomaly + (moved - average)
        increments_ref[:, here] = increments
        turned = anomaly.T
        spread_column = jnp.sum(turned * turned, axis=1, keepdims=True) / (MEMBERS - 1) + epsilon
        gain_column = 1.0 / ((MEMBERS - 1) * spread_column)
        turned_high, turned_low = two_parts(turned)
        turned_ref[here, :] = jnp.concatenate([turned_high[:, 0:GROUP], turned_low[:, 0:GROUP]], axis=1)
        gain_rows.append(1.0 / ((MEMBERS - 1) * spread))
        weight = mask_column[here] * gain_column
        if b > 0:
            before = b * BATCH_OBS
            links = accurate_dot(turned, increments_ref[:, 0:before])
            links = jnp.where(own_column[here] == own_row[:, 0:before], links * weight, 0.0)
            links_high, links_low = two_parts(links)
            links_high_ref[here, 0:before] = links_high
            links_low_ref[here, 0:before] = links_low
        if b < BATCHES - 1:
            after = slice((b + 1) * BATCH_OBS, NOBS)
            later = ensemble_ref[:, after]
            covariance = dot_parts(turned_high, turned_low, *two_parts(later))
            apart = (tile_row[:, after] - tile_column[here] + RADIUS) & (NTILES - 1)
            masks = jnp.zeros(apart.shape, f32)
            for n in range(WINDOW):
                masks = jnp.where(apart == n, in_columns_ref[here, n : n + 1], masks)
            ensemble_ref[:, after] = later + accurate_dot(increments, covariance * masks * gain_column)

    for b in reversed(range(BATCHES - 1)):
        here = slice(b * BATCH_OBS, (b + 1) * BATCH_OBS)
        after = slice((b + 1) * BATCH_OBS, NOBS)
        increments_ref[0:GROUP, here] += dot_parts(
            *two_parts(increments_ref[0:GROUP, after]), links_high_ref[after, here], links_low_ref[after, here]
        )
    factors = increments_ref[0:GROUP, :] * (mask_row * jnp.concatenate(gain_rows, axis=1))

    tile_here = jnp.where(own_column < 0, NOWHERE, own_column).astype(f32)
    tile_here = jnp.broadcast_to(tile_here, (NOBS, LANES)).astype(bf16)
    sorted_columns = dot(sort_ref[...], jnp.concatenate([turned_ref[...], tile_here], axis=1))
    high = sorted_columns[:, 0:GROUP].astype(bf16)
    low = sorted_columns[:, GROUP : 2 * GROUP].astype(bf16)
    replicate = jnp.where(
        lax.broadcasted_iota(i32, (GROUP, WIDE), 1) >> 3 == lax.broadcasted_iota(i32, (GROUP, WIDE), 0), 1.0, 0.0
    ).astype(bf16)
    columns_ref[0:NOBS, 0:WIDE] = dot(high, replicate).astype(bf16)
    columns_ref[0:NOBS, LOW] = dot(low, replicate).astype(bf16)
    nth_of_eight = (lax.broadcasted_iota(i32, (NOBS, LANES), 1) & (EIGHT - 1)).astype(f32)
    columns_ref[0:NOBS, TILES] = (sorted_columns[:, LANES : LANES + 1] - nth_of_eight).astype(bf16)
    columns_ref[NOBS:, 0 : 2 * WIDE] = jnp.zeros((WINDOW_ROWS, 2 * WIDE), bf16)
    columns_ref[NOBS:, TILES] = jnp.full((WINDOW_ROWS, LANES), NOWHERE, bf16)

    factors_high, factors_low = two_parts(factors)
    tile_there = jnp.where(own_row < 0, NOWHERE, own_row).astype(f32)
    tile_there = jnp.broadcast_to(tile_there, (GROUP, NOBS)).astype(bf16)
    sorted_rows = dot(jnp.concatenate([factors_high, factors_low, tile_there], axis=0), sort_back_ref[...])
    replicate = jnp.where(
        lax.broadcasted_iota(i32, (WIDE, GROUP), 0) >> 3 == lax.broadcasted_iota(i32, (WIDE, GROUP), 1), 1.0, 0.0
    ).astype(bf16)
    factors_ref[0:WIDE, 0:NOBS] = dot(replicate, sorted_rows[0:GROUP].astype(bf16)).astype(bf16)
    factors_ref[LOW, 0:NOBS] = dot(replicate, sorted_rows[GROUP : 2 * GROUP].astype(bf16)).astype(bf16)
    nth_of_eight = (lax.broadcasted_iota(i32, (16, NOBS), 0) & (EIGHT - 1)).astype(f32)
    factors_ref[TILE_ROWS, 0:NOBS] = (sorted_rows[2 * GROUP : 2 * GROUP + 16] - nth_of_eight).astype(bf16)
    factors_ref[0 : 2 * WIDE, NOBS:] = jnp.zeros((2 * WIDE, WINDOW_COLUMNS), bf16)
    factors_ref[TILE_ROWS, NOBS:] = jnp.full((16, WINDOW_COLUMNS), NOWHERE, bf16)


def observations(position, plan, facts, own, other):
    columns = struct((PADDED_ROWS, 2 * WIDE + LANES), bf16)
    factors = struct((2 * WIDE + 16, PADDED_COLUMNS), bf16)
    square = pltpu.VMEM((NOBS, NOBS), bf16)
    return pl.pallas_call(
        observation_kernel,
        out_shape=(columns, factors),
        in_specs=[SMEM, VMEM, VMEM, VMEM, VMEM],
        out_specs=(VMEM,) * 2,
        scratch_shapes=[
            pltpu.VMEM((MEMBERS, NOBS), f32),
            pltpu.VMEM((MEMBERS, NOBS), f32),
            square,
            pltpu.VMEM((128, NOBS), f32),
            pltpu.VMEM((NOBS, 128), f32),
            pltpu.VMEM((NOBS, 2 * GROUP), bf16),
            square,
            square,
            square,
            square,
        ],
        compiler_params=kernel_params(44),
        cost_estimate=pl.CostEstimate(flops=20 * 10**9, bytes_accessed=8 * 2**20, transcendentals=10**5),
        name="observations",
    )(position, plan, facts, own, other)


def for_windows(starts_ref, groups, size, align, visit):
    def start(g, i):
        return pl.multiple_of((starts_ref[g] & -align) + i * size, align)

    for g in groups:
        visit(g, start(g, 0))
    return functools.partial(for_rest, starts_ref, groups, size, align, visit, start)


def for_rest(starts_ref, groups, size, align, visit, start):
    for g in groups:
        count = (starts_ref[g + 1] - (starts_ref[g] & -align) + size - 1) // size

        def step(i, carry, g=g):
            visit(g, start(g, i))
            return carry

        lax.fori_loop(1, count, step, 0)


COVARIANCE_PIECES = 2
UPDATE_PIECES = 4


def piece_copies(pieces, from_ref, to_ref, sems):
    tiles = OWN_TILES // pieces
    return [
        pltpu.make_async_copy(
            from_ref.at[:, pl.ds(n * tiles, tiles), :], to_ref.at[:, pl.ds(n * tiles, tiles), :], sems.at[n]
        )
        for n in range(pieces)
    ]


def piece_groups(pieces, n):
    groups = GROUPS // pieces
    return range(n * groups, (n + 1) * groups)


def covariance_kernel(position_ref, starts_ref, block_ref, columns_in_ref, *refs):
    out_refs, (total_ref, held_ref, columns_ref, sems, columns_sems) = refs[: 2 * SUMS], refs[2 * SUMS :]
    usual = FIRST + WINDOW_ROWS
    columns_copy, more_copy = (
        pltpu.make_async_copy(columns_in_ref.at[rows], columns_ref.at[rows], columns_sems.at[n])
        for n, rows in enumerate((pl.ds(0, usual), pl.ds(usual, PADDED_ROWS - usual)))
    )
    columns_copy.start()
    arriving = piece_copies(COVARIANCE_PIECES, block_ref, held_ref, sems)
    for copy in arriving:
        copy.start()
    total_ref[...] = jnp.zeros_like(total_ref)
    zero = jnp.zeros((WINDOW_ROWS, LANES), bf16)

    def visit(g, start):
        rows = pl.ds(start, WINDOW_ROWS)
        found = columns_ref[rows, TILES] == jnp.full((WINDOW_ROWS, LANES), g * EIGHT, bf16)
        left = [
            jnp.concatenate(
                [
                    jnp.where(found, columns_ref[rows, part * WIDE + n * LANES : part * WIDE + (n + 1) * LANES], zero)
                    for n in range(WIDE // LANES)
                ],
                axis=1,
            )
            for part in range(2)
        ]
        right = held_ref[:, g * EIGHT : (g + 1) * EIGHT, :].reshape(WIDE, LANES)
        both = dot(jnp.concatenate(left, axis=0), jnp.concatenate(two_parts(right), axis=1))
        both = both[:WINDOW_ROWS] + both[WINDOW_ROWS:]
        total_ref[rows, :] += both[:, :LANES] + both[:, LANES:]

    columns_copy.wait()

    @pl.when(starts_ref[GROUPS] > FIRST)
    def _():
        more_copy.start()
        more_copy.wait()

    rest = []
    for n in range(COVARIANCE_PIECES):
        arriving[n].wait()
        rest.append(for_windows(starts_ref, piece_groups(COVARIANCE_PIECES, n), WINDOW_ROWS, 16, visit))
    for windows in rest:
        windows()
    for d in range(SUMS):
        to = position_ref[1] ^ d
        start = pl.multiple_of(to * FIRST_CHUNK, 16)
        out_refs[d][...] = total_ref[pl.ds(start, FIRST_CHUNK), :]
        start = pl.multiple_of(FIRST + to * REST_CHUNK, 16)
        out_refs[SUMS + d][...] = total_ref[pl.ds(start, REST_CHUNK), :]


def covariances(position, starts, block, columns):
    return pl.pallas_call(
        covariance_kernel,
        out_shape=(struct((FIRST_CHUNK, LANES)),) * SUMS + (struct((REST_CHUNK, LANES)),) * SUMS,
        in_specs=[SMEM, SMEM, ANY, ANY],
        out_specs=(VMEM,) * (2 * SUMS),
        scratch_shapes=[
            pltpu.VMEM((PADDED_ROWS, LANES), f32),
            pltpu.VMEM((GROUP, OWN_TILES, LANES), f32),
            pltpu.VMEM((PADDED_ROWS, 2 * WIDE + LANES), bf16),
            pltpu.SemaphoreType.DMA((COVARIANCE_PIECES,)),
            pltpu.SemaphoreType.DMA((2,)),
        ],
        compiler_params=kernel_params(60),
        cost_estimate=pl.CostEstimate(flops=3 * 10**9, bytes_accessed=7 * 2**20, transcendentals=0),
        name="covariances",
    )(position, starts, block, columns)


def update_kernel(position_ref, starts_ref, *refs):
    sums_refs = refs[: 2 * SUMS]
    block_ref, factors_ref, out_ref, right_ref, held_ref, in_sems, out_sems = refs[2 * SUMS :]
    arriving = piece_copies(UPDATE_PIECES, block_ref, held_ref, in_sems)
    leaving = piece_copies(UPDATE_PIECES, held_ref, out_ref, out_sems)
    for copy in arriving:
        copy.start()
    for d in range(SUMS):
        of = position_ref[1] ^ d
        start = pl.multiple_of(of * FIRST_CHUNK, 16)
        right_ref[pl.ds(start, FIRST_CHUNK), :] = jnp.concatenate(two_parts(sums_refs[d][...]), axis=1)
        start = pl.multiple_of(FIRST + of * REST_CHUNK, 16)
        right_ref[pl.ds(start, REST_CHUNK), :] = jnp.concatenate(two_parts(sums_refs[SUMS + d][...]), axis=1)
    right_ref[NOBS:, :] = jnp.zeros((WINDOW_COLUMNS, 2 * LANES), bf16)

    def visit(g, start):
        columns = pl.ds(start, WINDOW_COLUMNS)
        shape = (16, WINDOW_COLUMNS)
        found = factors_ref[TILE_ROWS, columns] == jnp.full(shape, g * EIGHT, bf16)
        found = jnp.where(found, jnp.ones(shape, bf16), jnp.zeros(shape, bf16))
        left = [
            (factors_ref[part, columns].reshape(WIDE // 16, 16, WINDOW_COLUMNS) * found[None]).reshape(WIDE, WINDOW_COLUMNS)
            for part in (slice(0, WIDE), LOW)
        ]
        both = dot(jnp.concatenate(left, axis=0), right_ref[columns, :])
        both = both[:WIDE] + both[WIDE:]
        held_ref[:, g * EIGHT : (g + 1) * EIGHT, :] += (both[:, :LANES] + both[:, LANES:]).reshape(GROUP, EIGHT, LANES)

    for n in range(UPDATE_PIECES):
        arriving[n].wait()
        for_windows(starts_ref, piece_groups(UPDATE_PIECES, n), WINDOW_COLUMNS, LANES, visit)()
        leaving[n].start()
    for copy in leaving:
        copy.wait()


def updated(position, starts, sums, block, factors):
    return pl.pallas_call(
        update_kernel,
        out_shape=struct((GROUP, OWN_TILES, LANES)),
        in_specs=[SMEM, SMEM] + [VMEM] * (2 * SUMS) + [ANY, VMEM],
        out_specs=ANY,
        scratch_shapes=[
            pltpu.VMEM((PADDED_COLUMNS, 2 * LANES), bf16),
            pltpu.VMEM((GROUP, OWN_TILES, LANES), f32),
            pltpu.SemaphoreType.DMA((UPDATE_PIECES,)),
            pltpu.SemaphoreType.DMA((UPDATE_PIECES,)),
        ],
        compiler_params=kernel_params(24),
        cost_estimate=pl.CostEstimate(flops=4 * 10**9, bytes_accessed=8 * 2**20, transcendentals=0),
        name="updated",
    )(position, starts, *sums, block, factors)


def exchange(value, axes=PEERS):
    return lax.all_to_all(value, axes, 0, 0, tiled=True)


def swapped(value, by):
    return lax.ppermute(value, "h", [(i, i ^ by) for i in range(SUMS)])


def summed(parts):
    total = parts[0]
    for by in range(1, SUMS):
        total = total + swapped(parts[by], by)
    return (total, *(swapped(total, by) for by in range(1, SUMS)))


def shards(state, locations, tile_mask, plan, obs_value, obs_error):
    residue = lax.axis_index(PEERS) // SLICES
    position = jnp.stack([residue, lax.axis_index("h"), lax.axis_index("c"), lax.axis_index(ALL)]).astype(i32)
    rows = state.reshape(ROWS, LANES)

    masks = own_masks(position, locations.reshape(-1, LANES), tile_mask)
    masks = exchange(masks.reshape(GROUP_CHIPS, 4, LANES), CHIPS).sum(axis=0)
    tiles = locations // TILE

    observed = own_columns(plan, locations, rows)
    mine = jnp.concatenate([observed, masks], axis=0)
    all_four = [mine] + [swapped(mine, by) for by in range(1, SUMS)]
    payload = jnp.concatenate(
        [*(each[0:8] for each in all_four), sum(each[8:12] for each in all_four), jnp.zeros((4, LANES), f32)], axis=0
    )
    gathered = exchange(jnp.broadcast_to(payload[None], (GROUP_CHIPS, 40, LANES)), CHIPS)
    block, gathered = lax.optimization_barrier((spread_out(rows), gathered))
    other = lax.ppermute(gathered, "c", [(0, 1), (1, 0)])
    block, other = lax.optimization_barrier((block, other))
    block = exchange(block)

    facts = jnp.concatenate(
        [tiles.astype(f32)[None], obs_value[None], obs_error[None], jnp.zeros((5, NOBS), f32)], axis=0
    )
    columns, factors = observations(
        position, plan[None], facts, gathered.reshape(-1, LANES), other.reshape(-1, LANES)
    )
    nth_own = (residue - tiles + RADIUS) & (RESIDUES - 1)
    own_tile = jnp.where(nth_own < WINDOW, ((tiles - RADIUS + nth_own) & (NTILES - 1)) // RESIDUES, OWN_TILES)
    starts = jnp.sum(own_tile[None, :] < EIGHT * jnp.arange(GROUPS + 1, dtype=i32)[:, None], axis=1, dtype=i32)
    nth_all = (jnp.arange(RESIDUES, dtype=i32)[:, None] - tiles[None, :] + RADIUS) & (RESIDUES - 1)
    most = jnp.max(jnp.sum(nth_all < WINDOW, axis=1, dtype=i32))

    parts = covariances(position, starts, block, columns)
    rest = lax.cond(most > FIRST, summed, lambda parts: parts, parts[SUMS:])
    sums = summed(parts[:SUMS]) + tuple(rest)
    block = exchange(updated(position, starts, sums, block, factors))
    return collect(block).reshape(state.shape)


def solution(mesh):
    fine = Mesh(mesh.devices.reshape(4, 4, 2, 2, 4), ALL)
    placed = (P(ALL, None), P(), P(ALL, None), P(), P(), P())
    return jax.shard_map(shards, mesh=fine, in_specs=placed, out_specs=P(ALL, None), check_vma=False)
```

```python
import functools

import jax
import jax.numpy as jnp
from jax import lax
from jax.experimental import pallas as pl
from jax.experimental.pallas import tpu as pltpu
from jax.sharding import Mesh, PartitionSpec as P

MEMBERS = 256
TILE = 512
NTILES = 2048
RADIUS = 4
WINDOW = 2 * RADIUS + 1
BATCH_OBS = 256
BATCHES = 4
NOBS = BATCH_OBS * BATCHES

ALL = ("y", "h", "l", "c", "x")
PEERS = ("c", "y", "l", "x")
CHIPS = ("y", "l", "x")
GROUP = 64
CORES = 2
GROUP_CHIPS = GROUP // CORES
SUMS = 4
RESIDUES = 16
SLICES = 4
LANES = 128
OWN_TILES = NTILES // RESIDUES
EIGHT = 8
WIDE = EIGHT * GROUP
GROUPS = OWN_TILES // EIGHT
WINDOW_ROWS = 128
WINDOW_COLUMNS = 256
PADDED_ROWS = NOBS + WINDOW_ROWS
PADDED_COLUMNS = NOBS + WINDOW_COLUMNS
LOW = slice(WIDE, 2 * WIDE)
TILES = slice(2 * WIDE, 2 * WIDE + LANES)
TILE_ROWS = slice(2 * WIDE, 2 * WIDE + 16)
NOWHERE = -512
FIRST = 640
FIRST_CHUNK = FIRST // SUMS
REST_CHUNK = (NOBS - FIRST) // SUMS

epsilon = 1e-06
f32 = jnp.float32
bf16 = jnp.bfloat16
i32 = jnp.int32

VMEM = pl.BlockSpec(memory_space=pltpu.VMEM)
SMEM = pl.BlockSpec(memory_space=pltpu.SMEM)
ANY = pl.BlockSpec(memory_space=pl.ANY)


def kernel_params(mib):
    return pltpu.CompilerParams(vmem_limit_bytes=mib * 1024 * 1024)


def struct(shape, dtype=f32):
    return jax.ShapeDtypeStruct(shape, dtype)


def two_parts(value):
    high = value.astype(bf16)
    return high, (value - high.astype(f32)).astype(bf16)


def three_parts(value):
    high = value.astype(bf16)
    rest = value - high.astype(f32)
    middle = rest.astype(bf16)
    return high, middle, (rest - middle.astype(f32)).astype(bf16)


def dot(a, b):
    return lax.dot_general(a, b, (((1,), (0,)), ((), ())), preferred_element_type=f32)


def dot_parts(a_high, a_low, b_high, b_low):
    return dot(a_high, b_high) + dot(a_high, b_low) + dot(a_low, b_high)


def accurate_dot(a, b):
    return dot_parts(*two_parts(a), *two_parts(b))


def masks_kernel(position_ref, locations_ref, tile_mask_ref, out_ref):
    tiles_here = tile_mask_ref.shape[0]
    first = position_ref[3] * tiles_here
    per_row = NOBS // LANES
    relative = (locations_ref[...] >> 9) - RADIUS - first
    masks = [
        jnp.concatenate([tile_mask_ref[i : i + 1, g * LANES : (g + 1) * LANES] for g in range(per_row)], axis=0)
        for i in range(tiles_here)
    ]
    for n in range(16):
        local = (relative + n) & (NTILES - 1)
        found = jnp.zeros((per_row, LANES), i32)
        if n < WINDOW:
            for i in range(tiles_here):
                found = jnp.where(local == i, masks[i], found)
        out_ref[n * per_row : (n + 1) * per_row, :] = found.astype(f32)


def own_masks(position, locations, tile_mask):
    return pl.pallas_call(
        masks_kernel,
        out_shape=struct((16 * NOBS // LANES, LANES)),
        in_specs=[SMEM, VMEM, VMEM],
        out_specs=VMEM,
        compiler_params=kernel_params(4),
        cost_estimate=pl.CostEstimate(flops=10**5, bytes_accessed=10**5, transcendentals=0),
        name="own_masks",
    )(position, locations, tile_mask)


PIECES = 8


def columns_kernel(
    plan_ref, locations_ref, state_ref, out_ref, spread_ref, held_ref, picked_ref, in_sems, out_sems
):
    tiles = OWN_TILES // PIECES
    arriving = [
        pltpu.make_async_copy(
            state_ref.at[pl.ds(n * tiles, tiles)], held_ref.at[pl.ds(n * tiles, tiles)], in_sems.at[n]
        )
        for n in range(PIECES)
    ]
    leaving = [pltpu.make_async_copy(held_ref.at[:, d, :], spread_ref.at[d], out_sems.at[d]) for d in range(GROUP)]
    for copy in arriving:
        copy.start()
    for copy in arriving:
        copy.wait()
    for copy in leaving:
        copy.start()
    lane = lax.broadcasted_iota(i32, (1, LANES), 1)

    def step(i, carry):
        base = pl.multiple_of(i * 8, 8)
        found = []
        for u in range(8):
            where = locations_ref[plan_ref[base + u]]
            row = held_ref[where >> 13, pl.ds((where >> 7) & (GROUP - 1), 1), :]
            found.append(jnp.where(lane == (where & (LANES - 1)), row, 0.0))
        picked_ref[pl.ds(base, 8), :] = jnp.concatenate(found, axis=0)
        return carry

    lax.fori_loop(0, NOBS // 8, step, 0, unroll=2)
    ones = jnp.ones((16, LANES), bf16)
    total = jnp.zeros((16, NOBS), f32)
    for part in three_parts(picked_ref[...]):
        total = total + lax.dot_general(ones, part, (((1,), (1,)), ((), ())), preferred_element_type=f32)
    for g in range(NOBS // LANES):
        out_ref[pl.ds(g, 1), :] = total[0:1, g * LANES : (g + 1) * LANES]
    for copy in leaving:
        copy.wait()


def own_columns_and_spread(plan, locations, state):
    return pl.pallas_call(
        columns_kernel,
        out_shape=(struct((NOBS // LANES, LANES)), struct((GROUP, OWN_TILES, LANES))),
        in_specs=[SMEM, SMEM, ANY],
        out_specs=(VMEM, ANY),
        scratch_shapes=[
            pltpu.VMEM((OWN_TILES, GROUP, LANES), f32),
            pltpu.VMEM((NOBS, LANES), f32),
            pltpu.SemaphoreType.DMA((PIECES,)),
            pltpu.SemaphoreType.DMA((GROUP,)),
        ],
        compiler_params=kernel_params(60),
        cost_estimate=pl.CostEstimate(flops=10**6, bytes_accessed=8 * 2**20, transcendentals=0),
        name="own_columns",
    )(plan, locations, state.reshape(OWN_TILES, GROUP, LANES))


def collect_kernel(in_ref, state_ref, held_ref, in_sems, out_sems):
    devices = GROUP // PIECES
    arriving = [
        pltpu.make_async_copy(
            in_ref.at[pl.ds(n * devices, devices)], held_ref.at[pl.ds(n * devices, devices)], in_sems.at[n]
        )
        for n in range(PIECES)
    ]
    leaving = [
        pltpu.make_async_copy(held_ref.at[d], state_ref.at[:, d, :], out_sems.at[d]) for d in range(GROUP)
    ]
    for copy in arriving:
        copy.start()
    for n in range(PIECES):
        arriving[n].wait()
        for copy in leaving[n * devices : (n + 1) * devices]:
            copy.start()
    for copy in leaving:
        copy.wait()


def collect(blocks):
    return pl.pallas_call(
        collect_kernel,
        out_shape=struct((OWN_TILES, GROUP, LANES)),
        in_specs=[ANY],
        out_specs=ANY,
        scratch_shapes=[
            pltpu.VMEM((GROUP, OWN_TILES, LANES), f32),
            pltpu.SemaphoreType.DMA((PIECES,)),
            pltpu.SemaphoreType.DMA((GROUP,)),
        ],
        compiler_params=kernel_params(60),
        cost_estimate=pl.CostEstimate(flops=10**6, bytes_accessed=8 * 2**20, transcendentals=0),
        name="collect",
    )(blocks)


def observation_kernel(
    position_ref, plan_ref, facts_ref, own_ref, other_ref,
    columns_ref, factors_ref,
    ensemble_ref, increments_ref, one_hot_ref, facts_scratch, in_columns_ref,
    turned_ref, links_high_ref, links_low_ref, sort_ref, sort_back_ref,
):
    core = position_ref[2]
    for d in range(SUMS):
        for gathered_ref, start in ((own_ref, core), (other_ref, 1 - core)):
            rows = pl.ds(pl.multiple_of(d * GROUP + start * GROUP_CHIPS, GROUP_CHIPS), GROUP_CHIPS)
            for g in range(NOBS // LANES):
                ensemble_ref[rows, g * LANES : (g + 1) * LANES] = gathered_ref[
                    pl.ds(d * 8 + g, GROUP_CHIPS, stride=40), :
                ]
    for g in range(NOBS // LANES):
        rows = pl.ds((g // 4) * 40 + 32 + g % 4, 16, stride=80)
        facts_scratch[0:16, g * LANES : (g + 1) * LANES] = own_ref[rows, :] + other_ref[rows, :]
    facts_scratch[16:24, :] = facts_ref[...]
    facts_scratch[24:128, :] = jnp.zeros((104, NOBS), f32)
    source = lax.broadcasted_iota(i32, (NOBS, NOBS), 0)
    one_hot_ref[...] = jnp.where(source == plan_ref[...], 1.0, 0.0).astype(bf16)
    high, middle, low = three_parts(facts_scratch[0:32, :])
    ordered = dot(high, one_hot_ref[...]) + dot(middle, one_hot_ref[...]) + dot(low, one_hot_ref[...])
    facts_scratch[0:32, :] = ordered
    for g in range(NOBS // LANES):
        in_columns_ref[g * LANES : (g + 1) * LANES, :] = facts_scratch[:, g * LANES : (g + 1) * LANES].T

    residue = position_ref[0]
    tile_row = facts_scratch[16:17, :].astype(i32)
    tile_column = in_columns_ref[:, 16:17].astype(i32)
    nth_row = (residue - tile_row + RADIUS) & (RESIDUES - 1)
    nth_column = (residue - tile_column + RADIUS) & (RESIDUES - 1)
    own_row = ((tile_row - RADIUS + nth_row) & (NTILES - 1)) >> 4
    own_column = ((tile_column - RADIUS + nth_column) & (NTILES - 1)) >> 4
    own_row = jnp.where(nth_row < WINDOW, own_row, -1)
    own_column = jnp.where(nth_column < WINDOW, own_column, -2)
    mask_column = jnp.zeros((NOBS, 1), f32)
    for n in range(WINDOW):
        mask_column = mask_column + jnp.where(nth_column == n, in_columns_ref[:, n : n + 1], 0.0)

    mask_row = jnp.zeros((1, NOBS), f32)
    for n in range(WINDOW):
        mask_row = mask_row + jnp.where(nth_row == n, facts_scratch[n : n + 1, :], 0.0)

    key_row = jnp.where(own_row < 0, OWN_TILES, own_row) * NOBS + lax.broadcasted_iota(i32, (1, NOBS), 1)
    key_column = jnp.where(own_column < 0, OWN_TILES, own_column) * NOBS + lax.broadcasted_iota(i32, (NOBS, 1), 0)
    rank_row = jnp.sum(jnp.where(key_column < key_row, 1.0, 0.0), axis=0, keepdims=True).astype(i32)
    rank_column = jnp.sum(jnp.where(key_row < key_column, 1.0, 0.0), axis=1, keepdims=True).astype(i32)
    sort_ref[...] = jnp.where(source == rank_row, 1.0, 0.0).astype(bf16)
    to = lax.broadcasted_iota(i32, (NOBS, NOBS), 1)
    sort_back_ref[...] = jnp.where(to == rank_column, 1.0, 0.0).astype(bf16)

    gain_rows = []
    for b in range(BATCHES):
        here = slice(b * BATCH_OBS, (b + 1) * BATCH_OBS)
        prior = ensemble_ref[:, here]
        average = jnp.sum(prior, axis=0, keepdims=True) / MEMBERS
        anomaly = prior - average
        spread = jnp.sum(anomaly * anomaly, axis=0, keepdims=True) / (MEMBERS - 1) + epsilon
        value = facts_scratch[17:18, here]
        error = facts_scratch[18:19, here]
        shrink = jnp.sqrt(error / (spread + error))
        moved = (average * error + value * spread) / (spread + error)
        increments = (shrink - 1.0) * anomaly + (moved - average)
        increments_ref[:, here] = increments
        turned = anomaly.T
        spread_column = jnp.sum(turned * turned, axis=1, keepdims=True) / (MEMBERS - 1) + epsilon
        gain_column = 1.0 / ((MEMBERS - 1) * spread_column)
        turned_high, turned_low = two_parts(turned)
        turned_ref[here, :] = jnp.concatenate([turned_high[:, 0:GROUP], turned_low[:, 0:GROUP]], axis=1)
        gain_rows.append(1.0 / ((MEMBERS - 1) * spread))
        weight = mask_column[here] * gain_column
        if b > 0:
            before = b * BATCH_OBS
            links = accurate_dot(turned, increments_ref[:, 0:before])
            links = jnp.where(own_column[here] == own_row[:, 0:before], links * weight, 0.0)
            links_high, links_low = two_parts(links)
            links_high_ref[here, 0:before] = links_high
            links_low_ref[here, 0:before] = links_low
        if b < BATCHES - 1:
            after = slice((b + 1) * BATCH_OBS, NOBS)
            later = ensemble_ref[:, after]
            covariance = dot_parts(turned_high, turned_low, *two_parts(later))
            apart = (tile_row[:, after] - tile_column[here] + RADIUS) & (NTILES - 1)
            masks = jnp.zeros(apart.shape, f32)
            for n in range(WINDOW):
                masks = jnp.where(apart == n, in_columns_ref[here, n : n + 1], masks)
            ensemble_ref[:, after] = later + accurate_dot(increments, covariance * masks * gain_column)

    for b in reversed(range(BATCHES - 1)):
        here = slice(b * BATCH_OBS, (b + 1) * BATCH_OBS)
        after = slice((b + 1) * BATCH_OBS, NOBS)
        increments_ref[0:GROUP, here] += dot_parts(
            *two_parts(increments_ref[0:GROUP, after]), links_high_ref[after, here], links_low_ref[after, here]
        )
    factors = increments_ref[0:GROUP, :] * (mask_row * jnp.concatenate(gain_rows, axis=1))

    tile_here = jnp.where(own_column < 0, NOWHERE, own_column).astype(f32)
    tile_here = jnp.broadcast_to(tile_here, (NOBS, LANES)).astype(bf16)
    sorted_columns = dot(sort_ref[...], jnp.concatenate([turned_ref[...], tile_here], axis=1))
    high = sorted_columns[:, 0:GROUP].astype(bf16)
    low = sorted_columns[:, GROUP : 2 * GROUP].astype(bf16)
    replicate = jnp.where(
        lax.broadcasted_iota(i32, (GROUP, WIDE), 1) >> 3 == lax.broadcasted_iota(i32, (GROUP, WIDE), 0), 1.0, 0.0
    ).astype(bf16)
    columns_ref[0:NOBS, 0:WIDE] = dot(high, replicate).astype(bf16)
    columns_ref[0:NOBS, LOW] = dot(low, replicate).astype(bf16)
    nth_of_eight = (lax.broadcasted_iota(i32, (NOBS, LANES), 1) & (EIGHT - 1)).astype(f32)
    columns_ref[0:NOBS, TILES] = (sorted_columns[:, LANES : LANES + 1] - nth_of_eight).astype(bf16)
    columns_ref[NOBS:, 0 : 2 * WIDE] = jnp.zeros((WINDOW_ROWS, 2 * WIDE), bf16)
    columns_ref[NOBS:, TILES] = jnp.full((WINDOW_ROWS, LANES), NOWHERE, bf16)

    factors_high, factors_low = two_parts(factors)
    tile_there = jnp.where(own_row < 0, NOWHERE, own_row).astype(f32)
    tile_there = jnp.broadcast_to(tile_there, (GROUP, NOBS)).astype(bf16)
    sorted_rows = dot(jnp.concatenate([factors_high, factors_low, tile_there], axis=0), sort_back_ref[...])
    replicate = jnp.where(
        lax.broadcasted_iota(i32, (WIDE, GROUP), 0) >> 3 == lax.broadcasted_iota(i32, (WIDE, GROUP), 1), 1.0, 0.0
    ).astype(bf16)
    factors_ref[0:WIDE, 0:NOBS] = dot(replicate, sorted_rows[0:GROUP].astype(bf16)).astype(bf16)
    factors_ref[LOW, 0:NOBS] = dot(replicate, sorted_rows[GROUP : 2 * GROUP].astype(bf16)).astype(bf16)
    nth_of_eight = (lax.broadcasted_iota(i32, (16, NOBS), 0) & (EIGHT - 1)).astype(f32)
    factors_ref[TILE_ROWS, 0:NOBS] = (sorted_rows[2 * GROUP : 2 * GROUP + 16] - nth_of_eight).astype(bf16)
    factors_ref[0 : 2 * WIDE, NOBS:] = jnp.zeros((2 * WIDE, WINDOW_COLUMNS), bf16)
    factors_ref[TILE_ROWS, NOBS:] = jnp.full((16, WINDOW_COLUMNS), NOWHERE, bf16)


def observations(position, plan, facts, own, other):
    columns = struct((PADDED_ROWS, 2 * WIDE + LANES), bf16)
    factors = struct((2 * WIDE + 16, PADDED_COLUMNS), bf16)
    square = pltpu.VMEM((NOBS, NOBS), bf16)
    return pl.pallas_call(
        observation_kernel,
        out_shape=(columns, factors),
        in_specs=[SMEM, VMEM, VMEM, VMEM, VMEM],
        out_specs=(VMEM,) * 2,
        scratch_shapes=[
            pltpu.VMEM((MEMBERS, NOBS), f32),
            pltpu.VMEM((MEMBERS, NOBS), f32),
            square,
            pltpu.VMEM((128, NOBS), f32),
            pltpu.VMEM((NOBS, 128), f32),
            pltpu.VMEM((NOBS, 2 * GROUP), bf16),
            square,
            square,
            square,
            square,
        ],
        compiler_params=kernel_params(44),
        cost_estimate=pl.CostEstimate(flops=20 * 10**9, bytes_accessed=8 * 2**20, transcendentals=10**5),
        name="observations",
    )(position, plan, facts, own, other)


def for_windows(starts_ref, groups, size, align, visit):
    def start(g, i):
        return pl.multiple_of((starts_ref[g] & -align) + i * size, align)

    for g in groups:
        visit(g, start(g, 0))
    return functools.partial(for_rest, starts_ref, groups, size, align, visit, start)


def for_rest(starts_ref, groups, size, align, visit, start):
    for g in groups:
        count = (starts_ref[g + 1] - (starts_ref[g] & -align) + size - 1) // size

        def step(i, carry, g=g):
            visit(g, start(g, i))
            return carry

        lax.fori_loop(1, count, step, 0)


COVARIANCE_PIECES = 2
UPDATE_PIECES = 4


def piece_copies(pieces, from_ref, to_ref, sems):
    tiles = OWN_TILES // pieces
    return [
        pltpu.make_async_copy(
            from_ref.at[:, pl.ds(n * tiles, tiles), :], to_ref.at[:, pl.ds(n * tiles, tiles), :], sems.at[n]
        )
        for n in range(pieces)
    ]


def piece_groups(pieces, n):
    groups = GROUPS // pieces
    return range(n * groups, (n + 1) * groups)


def covariance_kernel(position_ref, starts_ref, block_ref, columns_in_ref, *refs):
    out_refs, (total_ref, held_ref, columns_ref, sems, columns_sems) = refs[: 2 * SUMS], refs[2 * SUMS :]
    usual = FIRST + WINDOW_ROWS
    columns_copy, more_copy = (
        pltpu.make_async_copy(columns_in_ref.at[rows], columns_ref.at[rows], columns_sems.at[n])
        for n, rows in enumerate((pl.ds(0, usual), pl.ds(usual, PADDED_ROWS - usual)))
    )
    columns_copy.start()
    arriving = piece_copies(COVARIANCE_PIECES, block_ref, held_ref, sems)
    for copy in arriving:
        copy.start()
    total_ref[...] = jnp.zeros_like(total_ref)
    zero = jnp.zeros((WINDOW_ROWS, LANES), bf16)

    def visit(g, start):
        rows = pl.ds(start, WINDOW_ROWS)
        found = columns_ref[rows, TILES] == jnp.full((WINDOW_ROWS, LANES), g * EIGHT, bf16)
        left = [
            jnp.concatenate(
                [
                    jnp.where(found, columns_ref[rows, part * WIDE + n * LANES : part * WIDE + (n + 1) * LANES], zero)
                    for n in range(WIDE // LANES)
                ],
                axis=1,
            )
            for part in range(2)
        ]
        right = held_ref[:, g * EIGHT : (g + 1) * EIGHT, :].reshape(WIDE, LANES)
        both = dot(jnp.concatenate(left, axis=0), jnp.concatenate(two_parts(right), axis=1))
        both = both[:WINDOW_ROWS] + both[WINDOW_ROWS:]
        total_ref[rows, :] += both[:, :LANES] + both[:, LANES:]

    columns_copy.wait()

    @pl.when(starts_ref[GROUPS] > FIRST)
    def _():
        more_copy.start()
        more_copy.wait()

    rest = []
    for n in range(COVARIANCE_PIECES):
        arriving[n].wait()
        rest.append(for_windows(starts_ref, piece_groups(COVARIANCE_PIECES, n), WINDOW_ROWS, 16, visit))
    for windows in rest:
        windows()
    for d in range(SUMS):
        to = position_ref[1] ^ d
        start = pl.multiple_of(to * FIRST_CHUNK, 16)
        out_refs[d][...] = total_ref[pl.ds(start, FIRST_CHUNK), :]
        start = pl.multiple_of(FIRST + to * REST_CHUNK, 16)
        out_refs[SUMS + d][...] = total_ref[pl.ds(start, REST_CHUNK), :]


def covariances(position, starts, block, columns):
    return pl.pallas_call(
        covariance_kernel,
        out_shape=(struct((FIRST_CHUNK, LANES)),) * SUMS + (struct((REST_CHUNK, LANES)),) * SUMS,
        in_specs=[SMEM, SMEM, ANY, ANY],
        out_specs=(VMEM,) * (2 * SUMS),
        scratch_shapes=[
            pltpu.VMEM((PADDED_ROWS, LANES), f32),
            pltpu.VMEM((GROUP, OWN_TILES, LANES), f32),
            pltpu.VMEM((PADDED_ROWS, 2 * WIDE + LANES), bf16),
            pltpu.SemaphoreType.DMA((COVARIANCE_PIECES,)),
            pltpu.SemaphoreType.DMA((2,)),
        ],
        compiler_params=kernel_params(60),
        cost_estimate=pl.CostEstimate(flops=3 * 10**9, bytes_accessed=7 * 2**20, transcendentals=0),
        name="covariances",
    )(position, starts, block, columns)


def update_kernel(position_ref, starts_ref, *refs):
    sums_refs = refs[: 2 * SUMS]
    block_ref, factors_ref, out_ref, right_ref, held_ref, in_sems, out_sems = refs[2 * SUMS :]
    arriving = piece_copies(UPDATE_PIECES, block_ref, held_ref, in_sems)
    leaving = piece_copies(UPDATE_PIECES, held_ref, out_ref, out_sems)
    for copy in arriving:
        copy.start()
    for d in range(SUMS):
        of = position_ref[1] ^ d
        start = pl.multiple_of(of * FIRST_CHUNK, 16)
        right_ref[pl.ds(start, FIRST_CHUNK), :] = jnp.concatenate(two_parts(sums_refs[d][...]), axis=1)
        start = pl.multiple_of(FIRST + of * REST_CHUNK, 16)
        right_ref[pl.ds(start, REST_CHUNK), :] = jnp.concatenate(two_parts(sums_refs[SUMS + d][...]), axis=1)
    right_ref[NOBS:, :] = jnp.zeros((WINDOW_COLUMNS, 2 * LANES), bf16)

    def visit(g, start):
        columns = pl.ds(start, WINDOW_COLUMNS)
        shape = (16, WINDOW_COLUMNS)
        found = factors_ref[TILE_ROWS, columns] == jnp.full(shape, g * EIGHT, bf16)
        found = jnp.where(found, jnp.ones(shape, bf16), jnp.zeros(shape, bf16))
        left = [
            (factors_ref[part, columns].reshape(WIDE // 16, 16, WINDOW_COLUMNS) * found[None]).reshape(WIDE, WINDOW_COLUMNS)
            for part in (slice(0, WIDE), LOW)
        ]
        both = dot(jnp.concatenate(left, axis=0), right_ref[columns, :])
        both = both[:WIDE] + both[WIDE:]
        held_ref[:, g * EIGHT : (g + 1) * EIGHT, :] += (both[:, :LANES] + both[:, LANES:]).reshape(GROUP, EIGHT, LANES)

    for n in range(UPDATE_PIECES):
        arriving[n].wait()
        for_windows(starts_ref, piece_groups(UPDATE_PIECES, n), WINDOW_COLUMNS, LANES, visit)()
        leaving[n].start()
    for copy in leaving:
        copy.wait()


def updated(position, starts, sums, block, factors):
    return pl.pallas_call(
        update_kernel,
        out_shape=struct((GROUP, OWN_TILES, LANES)),
        in_specs=[SMEM, SMEM] + [VMEM] * (2 * SUMS) + [ANY, VMEM],
        out_specs=ANY,
        scratch_shapes=[
            pltpu.VMEM((PADDED_COLUMNS, 2 * LANES), bf16),
            pltpu.VMEM((GROUP, OWN_TILES, LANES), f32),
            pltpu.SemaphoreType.DMA((UPDATE_PIECES,)),
            pltpu.SemaphoreType.DMA((UPDATE_PIECES,)),
        ],
        compiler_params=kernel_params(24),
        cost_estimate=pl.CostEstimate(flops=4 * 10**9, bytes_accessed=8 * 2**20, transcendentals=0),
        name="updated",
    )(position, starts, *sums, block, factors)


def exchange(value, axes=PEERS):
    return lax.all_to_all(value, axes, 0, 0, tiled=True)


def swapped(value, by):
    return lax.ppermute(value, "h", [(i, i ^ by) for i in range(SUMS)])


def summed(parts):
    total = parts[0]
    for by in range(1, SUMS):
        total = total + swapped(parts[by], by)
    return (total, *(swapped(total, by) for by in range(1, SUMS)))


def shards(state, locations, tile_mask, plan, obs_value, obs_error):
    residue = lax.axis_index(PEERS) // SLICES
    position = jnp.stack([residue, lax.axis_index("h"), lax.axis_index("c"), lax.axis_index(ALL)]).astype(i32)

    masks = own_masks(position, locations.reshape(-1, LANES), tile_mask)
    masks = exchange(masks.reshape(GROUP_CHIPS, 4, LANES), CHIPS).sum(axis=0)
    tiles = locations // TILE

    observed, block = own_columns_and_spread(plan, locations, state)
    mine = jnp.concatenate([observed, masks], axis=0)
    all_four = [mine] + [swapped(mine, by) for by in range(1, SUMS)]
    payload = jnp.concatenate(
        [*(each[0:8] for each in all_four), sum(each[8:12] for each in all_four), jnp.zeros((4, LANES), f32)], axis=0
    )
    gathered = exchange(jnp.broadcast_to(payload[None], (GROUP_CHIPS, 40, LANES)), CHIPS)
    other = lax.ppermute(gathered, "c", [(0, 1), (1, 0)])
    block, other = lax.optimization_barrier((block, other))
    block = exchange(block)

    facts = jnp.concatenate(
        [tiles.astype(f32)[None], obs_value[None], obs_error[None], jnp.zeros((5, NOBS), f32)], axis=0
    )
    columns, factors = observations(
        position, plan[None], facts, gathered.reshape(-1, LANES), other.reshape(-1, LANES)
    )
    nth_own = (residue - tiles + RADIUS) & (RESIDUES - 1)
    own_tile = jnp.where(nth_own < WINDOW, ((tiles - RADIUS + nth_own) & (NTILES - 1)) // RESIDUES, OWN_TILES)
    starts = jnp.sum(own_tile[None, :] < EIGHT * jnp.arange(GROUPS + 1, dtype=i32)[:, None], axis=1, dtype=i32)
    nth_all = (jnp.arange(RESIDUES, dtype=i32)[:, None] - tiles[None, :] + RADIUS) & (RESIDUES - 1)
    most = jnp.max(jnp.sum(nth_all < WINDOW, axis=1, dtype=i32))

    parts = covariances(position, starts, block, columns)
    rest = lax.cond(most > FIRST, summed, lambda parts: parts, parts[SUMS:])
    sums = summed(parts[:SUMS]) + tuple(rest)
    block = exchange(updated(position, starts, sums, block, factors))
    return collect(block).reshape(state.shape)


def solution(mesh):
    fine = Mesh(mesh.devices.reshape(4, 4, 2, 2, 4), ALL)
    placed = (P(ALL, None), P(), P(ALL, None), P(), P(), P())
    return jax.shard_map(shards, mesh=fine, in_specs=placed, out_specs=P(ALL, None), check_vma=False)
```

```python
import functools

import jax
import jax.numpy as jnp
from jax import lax
from jax.experimental import pallas as pl
from jax.experimental.pallas import tpu as pltpu
from jax.sharding import Mesh, PartitionSpec as P

MEMBERS = 256
TILE = 512
NTILES = 2048
RADIUS = 4
WINDOW = 2 * RADIUS + 1
BATCH_OBS = 256
BATCHES = 4
NOBS = BATCH_OBS * BATCHES

ALL = ("y", "h", "l", "c", "x")
PEERS = ("c", "y", "l", "x")
CHIPS = ("y", "l", "x")
GROUP = 64
CORES = 2
GROUP_CHIPS = GROUP // CORES
SUMS = 4
RESIDUES = 16
SLICES = 4
LANES = 128
OWN_TILES = NTILES // RESIDUES
ROWS = NTILES * TILE // LANES
EIGHT = 8
WIDE = EIGHT * GROUP
GROUPS = OWN_TILES // EIGHT
WINDOW_ROWS = 128
WINDOW_COLUMNS = 256
PADDED_ROWS = NOBS + WINDOW_ROWS
PADDED_COLUMNS = NOBS + WINDOW_COLUMNS
LOW = slice(WIDE, 2 * WIDE)
TILES = slice(2 * WIDE, 2 * WIDE + LANES)
TILE_ROWS = slice(2 * WIDE, 2 * WIDE + 16)
NOWHERE = -512
BLOCK_TILES = 16
FIRST = 640
FIRST_CHUNK = FIRST // SUMS
REST_CHUNK = (NOBS - FIRST) // SUMS

epsilon = 1e-06
f32 = jnp.float32
bf16 = jnp.bfloat16
i32 = jnp.int32

VMEM = pl.BlockSpec(memory_space=pltpu.VMEM)
SMEM = pl.BlockSpec(memory_space=pltpu.SMEM)
ANY = pl.BlockSpec(memory_space=pl.ANY)


def kernel_params(mib):
    return pltpu.CompilerParams(vmem_limit_bytes=mib * 1024 * 1024)


def struct(shape, dtype=f32):
    return jax.ShapeDtypeStruct(shape, dtype)


def two_parts(value):
    high = value.astype(bf16)
    return high, (value - high.astype(f32)).astype(bf16)


def three_parts(value):
    high = value.astype(bf16)
    rest = value - high.astype(f32)
    middle = rest.astype(bf16)
    return high, middle, (rest - middle.astype(f32)).astype(bf16)


def dot(a, b):
    return lax.dot_general(a, b, (((1,), (0,)), ((), ())), preferred_element_type=f32)


def dot_parts(a_high, a_low, b_high, b_low):
    return dot(a_high, b_high) + dot(a_high, b_low) + dot(a_low, b_high)


def accurate_dot(a, b):
    return dot_parts(*two_parts(a), *two_parts(b))


def masks_kernel(position_ref, locations_in_ref, tile_mask_in_ref, out_ref, locations_ref, tile_mask_ref, sems):
    copies = [
        pltpu.make_async_copy(locations_in_ref, locations_ref, sems.at[0]),
        pltpu.make_async_copy(tile_mask_in_ref, tile_mask_ref, sems.at[1]),
    ]
    for copy in copies:
        copy.start()
    for copy in copies:
        copy.wait()
    tiles_here = tile_mask_ref.shape[0]
    first = position_ref[3] * tiles_here
    per_row = NOBS // LANES
    relative = (locations_ref[...] >> 9) - RADIUS - first
    masks = [
        jnp.concatenate([tile_mask_ref[i : i + 1, g * LANES : (g + 1) * LANES] for g in range(per_row)], axis=0)
        for i in range(tiles_here)
    ]
    for n in range(16):
        local = (relative + n) & (NTILES - 1)
        found = jnp.zeros((per_row, LANES), i32)
        if n < WINDOW:
            for i in range(tiles_here):
                found = jnp.where(local == i, masks[i], found)
        out_ref[n * per_row : (n + 1) * per_row, :] = found.astype(f32)


def own_masks(position, locations, tile_mask):
    return pl.pallas_call(
        masks_kernel,
        out_shape=struct((16 * NOBS // LANES, LANES)),
        in_specs=[SMEM, ANY, ANY],
        out_specs=VMEM,
        scratch_shapes=[
            pltpu.VMEM(locations.shape, i32), pltpu.VMEM(tile_mask.shape, i32), pltpu.SemaphoreType.DMA((2,))
        ],
        compiler_params=kernel_params(60),
        cost_estimate=pl.CostEstimate(flops=10**5, bytes_accessed=10**5, transcendentals=0),
        name="own_masks",
    )(position, locations, tile_mask)


def columns_kernel(plan_ref, locations_ref, state_ref, out_ref, picked_ref):
    lane = lax.broadcasted_iota(i32, (1, LANES), 1)

    def step(i, carry):
        base = pl.multiple_of(i * 8, 8)
        found = []
        for u in range(8):
            where = locations_ref[plan_ref[base + u]]
            row = state_ref[pl.ds(where >> 7, 1), :]
            found.append(jnp.where(lane == (where & (LANES - 1)), row, 0.0))
        picked_ref[pl.ds(base, 8), :] = jnp.concatenate(found, axis=0)
        return carry

    lax.fori_loop(0, NOBS // 8, step, 0, unroll=2)
    ones = jnp.ones((16, LANES), bf16)
    total = jnp.zeros((16, NOBS), f32)
    for part in three_parts(picked_ref[...]):
        total = total + lax.dot_general(ones, part, (((1,), (1,)), ((), ())), preferred_element_type=f32)
    for g in range(NOBS // LANES):
        out_ref[pl.ds(g, 1), :] = total[0:1, g * LANES : (g + 1) * LANES]


def own_columns(plan, locations, rows):
    return pl.pallas_call(
        columns_kernel,
        out_shape=struct((NOBS // LANES, LANES)),
        in_specs=[SMEM, SMEM, VMEM],
        out_specs=VMEM,
        scratch_shapes=[pltpu.VMEM((NOBS, LANES), f32)],
        compiler_params=kernel_params(24),
        cost_estimate=pl.CostEstimate(flops=10**6, bytes_accessed=8 * 2**20, transcendentals=0),
        name="own_columns",
    )(plan, locations, rows)


def spread_kernel(state_ref, out_ref):
    for d in range(GROUP):
        out_ref[d] = state_ref[pl.ds(d, BLOCK_TILES, stride=GROUP), :]


def spread_out(rows):
    return pl.pallas_call(
        spread_kernel,
        grid=(OWN_TILES // BLOCK_TILES,),
        out_shape=struct((GROUP, OWN_TILES, LANES)),
        in_specs=[pl.BlockSpec((GROUP * BLOCK_TILES, LANES), lambda i: (i, 0))],
        out_specs=pl.BlockSpec((GROUP, BLOCK_TILES, LANES), lambda i: (0, i, 0)),
        compiler_params=kernel_params(16),
        cost_estimate=pl.CostEstimate(flops=10**6, bytes_accessed=8 * 2**20, transcendentals=0),
        name="spread_out",
    )(rows)


PIECES = 8


def collect_kernel(in_ref, state_ref, held_ref, in_sems, out_sems):
    devices = GROUP // PIECES
    arriving = [
        pltpu.make_async_copy(
            in_ref.at[pl.ds(n * devices, devices)], held_ref.at[pl.ds(n * devices, devices)], in_sems.at[n]
        )
        for n in range(PIECES)
    ]
    leaving = [
        pltpu.make_async_copy(held_ref.at[d], state_ref.at[:, d, :], out_sems.at[d]) for d in range(GROUP)
    ]
    for copy in arriving:
        copy.start()
    for n in range(PIECES):
        arriving[n].wait()
        for copy in leaving[n * devices : (n + 1) * devices]:
            copy.start()
    for copy in leaving:
        copy.wait()


def collect(blocks):
    return pl.pallas_call(
        collect_kernel,
        out_shape=struct((OWN_TILES, GROUP, LANES)),
        in_specs=[ANY],
        out_specs=ANY,
        scratch_shapes=[
            pltpu.VMEM((GROUP, OWN_TILES, LANES), f32),
            pltpu.SemaphoreType.DMA((PIECES,)),
            pltpu.SemaphoreType.DMA((GROUP,)),
        ],
        compiler_params=kernel_params(60),
        cost_estimate=pl.CostEstimate(flops=10**6, bytes_accessed=8 * 2**20, transcendentals=0),
        name="collect",
    )(blocks)


def observation_kernel(
    position_ref, plan_ref, facts_ref, own_ref, other_ref,
    columns_ref, factors_ref,
    ensemble_ref, increments_ref, one_hot_ref, facts_scratch, in_columns_ref,
    turned_ref, links_high_ref, links_low_ref, sort_ref, sort_back_ref,
):
    core = position_ref[2]
    for d in range(SUMS):
        for gathered_ref, start in ((own_ref, core), (other_ref, 1 - core)):
            rows = pl.ds(pl.multiple_of(d * GROUP + start * GROUP_CHIPS, GROUP_CHIPS), GROUP_CHIPS)
            for g in range(NOBS // LANES):
                ensemble_ref[rows, g * LANES : (g + 1) * LANES] = gathered_ref[
                    pl.ds(d * 8 + g, GROUP_CHIPS, stride=40), :
                ]
    for g in range(NOBS // LANES):
        rows = pl.ds((g // 4) * 40 + 32 + g % 4, 16, stride=80)
        facts_scratch[0:16, g * LANES : (g + 1) * LANES] = own_ref[rows, :] + other_ref[rows, :]
    facts_scratch[16:24, :] = facts_ref[...]
    facts_scratch[24:128, :] = jnp.zeros((104, NOBS), f32)
    source = lax.broadcasted_iota(i32, (NOBS, NOBS), 0)
    one_hot_ref[...] = jnp.where(source == plan_ref[...], 1.0, 0.0).astype(bf16)
    high, middle, low = three_parts(facts_scratch[0:32, :])
    ordered = dot(high, one_hot_ref[...]) + dot(middle, one_hot_ref[...]) + dot(low, one_hot_ref[...])
    facts_scratch[0:32, :] = ordered
    for g in range(NOBS // LANES):
        in_columns_ref[g * LANES : (g + 1) * LANES, :] = facts_scratch[:, g * LANES : (g + 1) * LANES].T

    residue = position_ref[0]
    tile_row = facts_scratch[16:17, :].astype(i32)
    tile_column = in_columns_ref[:, 16:17].astype(i32)
    nth_row = (residue - tile_row + RADIUS) & (RESIDUES - 1)
    nth_column = (residue - tile_column + RADIUS) & (RESIDUES - 1)
    own_row = ((tile_row - RADIUS + nth_row) & (NTILES - 1)) >> 4
    own_column = ((tile_column - RADIUS + nth_column) & (NTILES - 1)) >> 4
    own_row = jnp.where(nth_row < WINDOW, own_row, -1)
    own_column = jnp.where(nth_column < WINDOW, own_column, -2)
    mask_column = jnp.zeros((NOBS, 1), f32)
    for n in range(WINDOW):
        mask_column = mask_column + jnp.where(nth_column == n, in_columns_ref[:, n : n + 1], 0.0)

    mask_row = jnp.zeros((1, NOBS), f32)
    for n in range(WINDOW):
        mask_row = mask_row + jnp.where(nth_row == n, facts_scratch[n : n + 1, :], 0.0)

    key_row = jnp.where(own_row < 0, OWN_TILES, own_row) * NOBS + lax.broadcasted_iota(i32, (1, NOBS), 1)
    key_column = jnp.where(own_column < 0, OWN_TILES, own_column) * NOBS + lax.broadcasted_iota(i32, (NOBS, 1), 0)
    rank_row = jnp.sum(jnp.where(key_column < key_row, 1.0, 0.0), axis=0, keepdims=True).astype(i32)
    rank_column = jnp.sum(jnp.where(key_row < key_column, 1.0, 0.0), axis=1, keepdims=True).astype(i32)
    sort_ref[...] = jnp.where(source == rank_row, 1.0, 0.0).astype(bf16)
    to = lax.broadcasted_iota(i32, (NOBS, NOBS), 1)
    sort_back_ref[...] = jnp.where(to == rank_column, 1.0, 0.0).astype(bf16)

    gain_rows = []
    for b in range(BATCHES):
        here = slice(b * BATCH_OBS, (b + 1) * BATCH_OBS)
        prior = ensemble_ref[:, here]
        average = jnp.sum(prior, axis=0, keepdims=True) / MEMBERS
        anomaly = prior - average
        spread = jnp.sum(anomaly * anomaly, axis=0, keepdims=True) / (MEMBERS - 1) + epsilon
        value = facts_scratch[17:18, here]
        error = facts_scratch[18:19, here]
        shrink = jnp.sqrt(error / (spread + error))
        moved = (average * error + value * spread) / (spread + error)
        increments = (shrink - 1.0) * anomaly + (moved - average)
        increments_ref[:, here] = increments
        turned = anomaly.T
        spread_column = jnp.sum(turned * turned, axis=1, keepdims=True) / (MEMBERS - 1) + epsilon
        gain_column = 1.0 / ((MEMBERS - 1) * spread_column)
        turned_high, turned_low = two_parts(turned)
        turned_ref[here, :] = jnp.concatenate([turned_high[:, 0:GROUP], turned_low[:, 0:GROUP]], axis=1)
        gain_rows.append(1.0 / ((MEMBERS - 1) * spread))
        weight = mask_column[here] * gain_column
        if b > 0:
            before = b * BATCH_OBS
            links = accurate_dot(turned, increments_ref[:, 0:before])
            links = jnp.where(own_column[here] == own_row[:, 0:before], links * weight, 0.0)
            links_high, links_low = two_parts(links)
            links_high_ref[here, 0:before] = links_high
            links_low_ref[here, 0:before] = links_low
        if b < BATCHES - 1:
            after = slice((b + 1) * BATCH_OBS, NOBS)
            later = ensemble_ref[:, after]
            covariance = dot_parts(turned_high, turned_low, *two_parts(later))
            apart = (tile_row[:, after] - tile_column[here] + RADIUS) & (NTILES - 1)
            masks = jnp.zeros(apart.shape, f32)
            for n in range(WINDOW):
                masks = jnp.where(apart == n, in_columns_ref[here, n : n + 1], masks)
            ensemble_ref[:, after] = later + accurate_dot(increments, covariance * masks * gain_column)

    for b in reversed(range(BATCHES - 1)):
        here = slice(b * BATCH_OBS, (b + 1) * BATCH_OBS)
        after = slice((b + 1) * BATCH_OBS, NOBS)
        increments_ref[0:GROUP, here] += dot_parts(
            *two_parts(increments_ref[0:GROUP, after]), links_high_ref[after, here], links_low_ref[after, here]
        )
    factors = increments_ref[0:GROUP, :] * (mask_row * jnp.concatenate(gain_rows, axis=1))

    tile_here = jnp.where(own_column < 0, NOWHERE, own_column).astype(f32)
    tile_here = jnp.broadcast_to(tile_here, (NOBS, LANES)).astype(bf16)
    sorted_columns = dot(sort_ref[...], jnp.concatenate([turned_ref[...], tile_here], axis=1))
    high = sorted_columns[:, 0:GROUP].astype(bf16)
    low = sorted_columns[:, GROUP : 2 * GROUP].astype(bf16)
    replicate = jnp.where(
        lax.broadcasted_iota(i32, (GROUP, WIDE), 1) >> 3 == lax.broadcasted_iota(i32, (GROUP, WIDE), 0), 1.0, 0.0
    ).astype(bf16)
    columns_ref[0:NOBS, 0:WIDE] = dot(high, replicate).astype(bf16)
    columns_ref[0:NOBS, LOW] = dot(low, replicate).astype(bf16)
    nth_of_eight = (lax.broadcasted_iota(i32, (NOBS, LANES), 1) & (EIGHT - 1)).astype(f32)
    columns_ref[0:NOBS, TILES] = (sorted_columns[:, LANES : LANES + 1] - nth_of_eight).astype(bf16)
    columns_ref[NOBS:, 0 : 2 * WIDE] = jnp.zeros((WINDOW_ROWS, 2 * WIDE), bf16)
    columns_ref[NOBS:, TILES] = jnp.full((WINDOW_ROWS, LANES), NOWHERE, bf16)

    factors_high, factors_low = two_parts(factors)
    tile_there = jnp.where(own_row < 0, NOWHERE, own_row).astype(f32)
    tile_there = jnp.broadcast_to(tile_there, (GROUP, NOBS)).astype(bf16)
    sorted_rows = dot(jnp.concatenate([factors_high, factors_low, tile_there], axis=0), sort_back_ref[...])
    replicate = jnp.where(
        lax.broadcasted_iota(i32, (WIDE, GROUP), 0) >> 3 == lax.broadcasted_iota(i32, (WIDE, GROUP), 1), 1.0, 0.0
    ).astype(bf16)
    factors_ref[0:WIDE, 0:NOBS] = dot(replicate, sorted_rows[0:GROUP].astype(bf16)).astype(bf16)
    factors_ref[LOW, 0:NOBS] = dot(replicate, sorted_rows[GROUP : 2 * GROUP].astype(bf16)).astype(bf16)
    nth_of_eight = (lax.broadcasted_iota(i32, (16, NOBS), 0) & (EIGHT - 1)).astype(f32)
    factors_ref[TILE_ROWS, 0:NOBS] = (sorted_rows[2 * GROUP : 2 * GROUP + 16] - nth_of_eight).astype(bf16)
    factors_ref[0 : 2 * WIDE, NOBS:] = jnp.zeros((2 * WIDE, WINDOW_COLUMNS), bf16)
    factors_ref[TILE_ROWS, NOBS:] = jnp.full((16, WINDOW_COLUMNS), NOWHERE, bf16)


def observations(position, plan, facts, own, other):
    columns = struct((PADDED_ROWS, 2 * WIDE + LANES), bf16)
    factors = struct((2 * WIDE + 16, PADDED_COLUMNS), bf16)
    square = pltpu.VMEM((NOBS, NOBS), bf16)
    return pl.pallas_call(
        observation_kernel,
        out_shape=(columns, factors),
        in_specs=[SMEM, VMEM, VMEM, VMEM, VMEM],
        out_specs=(VMEM,) * 2,
        scratch_shapes=[
            pltpu.VMEM((MEMBERS, NOBS), f32),
            pltpu.VMEM((MEMBERS, NOBS), f32),
            square,
            pltpu.VMEM((128, NOBS), f32),
            pltpu.VMEM((NOBS, 128), f32),
            pltpu.VMEM((NOBS, 2 * GROUP), bf16),
            square,
            square,
            square,
            square,
        ],
        compiler_params=kernel_params(44),
        cost_estimate=pl.CostEstimate(flops=20 * 10**9, bytes_accessed=8 * 2**20, transcendentals=10**5),
        name="observations",
    )(position, plan, facts, own, other)


def for_windows(starts_ref, groups, size, align, visit):
    def start(g, i):
        return pl.multiple_of((starts_ref[g] & -align) + i * size, align)

    for g in groups:
        visit(g, start(g, 0))
    return functools.partial(for_rest, starts_ref, groups, size, align, visit, start)


def for_rest(starts_ref, groups, size, align, visit, start):
    for g in groups:
        count = (starts_ref[g + 1] - (starts_ref[g] & -align) + size - 1) // size

        def step(i, carry, g=g):
            visit(g, start(g, i))
            return carry

        lax.fori_loop(1, count, step, 0)


COVARIANCE_PIECES = 2
UPDATE_PIECES = 4


def piece_copies(pieces, from_ref, to_ref, sems):
    tiles = OWN_TILES // pieces
    return [
        pltpu.make_async_copy(
            from_ref.at[:, pl.ds(n * tiles, tiles), :], to_ref.at[:, pl.ds(n * tiles, tiles), :], sems.at[n]
        )
        for n in range(pieces)
    ]


def piece_groups(pieces, n):
    groups = GROUPS // pieces
    return range(n * groups, (n + 1) * groups)


def covariance_kernel(position_ref, starts_ref, block_ref, columns_in_ref, *refs):
    out_refs, (total_ref, held_ref, columns_ref, sems, columns_sems) = refs[: 2 * SUMS], refs[2 * SUMS :]
    usual = FIRST + WINDOW_ROWS
    columns_copy, more_copy = (
        pltpu.make_async_copy(columns_in_ref.at[rows], columns_ref.at[rows], columns_sems.at[n])
        for n, rows in enumerate((pl.ds(0, usual), pl.ds(usual, PADDED_ROWS - usual)))
    )
    columns_copy.start()
    arriving = piece_copies(COVARIANCE_PIECES, block_ref, held_ref, sems)
    for copy in arriving:
        copy.start()
    total_ref[...] = jnp.zeros_like(total_ref)
    zero = jnp.zeros((WINDOW_ROWS, LANES), bf16)

    def visit(g, start):
        rows = pl.ds(start, WINDOW_ROWS)
        found = columns_ref[rows, TILES] == jnp.full((WINDOW_ROWS, LANES), g * EIGHT, bf16)
        left = [
            jnp.concatenate(
                [
                    jnp.where(found, columns_ref[rows, part * WIDE + n * LANES : part * WIDE + (n + 1) * LANES], zero)
                    for n in range(WIDE // LANES)
                ],
                axis=1,
            )
            for part in range(2)
        ]
        right = held_ref[:, g * EIGHT : (g + 1) * EIGHT, :].reshape(WIDE, LANES)
        both = dot(jnp.concatenate(left, axis=0), jnp.concatenate(two_parts(right), axis=1))
        both = both[:WINDOW_ROWS] + both[WINDOW_ROWS:]
        total_ref[rows, :] += both[:, :LANES] + both[:, LANES:]

    columns_copy.wait()

    @pl.when(starts_ref[GROUPS] > FIRST)
    def _():
        more_copy.start()
        more_copy.wait()

    rest = []
    for n in range(COVARIANCE_PIECES):
        arriving[n].wait()
        rest.append(for_windows(starts_ref, piece_groups(COVARIANCE_PIECES, n), WINDOW_ROWS, 16, visit))
    for windows in rest:
        windows()
    for d in range(SUMS):
        to = (position_ref[1] + d) & (SUMS - 1)
        start = pl.multiple_of(to * FIRST_CHUNK, 16)
        out_refs[d][...] = total_ref[pl.ds(start, FIRST_CHUNK), :]
        start = pl.multiple_of(FIRST + to * REST_CHUNK, 16)
        out_refs[SUMS + d][...] = total_ref[pl.ds(start, REST_CHUNK), :]


def covariances(position, starts, block, columns):
    return pl.pallas_call(
        covariance_kernel,
        out_shape=(struct((FIRST_CHUNK, LANES)),) * SUMS + (struct((REST_CHUNK, LANES)),) * SUMS,
        in_specs=[SMEM, SMEM, ANY, ANY],
        out_specs=(VMEM,) * (2 * SUMS),
        scratch_shapes=[
            pltpu.VMEM((PADDED_ROWS, LANES), f32),
            pltpu.VMEM((GROUP, OWN_TILES, LANES), f32),
            pltpu.VMEM((PADDED_ROWS, 2 * WIDE + LANES), bf16),
            pltpu.SemaphoreType.DMA((COVARIANCE_PIECES,)),
            pltpu.SemaphoreType.DMA((2,)),
        ],
        compiler_params=kernel_params(60),
        cost_estimate=pl.CostEstimate(flops=3 * 10**9, bytes_accessed=7 * 2**20, transcendentals=0),
        name="covariances",
    )(position, starts, block, columns)


def update_kernel(position_ref, starts_ref, *refs):
    sums_refs = refs[: 2 * SUMS]
    block_ref, factors_ref, out_ref, right_ref, held_ref, in_sems, out_sems = refs[2 * SUMS :]
    arriving = piece_copies(UPDATE_PIECES, block_ref, held_ref, in_sems)
    leaving = piece_copies(UPDATE_PIECES, held_ref, out_ref, out_sems)
    for copy in arriving:
        copy.start()
    for d in range(SUMS):
        of = (position_ref[1] - d) & (SUMS - 1)
        start = pl.multiple_of(of * FIRST_CHUNK, 16)
        right_ref[pl.ds(start, FIRST_CHUNK), :] = jnp.concatenate(two_parts(sums_refs[d][...]), axis=1)
        start = pl.multiple_of(FIRST + of * REST_CHUNK, 16)
        right_ref[pl.ds(start, REST_CHUNK), :] = jnp.concatenate(two_parts(sums_refs[SUMS + d][...]), axis=1)
    right_ref[NOBS:, :] = jnp.zeros((WINDOW_COLUMNS, 2 * LANES), bf16)

    def visit(g, start):
        columns = pl.ds(start, WINDOW_COLUMNS)
        shape = (16, WINDOW_COLUMNS)
        found = factors_ref[TILE_ROWS, columns] == jnp.full(shape, g * EIGHT, bf16)
        found = jnp.where(found, jnp.ones(shape, bf16), jnp.zeros(shape, bf16))
        left = [
            (factors_ref[part, columns].reshape(WIDE // 16, 16, WINDOW_COLUMNS) * found[None]).reshape(WIDE, WINDOW_COLUMNS)
            for part in (slice(0, WIDE), LOW)
        ]
        both = dot(jnp.concatenate(left, axis=0), right_ref[columns, :])
        both = both[:WIDE] + both[WIDE:]
        held_ref[:, g * EIGHT : (g + 1) * EIGHT, :] += (both[:, :LANES] + both[:, LANES:]).reshape(GROUP, EIGHT, LANES)

    for n in range(UPDATE_PIECES):
        arriving[n].wait()
        for_windows(starts_ref, piece_groups(UPDATE_PIECES, n), WINDOW_COLUMNS, LANES, visit)()
        leaving[n].start()
    for copy in leaving:
        copy.wait()


def updated(position, starts, sums, block, factors):
    return pl.pallas_call(
        update_kernel,
        out_shape=struct((GROUP, OWN_TILES, LANES)),
        in_specs=[SMEM, SMEM] + [VMEM] * (2 * SUMS) + [ANY, VMEM],
        out_specs=ANY,
        scratch_shapes=[
            pltpu.VMEM((PADDED_COLUMNS, 2 * LANES), bf16),
            pltpu.VMEM((GROUP, OWN_TILES, LANES), f32),
            pltpu.SemaphoreType.DMA((UPDATE_PIECES,)),
            pltpu.SemaphoreType.DMA((UPDATE_PIECES,)),
        ],
        compiler_params=kernel_params(24),
        cost_estimate=pl.CostEstimate(flops=4 * 10**9, bytes_accessed=8 * 2**20, transcendentals=0),
        name="updated",
    )(position, starts, *sums, block, factors)


def exchange(value, axes=PEERS):
    return lax.all_to_all(value, axes, 0, 0, tiled=True)


def passed_along(value, by):
    return lax.ppermute(value, "h", [(i, (i + by) % SUMS) for i in range(SUMS)])


def summed(parts):
    total = parts[0]
    for by in range(1, SUMS):
        total = total + passed_along(parts[by], by)
    return (total, *(passed_along(total, by) for by in range(1, SUMS)))


def shards(state, locations, tile_mask, plan, obs_value, obs_error):
    residue = lax.axis_index(PEERS) // SLICES
    position = jnp.stack([residue, lax.axis_index("h"), lax.axis_index("c"), lax.axis_index(ALL)]).astype(i32)
    rows = state.reshape(ROWS, LANES)

    masks = own_masks(position, locations.reshape(-1, LANES), tile_mask)
    masks = exchange(masks.reshape(GROUP_CHIPS, 4, LANES), CHIPS).sum(axis=0)
    tiles = locations // TILE

    observed = own_columns(plan, locations, rows)
    mine = jnp.concatenate([observed, masks], axis=0)
    all_four = [mine] + [passed_along(mine, by) for by in range(1, SUMS)]
    payload = jnp.concatenate(
        [*(each[0:8] for each in all_four), sum(each[8:12] for each in all_four), jnp.zeros((4, LANES), f32)], axis=0
    )
    gathered = exchange(jnp.broadcast_to(payload[None], (GROUP_CHIPS, 40, LANES)), CHIPS)
    block, gathered = lax.optimization_barrier((spread_out(rows), gathered))
    other = lax.ppermute(gathered, "c", [(0, 1), (1, 0)])
    block, other = lax.optimization_barrier((block, other))
    block = exchange(block)

    facts = jnp.concatenate(
        [tiles.astype(f32)[None], obs_value[None], obs_error[None], jnp.zeros((5, NOBS), f32)], axis=0
    )
    columns, factors = observations(
        position, plan[None], facts, gathered.reshape(-1, LANES), other.reshape(-1, LANES)
    )
    nth_own = (residue - tiles + RADIUS) & (RESIDUES - 1)
    own_tile = jnp.where(nth_own < WINDOW, ((tiles - RADIUS + nth_own) & (NTILES - 1)) // RESIDUES, OWN_TILES)
    starts = jnp.sum(own_tile[None, :] < EIGHT * jnp.arange(GROUPS + 1, dtype=i32)[:, None], axis=1, dtype=i32)
    nth_all = (jnp.arange(RESIDUES, dtype=i32)[:, None] - tiles[None, :] + RADIUS) & (RESIDUES - 1)
    most = jnp.max(jnp.sum(nth_all < WINDOW, axis=1, dtype=i32))

    parts = covariances(position, starts, block, columns)
    rest = lax.cond(most > FIRST, summed, lambda parts: parts, parts[SUMS:])
    sums = summed(parts[:SUMS]) + tuple(rest)
    block = exchange(updated(position, starts, sums, block, factors))
    return collect(block).reshape(state.shape)


def solution(mesh):
    fine = Mesh(mesh.devices.reshape(4, 4, 2, 2, 4), ALL)
    placed = (P(ALL, None), P(), P(ALL, None), P(), P(), P())
    return jax.shard_map(shards, mesh=fine, in_specs=placed, out_specs=P(ALL, None), check_vma=False)
```
